256 devices in a mesh: head: 8 (over y_hi, x), ctx: 32 (over z, y_lo, core).
Axes of the slice: x: 4, y: 4 (y_hi: 2, y_lo: 2; y = y_hi * 2 + y_lo), z: 8, core: 2. Of those that a mesh axis runs over, the one named last changes fastest.
Arguments:
- main_queries: bfloat16 [64, 4096, 576], P('head', 'ctx')
- latent_keys: bfloat16 [5120, 576], P('ctx'), may hold values from -6 to 6
- index_queries: bfloat16 [4096, 64, 128], P('ctx'), may hold values from -6 to 6
- index_weights: float32 [4096, 64], P('ctx')
- index_keys: bfloat16 [5120, 128], P('ctx'), may hold values from -6 to 6
- tile_order: int32 [128], P('ctx'), may hold values from 0 to 127, each once
- offset: int32 [1], replicated, may hold values from 864 to 1024
Outputs:
- divergence: float32 [4096], P('ctx')
- weight_grad: float32 [4096, 64], P('ctx')
- key_grad: float32 [5120, 128], P('ctx')
The draws below stay inside these ranges and needn't reach their ends.
All inputs are finite; a program needn't handle non-finite values.
Results may differ from the reference program's by a relative error of at most 0.0075.
Values may be sent and summed in bfloat16 or wider, within the bound.
No kernel may reach another device: no remote copies, remote signals or barrier semaphores. Data moves between devices by JAX's collectives and lax.ppermute only.
A program may use at most 64 MiB of HBM per device.

```python
import jax
import jax.numpy as jnp
from jax import lax

H = 64
DQ = 576
NI = 64
DI = 128
TILE = 32
KEY_DEV = 160
TOKENS = 4096
KEYS = 5120
NTILES = 128


def draw_main_queries(key, part):
    key = jax.random.fold_in(key, 11)
    values = jax.random.normal(key, (H, TOKENS, DQ), jnp.float32)
    return values.astype(jnp.bfloat16)


def draw_index_weights(key, part):
    key = jax.random.fold_in(key, 23)
    values = 0.5 * jax.random.normal(key, (TOKENS, NI), jnp.float32)
    return values


def level_of(rng, shape, cuts, low, high):
    level = 1.0
    for axis_at, parts in cuts:
        draws = jax.random.uniform(jax.random.fold_in(jax.random.fold_in(rng, 6), axis_at), (parts,), jnp.float32, low / len(cuts), high / len(cuts))
        level = level * jnp.repeat(jnp.exp(draws), shape[axis_at] // parts).reshape((-1,) + (1,) * (len(shape) - 1 - axis_at))
    return level


def bell_draw(stream_key, shape, scale, most, pieces=(), held_as=jnp.bfloat16):
    factor_of = level_of(stream_key, shape, pieces, -0.22, 0.18) if pieces else 1.0
    array = jax.random.normal(stream_key, shape, jnp.float32) * scale * factor_of
    return jnp.minimum(jnp.maximum(array, -most), most).astype(held_as)


def setup_inputs(seed: int = 0) -> dict:
    arg_keys = jax.random.split(jax.random.key(seed), 8)
    return {
        "main_queries": draw_main_queries(jax.random.fold_in(arg_keys[7], 71), 0),
        "latent_keys": bell_draw(arg_keys[1], (KEYS, DQ), 1.0, 6.0, ((0, 32),)),
        "index_queries": bell_draw(arg_keys[2], (TOKENS, NI, DI), 1.0, 6.0, ((0, 32),)),
        "index_weights": draw_index_weights(jax.random.fold_in(arg_keys[7], 71), 0),
        "index_keys": bell_draw(arg_keys[4], (KEYS, DI), 1.0, 6.0, ((0, 32),)),
        "tile_order": jax.random.permutation(arg_keys[5], NTILES).astype(jnp.int32),
        "offset": jax.random.randint(arg_keys[6], (1,), KEYS - TOKENS - KEY_DEV, KEYS - TOKENS + 1).astype(jnp.int32),
    }


score_scale = 192.0 ** -0.5


def row_block(row_queries, row_weights, visible, target, index_keys):
    index_scale = DI ** -0.5
    inner = jnp.einsum('tjd,sd->tjs', row_queries.astype(jnp.float32), index_keys.astype(jnp.float32))
    logits = jnp.sum(row_weights[:, :, None] * jax.nn.relu(inner), axis=1) * index_scale
    masked = jnp.where(visible, logits, -jnp.inf)
    log_probs = masked - jax.scipy.special.logsumexp(masked, axis=1, keepdims=True)
    index_probs = jnp.where(visible, jnp.exp(log_probs), 0.0)
    live = visible & (target > 0)
    safe_target = jnp.where(target > 0, target, 1.0)
    divergence = jnp.sum(jnp.where(live, target * (jnp.log(safe_target) - log_probs), 0.0), axis=1)
    grad_logit = jnp.where(visible, index_probs - target, 0.0)
    weight_grad = jnp.sum(grad_logit[:, None, :] * jax.nn.relu(inner), axis=2) * index_scale
    coeff = (grad_logit[:, None, :] * row_weights[:, :, None] * index_scale * (inner > 0)).astype(jnp.bfloat16)
    key_part = jnp.einsum('tjs,tjd->sd', coeff.astype(jnp.float32), row_queries.astype(jnp.float32))
    return divergence, weight_grad, key_part


def reference(main_queries, latent_keys, index_queries, index_weights, index_keys, tile_order, offset):
    positions = offset[0] + jnp.repeat(tile_order, TILE, total_repeat_length=TOKENS) * TILE + jnp.arange(TOKENS, dtype=jnp.int32) % TILE
    visible_int = jnp.where(jnp.arange(KEYS, dtype=jnp.int32)[None, :] <= positions[:, None], 1, 0).astype(jnp.int32)
    visible = visible_int > 0

    def head_step(head_id, total):
        queries = lax.dynamic_index_in_dim(main_queries, head_id, 0, keepdims=False)
        scores = jnp.dot(queries, latent_keys.T, preferred_element_type=jnp.float32) * score_scale
        scores = jnp.where(visible, scores, -jnp.inf)
        return total + jax.nn.softmax(scores, axis=1)

    total = lax.fori_loop(0, H, head_step, jnp.zeros((TOKENS, KEYS), jnp.float32))
    target = total / H
    row_size = 128 if TOKENS % 128 == 0 else TOKENS
    blocks = TOKENS // row_size

    def one_block(items):
        return row_block(items[0], items[1], items[2], items[3], index_keys)

    divergence, weight_grad, key_parts = lax.map(one_block, (
        index_queries.reshape(blocks, row_size, NI, DI),
        index_weights.reshape(blocks, row_size, NI),
        visible.reshape(blocks, row_size, KEYS),
        target.reshape(blocks, row_size, KEYS)))
    return divergence.reshape(TOKENS), weight_grad.reshape(TOKENS, NI), jnp.sum(key_parts, axis=0)
```

```python
import math

import jax
import jax.numpy as jnp
import numpy as np
from jax import lax
from jax.experimental import pallas as pl
from jax.experimental.pallas import tpu as pltpu
from jax.sharding import Mesh
from jax.sharding import PartitionSpec as P

TILE = 32
DQ = 576
DI = 128
NI = 64
HALF = 80
UNIT = 16
BLOCKS = 16
ROWS = 320
SCORE2 = 192.0 ** (-0.5) * math.log2(math.e)
INDEX_SCALE = DI ** (-0.5)
ALL = ("yhi", "xh", "xp", "z", "ylo", "core")
NEG = -jnp.inf


def flat(x, y, z, c):
    return ((y // 2) * 4 + x) * 32 + (z * 2 + (y % 2)) * 2 + c


def shift(value, dx=0, dy=0, dz=0, flip=0):
    pairs = [
        (flat(x, y, z, c), flat((x + dx) % 4, (y + dy) % 4, (z + dz) % 8, c ^ flip))
        for x in range(4)
        for y in range(4)
        for z in range(8)
        for c in range(2)
    ]
    return lax.ppermute(value, ALL, pairs)


def swap_core(value):
    return shift(value, flip=1)


def score_kernel(n, meta, *refs):
    blocks, (qa, qb, wa, wb) = refs[:n], refs[n : n + 4]
    e_ref, m_ref, l_ref, keys, bias, raw = refs[n + 4 :]

    @pl.when(pl.program_id(0) == 0)
    def _():
        place = jnp.concatenate([wa[NI : NI + 1, :], wb[NI : NI + 1, :]], axis=1)
        rows = lax.broadcasted_iota(jnp.int32, (HALF, 256), 0).astype(jnp.float32)
        for i in range(n):
            keys[i * HALF : (i + 1) * HALF, :] = blocks[i][:, DI : DI + DQ]
            base = meta[i].astype(jnp.float32)
            bias[i * HALF : (i + 1) * HALF, :] = jnp.where(rows + base <= place, 0.0, NEG)

    queries = jnp.concatenate([qa[0], qb[0]], axis=1)
    scores = jnp.dot(keys[...], queries, preferred_element_type=jnp.float32) + bias[...]
    raw[...] = scores
    top = jnp.max(scores, axis=0, keepdims=True)
    safe = jnp.where(top == NEG, 0.0, top)
    exps = jnp.exp2((raw[...] - safe) * SCORE2)
    e_ref[0] = exps.astype(jnp.bfloat16)
    m_ref[0] = top
    l_ref[0] = jnp.sum(exps, axis=0, keepdims=True)


def score_call(meta, blocks, qa, qb, wa, wb):
    n = len(blocks)
    heads = qa.shape[0]
    whole = lambda shape: pl.BlockSpec(shape, lambda h, meta: (0,) * len(shape))
    per_head = lambda shape: pl.BlockSpec((1,) + shape, lambda h, meta: (h, 0, 0))
    return pl.pallas_call(
        lambda *refs: score_kernel(n, *refs),
        grid_spec=pltpu.PrefetchScalarGridSpec(
            num_scalar_prefetch=1,
            grid=(heads,),
            in_specs=[whole((HALF, DI + DQ))] * n
            + [per_head((DQ, 128))] * 2
            + [whole((72, 128))] * 2,
            out_specs=[per_head((n * HALF, 256)), per_head((1, 256)), per_head((1, 256))],
            scratch_shapes=[
                pltpu.VMEM((n * HALF, DQ), jnp.bfloat16),
                pltpu.VMEM((n * HALF, 256), jnp.float32),
                pltpu.VMEM((n * HALF, 256), jnp.float32),
            ],
        ),
        out_shape=[
            jax.ShapeDtypeStruct((heads, n * HALF, 256), jnp.bfloat16),
            jax.ShapeDtypeStruct((heads, 1, 256), jnp.float32),
            jax.ShapeDtypeStruct((heads, 1, 256), jnp.float32),
        ],
        cost_estimate=pl.CostEstimate(
            flops=2 * heads * n * HALF * 256 * DQ,
            bytes_accessed=heads * n * HALF * 512,
            transcendentals=heads * n * HALF * 256,
        ),
        compiler_params=pltpu.CompilerParams(vmem_limit_bytes=40 << 20),
        name="scores",
    )(meta, *blocks, qa, qb, wa, wb)


def head_sum_kernel(meta, e0, e1, r0, r1, out):
    i = pl.program_id(0)
    total = jnp.zeros((HALF, 256), jnp.float32)
    for e_ref, r_ref in ((e0, r0), (e1, r1)):
        for h in range(8):
            total = total + e_ref[h].astype(jnp.float32) * r_ref[h]
    total = total.astype(jnp.bfloat16)
    slot = meta[BLOCKS + i]
    for q in range(4):
        out[q, pl.ds(pl.multiple_of(slot * UNIT, UNIT), UNIT), :] = total[q * UNIT : (q + 1) * UNIT]
    extra = pl.multiple_of(256 + (slot >> 2) * UNIT, UNIT)
    out[slot & 3, pl.ds(extra, UNIT), :] = total[4 * UNIT :]


def head_sum_call(meta, e0, e1, r0, r1):
    piece = pl.BlockSpec((8, HALF, 256), lambda i, meta: (0, i, 0))
    ratio = pl.BlockSpec((8, 1, 256), lambda i, meta: (0, 0, 0))
    return pl.pallas_call(
        head_sum_kernel,
        grid_spec=pltpu.PrefetchScalarGridSpec(
            num_scalar_prefetch=1,
            grid=(BLOCKS,),
            in_specs=[piece, piece, ratio, ratio],
            out_specs=pl.BlockSpec((4, ROWS, 256), lambda i, meta: (0, 0, 0)),
        ),
        out_shape=jax.ShapeDtypeStruct((4, ROWS, 256), jnp.bfloat16),
        cost_estimate=pl.CostEstimate(flops=0, bytes_accessed=11 << 20, transcendentals=0),
        compiler_params=pltpu.CompilerParams(vmem_limit_bytes=40 << 20),
        name="head_sum",
    )(meta, e0, e1, r0, r1)


def key_places(meta):
    core, half, quarter = meta[32], meta[33], meta[34]
    rows = lax.broadcasted_iota(jnp.int32, (UNIT, 256), 0)
    out = []
    for u in range(16):
        out.append(rows + ((u // 2 * 4 + (u % 2) * 2 + core) * 160 + half * HALF + quarter * UNIT))
    for e in range(4):
        z, ylo = 2 * e + (quarter >> 1), quarter & 1
        out.append(rows + ((z * 4 + ylo * 2 + core) * 160 + half * HALF + 4 * UNIT))
    return out


def inner_of(keys, ia, ib, j):
    queries = jnp.concatenate([ia[j], ib[j]], axis=0)
    return lax.dot_general(
        keys[...], queries, (((1,), (1,)), ((), ())), preferred_element_type=jnp.float32
    ), queries


JSTEP = 8


def forward_kernel(meta, *refs):
    blocks = refs[:BLOCKS]
    ia, ib, wa, wb, wja, wjb, keys, logits, stats = refs[BLOCKS:]
    step = pl.program_id(0)

    @pl.when(step == 0)
    def _():
        quarter = meta[34]
        for i in range(BLOCKS):
            slot = meta[BLOCKS + i]
            mine = pl.ds(pl.multiple_of(quarter * UNIT, UNIT), UNIT)
            keys[pl.ds(pl.multiple_of(slot * UNIT, UNIT), UNIT), :] = blocks[i][mine, 0:DI]

            @pl.when((slot & 3) == quarter)
            def _():
                extra = pl.multiple_of(256 + (slot >> 2) * UNIT, UNIT)
                keys[pl.ds(extra, UNIT), :] = blocks[i][4 * UNIT :, 0:DI]

        logits[...] = jnp.zeros_like(logits)

    total = logits[...]
    for j in range(JSTEP):
        inner, _ = inner_of(keys, ia, ib, j)
        weight = jnp.concatenate([wja[j : j + 1, :], wjb[j : j + 1, :]], axis=1)
        total = total + weight * jnp.maximum(inner, 0.0)
    logits[...] = total

    @pl.when(step == NI // JSTEP - 1)
    def _():
        place = jnp.concatenate([wa[NI : NI + 1, :], wb[NI : NI + 1, :]], axis=1)
        places = key_places(meta)
        top = jnp.full((1, 256), NEG, jnp.float32)
        for u in range(20):
            cut = slice(u * UNIT, (u + 1) * UNIT)
            value = logits[cut, :] * INDEX_SCALE
            value = jnp.where(places[u].astype(jnp.float32) <= place, value, NEG)
            logits[cut, :] = value
            top = jnp.maximum(top, jnp.max(value, axis=0, keepdims=True))
        safe = jnp.where(top == NEG, 0.0, top)
        total = jnp.sum(jnp.exp(logits[...] - safe), axis=0, keepdims=True)
        stats[...] = jnp.zeros_like(stats)
        stats[0:1, :] = top
        stats[1:2, :] = total


def j_specs():
    whole = lambda shape: pl.BlockSpec(shape, lambda s, meta: (0,) * len(shape))
    queries = pl.BlockSpec((JSTEP, 128, DI), lambda s, meta: (s, 0, 0))
    weights = pl.BlockSpec((JSTEP, 128), lambda s, meta: (s, 0))
    return whole, [queries, queries, whole((72, 128)), whole((72, 128)), weights, weights]


def forward_call(meta, blocks, ia, ib, wa, wb):
    whole, specs = j_specs()
    return pl.pallas_call(
        forward_kernel,
        grid_spec=pltpu.PrefetchScalarGridSpec(
            num_scalar_prefetch=1,
            grid=(NI // JSTEP,),
            in_specs=[whole((HALF, DI + DQ))] * BLOCKS + specs,
            out_specs=[whole((ROWS, DI)), whole((ROWS, 256)), whole((8, 256))],
        ),
        out_shape=[
            jax.ShapeDtypeStruct((ROWS, DI), jnp.bfloat16),
            jax.ShapeDtypeStruct((ROWS, 256), jnp.float32),
            jax.ShapeDtypeStruct((8, 256), jnp.float32),
        ],
        cost_estimate=pl.CostEstimate(
            flops=2 * NI * ROWS * 256 * DI, bytes_accessed=5 << 20, transcendentals=0
        ),
        compiler_params=pltpu.CompilerParams(vmem_limit_bytes=40 << 20),
        name="index_forward",
    )(meta, *blocks, ia, ib, wa, wb, wa, wb)


def backward_kernel(meta, keys, logits, stats, target, ia, ib, wa, wb, wja, wjb, wg, div, kg, grad, acc):
    step = pl.program_id(0)

    @pl.when(step == 0)
    def _():
        tops = [stats[d, 0:1, :] for d in range(8)]
        top = tops[0]
        for d in range(1, 8):
            top = jnp.maximum(top, tops[d])
        total = jnp.zeros((1, 256), jnp.float32)
        for d in range(8):
            total = total + stats[d, 1:2, :] * jnp.exp(tops[d] - top)
        norm = top + jnp.log(total)
        goal = jnp.zeros((ROWS, 256), jnp.float32)
        for d in range(4):
            goal = goal + target[d].astype(jnp.float32)
        goal = goal * (1.0 / 64.0)
        value = logits[...]
        seen = value != NEG
        logp = value - norm
        live = seen & (goal > 0)
        safe = jnp.where(goal > 0, goal, 1.0)
        part = jnp.where(live, goal * (jnp.log(safe) - logp), 0.0)
        div[...] = jnp.zeros_like(div)
        div[0:1, :] = jnp.sum(part, axis=0, keepdims=True)
        grad[...] = jnp.where(seen, jnp.exp(logp) - goal, 0.0) * INDEX_SCALE
        acc[...] = jnp.zeros_like(acc)

    total = acc[...]
    slope = grad[...]
    for j in range(JSTEP):
        inner, queries = inner_of(keys, ia, ib, j)
        weight = jnp.concatenate([wja[j : j + 1, :], wjb[j : j + 1, :]], axis=1)
        wg[j : j + 1, :] = jnp.sum(slope * jnp.maximum(inner, 0.0), axis=0, keepdims=True)
        coeff = jnp.where(inner > 0, slope * weight, 0.0).astype(jnp.bfloat16)
        total = total + jnp.dot(coeff, queries, preferred_element_type=jnp.float32)
    acc[...] = total

    @pl.when(step == NI // JSTEP - 1)
    def _():
        quarter = meta[34]
        for b in range(BLOCKS):
            kg[b, 0:UNIT, :] = acc[b * UNIT : (b + 1) * UNIT, :]
            at = 256 + (b // 4) * UNIT
            kg[b, UNIT:, :] = jnp.where(quarter == b % 4, acc[at : at + UNIT, :], 0.0)


def backward_call(meta, keys, logits, stats, target, ia, ib, wa, wb):
    whole, specs = j_specs()
    return pl.pallas_call(
        backward_kernel,
        grid_spec=pltpu.PrefetchScalarGridSpec(
            num_scalar_prefetch=1,
            grid=(NI // JSTEP,),
            in_specs=[
                whole((ROWS, DI)),
                whole((ROWS, 256)),
                whole((8, 8, 256)),
                whole((4, ROWS, 256)),
            ]
            + specs,
            out_specs=[
                pl.BlockSpec((JSTEP, 256), lambda s, meta: (s, 0)),
                whole((8, 256)),
                whole((BLOCKS, 2 * UNIT, DI)),
            ],
            scratch_shapes=[
                pltpu.VMEM((ROWS, 256), jnp.float32),
                pltpu.VMEM((ROWS, DI), jnp.float32),
            ],
        ),
        out_shape=[
            jax.ShapeDtypeStruct((NI, 256), jnp.float32),
            jax.ShapeDtypeStruct((8, 256), jnp.float32),
            jax.ShapeDtypeStruct((BLOCKS, 2 * UNIT, DI), jnp.float32),
        ],
        cost_estimate=pl.CostEstimate(
            flops=4 * NI * ROWS * 256 * DI, bytes_accessed=6 << 20, transcendentals=0
        ),
        compiler_params=pltpu.CompilerParams(vmem_limit_bytes=40 << 20),
        name="index_backward",
    )(meta, keys, logits, stats, target, ia, ib, wa, wb, wa, wb)


def merge(m0, l0, m1, l1):
    top = jnp.maximum(m0, m1)
    return top, l0 * jnp.exp2((m0 - top) * SCORE2) + l1 * jnp.exp2((m1 - top) * SCORE2)


def swap_halves(value):
    return jnp.concatenate([value[..., 128:], value[..., :128]], axis=-1)


def gather_head(value):
    wide = jnp.broadcast_to(value[None], (8,) + value.shape)
    return lax.all_to_all(wide, ("yhi", "xh", "xp"), 0, 0, tiled=True)


def body(main_queries, latent_keys, index_queries, index_weights, index_keys, tile_order, offset):
    z, ylo, core = lax.axis_index("z"), lax.axis_index("ylo"), lax.axis_index("core")
    half = lax.axis_index("xp")
    quarter = lax.axis_index("yhi") * 2 + lax.axis_index("xh")

    rows = jnp.arange(128, dtype=jnp.int32)
    place = offset[0] + jnp.repeat(tile_order, TILE, total_repeat_length=128) * TILE + rows % TILE
    wa = jnp.concatenate(
        [index_weights.T, place.astype(jnp.float32)[None], jnp.zeros((7, 128), jnp.float32)], axis=0
    )
    own = jnp.concatenate([index_keys, latent_keys], axis=1)
    own = lax.dynamic_slice_in_dim(own, half * HALF, HALF, 0)

    queries = main_queries.transpose(0, 2, 1)
    column = [(0, own)]
    forward = back = own
    for s in range(1, 5):
        forward = shift(forward, dz=1)
        column.append((-s, forward))
        if s < 4:
            back = shift(back, dz=7)
            column.append((s, back))
    other = [(dz, shift(block, dy=1 if dz <= 0 else 3)) for dz, block in column]
    blocks = [block for _, block in column + other]
    spots = [(dz, 0) for dz, _ in column] + [(dz, 1) for dz, _ in other]

    near = jnp.concatenate([shift(queries[:4], dx=1), shift(queries[4:], dx=3)], axis=0)
    wb = swap_core(wa)
    queries_b = swap_core(queries)
    near_b = swap_core(near)
    ia = index_queries.transpose(1, 0, 2)
    ib = swap_core(ia)

    zs = jnp.stack([(z + dz) % 8 for dz, _ in spots])
    ys = jnp.stack([ylo ^ dy for _, dy in spots])
    bases = (zs * 4 + ys * 2 + core) * 160 + half * HALF
    meta = jnp.concatenate(
        [bases, zs * 2 + ys, jnp.stack([core, half, quarter])]
    ).astype(jnp.int32)

    e0, m0, l0 = score_call(meta, blocks, queries, queries_b, wa, wb)
    e1, m1, l1 = score_call(meta, blocks, near, near_b, wa, wb)
    keys, logits, stats = forward_call(meta, blocks, ia, ib, wa, wb)

    m = jnp.concatenate([m0, m1], axis=0)[:, 0]
    l = jnp.concatenate([l0, l1], axis=0)[:, 0]
    away = swap_core(swap_halves(jnp.stack([m, l])))
    m2, l2 = merge(m, l, away[0], away[1])
    part = lambda a, b: jnp.stack(
        [jnp.concatenate([v[4 * a : 4 * a + 4], v[4 * b : 4 * b + 4]]) for v in (m2, l2)]
    )
    left = shift(part(0, 3), dx=1)
    right = shift(part(1, 2), dx=3)
    peer = jnp.concatenate([right[:, 4:], left[:, 4:], left[:, :4], right[:, :4]], axis=1)
    top, total = merge(m2, l2, peer[0], peer[1])
    ratio = (jnp.exp2((m - top) * SCORE2) / total)[:, None, :]
    sums = head_sum_call(meta, e0, e1, ratio[:8], ratio[8:])
    target = lax.all_to_all(sums, ("yhi", "xh"), 0, 0, tiled=True)

    far = swap_core(swap_halves(stats))
    itop = jnp.maximum(stats[0], far[0])
    isum = stats[1] * jnp.exp(stats[0] - itop) + far[1] * jnp.exp(far[0] - itop)
    istats = jnp.concatenate([itop[None], isum[None], jnp.zeros((6, 256), jnp.float32)], axis=0)
    istats = gather_head(istats)

    wg, div, kg = backward_call(meta, keys, logits, istats, target, ia, ib, wa, wb)
    rows_out = jnp.concatenate([wg, div], axis=0)
    rows_out = rows_out[:, :128] + swap_core(rows_out[:, 128:])
    kg = jnp.sum(lax.all_to_all(kg, ("z", "ylo"), 0, 0, tiled=True), axis=0)
    last = gather_head(jnp.concatenate([kg, rows_out], axis=0))
    rows_sum = jnp.sum(last[:, 2 * UNIT :], axis=0)
    pieces = last[:, : 2 * UNIT].reshape(4, 2, 2 * UNIT, DI)
    main = pieces[:, :, :UNIT].transpose(1, 0, 2, 3).reshape(2, 4 * UNIT, DI)
    extra = jnp.sum(pieces[:, :, UNIT:], axis=0)
    key_grad = jnp.concatenate([main, extra], axis=1).reshape(160, DI)
    return rows_sum[NI], rows_sum[:NI].T, key_grad


def solution(mesh):
    fine = Mesh(np.asarray(mesh.devices).reshape(2, 2, 2, 8, 2, 2), ALL)
    head, ctx = ("yhi", "xh", "xp"), ("z", "ylo", "core")
    in_specs = (
        P(head, ctx, None),
        P(ctx, None),
        P(ctx, None, None),
        P(ctx, None),
        P(ctx, None),
        P(ctx),
        P(),
    )
    out_specs = (P(ctx), P(ctx, None), P(ctx, None))
    return jax.shard_map(body, mesh=fine, in_specs=in_specs, out_specs=out_specs, check_vma=False)
```

```python
import math

import jax
import jax.numpy as jnp
import numpy as np
from jax import lax
from jax.experimental import pallas as pl
from jax.experimental.pallas import tpu as pltpu
from jax.sharding import Mesh
from jax.sharding import PartitionSpec as P

TILE = 32
DQ = 576
DI = 128
NI = 64
HALF = 80
UNIT = 16
BLOCKS = 16
ROWS = 320
SCORE2 = 192.0 ** (-0.5) * math.log2(math.e)
INDEX_SCALE = DI ** (-0.5)
ALL = ("yhi", "xh", "xp", "z", "ylo", "core")
NEG = -jnp.inf
VMEM = 18 << 20


def flat(x, y, z, c):
    return ((y // 2) * 4 + x) * 32 + (z * 2 + (y % 2)) * 2 + c


def shift(value, dx=0, dy=0, dz=0, flip=0):
    pairs = [
        (flat(x, y, z, c), flat((x + dx) % 4, (y + dy) % 4, (z + dz) % 8, c ^ flip))
        for x in range(4)
        for y in range(4)
        for z in range(8)
        for c in range(2)
    ]
    return lax.ppermute(value, ALL, pairs)


def swap_core(value):
    return shift(value, flip=1)


def score_kernel(spans, first, meta, *refs):
    n = len(spans)
    blocks, (qa, qb, na, nb, wa, wb) = refs[:n], refs[n : n + 6]
    e_ref, m_ref, l_ref, keys, bias, raw, tops = refs[n + 6 :]
    step = pl.program_id(0)
    rows = keys.shape[0]
    cut = 320

    @pl.when(step == 0)
    def _():
        at = 0
        for block, span in zip(blocks, spans):
            keys[at : at + span, :] = block[:, DI : DI + DQ]
            at += span
        place = jnp.concatenate([wa[NI : NI + 1, :], wb[NI : NI + 1, :]], axis=1)
        offsets = lax.broadcasted_iota(jnp.int32, (HALF, 256), 0).astype(jnp.float32)
        for i in range(rows // HALF):
            base = meta[first + i].astype(jnp.float32)
            bias[i * HALF : (i + 1) * HALF, :] = jnp.where(offsets + base <= place, 0.0, NEG)
        tops[...] = jnp.zeros_like(tops)

    def work(now, last):
        own = jnp.concatenate([qa[0], qb[0]], axis=1)
        near = jnp.concatenate([na[0], nb[0]], axis=1)
        queries = jnp.where(step < 4, own, near)
        top = jnp.max(tops[last], axis=0, keepdims=True)
        safe = jnp.where(top == NEG, 0.0, top)
        new = jnp.full((8, 256), NEG, jnp.float32)
        total = jnp.zeros((8, 256), jnp.float32)
        for t in range(0, rows, cut):
            piece = slice(t, t + cut)
            scores = jnp.dot(keys[piece, :], queries, preferred_element_type=jnp.float32)
            scores = scores + bias[piece, :]
            raw[now, piece, :] = scores
            new = jnp.maximum(new, jnp.max(scores.reshape(cut // 8, 8, 256), axis=0))
            exps = jnp.exp2((raw[last, piece, :] - safe) * SCORE2)
            e_ref[0, piece, :] = exps.astype(jnp.bfloat16)
            total = total + jnp.sum(exps.reshape(cut // 8, 8, 256), axis=0)
        tops[now] = new
        m_ref[0] = top
        l_ref[0] = jnp.sum(total, axis=0, keepdims=True)

    @pl.when(step % 2 == 0)
    def _():
        work(0, 1)

    @pl.when(step % 2 == 1)
    def _():
        work(1, 0)


def score_call(meta, first, blocks, group, qa, qb, na, nb, wa, wb):
    spans = [block.shape[0] for block in blocks]
    rows = sum(spans)
    whole = lambda shape: pl.BlockSpec(shape, lambda h, meta: (0,) * len(shape))
    own = pl.BlockSpec((1, DQ, 128), lambda h, meta: (jnp.minimum(h, 3) + 4 * group, 0, 0))
    near = pl.BlockSpec((1, DQ, 128), lambda h, meta: (jnp.clip(h - 4, 0, 3), 0, 0))
    lag = lambda shape: pl.BlockSpec((1,) + shape, lambda h, meta: (jnp.maximum(h - 1, 0), 0, 0))
    return pl.pallas_call(
        lambda *refs: score_kernel(spans, first, *refs),
        grid_spec=pltpu.PrefetchScalarGridSpec(
            num_scalar_prefetch=1,
            grid=(9,),
            in_specs=[whole(block.shape) for block in blocks]
            + [own, own, near, near]
            + [whole((72, 128))] * 2,
            out_specs=[lag((rows, 256)), lag((1, 256)), lag((1, 256))],
            scratch_shapes=[
                pltpu.VMEM((rows, DQ), jnp.bfloat16),
                pltpu.VMEM((rows, 256), jnp.float32),
                pltpu.VMEM((2, rows, 256), jnp.float32),
                pltpu.VMEM((2, 8, 256), jnp.float32),
            ],
        ),
        out_shape=[
            jax.ShapeDtypeStruct((8, rows, 256), jnp.bfloat16),
            jax.ShapeDtypeStruct((8, 1, 256), jnp.float32),
            jax.ShapeDtypeStruct((8, 1, 256), jnp.float32),
        ],
        cost_estimate=pl.CostEstimate(
            flops=24 * rows * 256 * DQ, bytes_accessed=8 * rows * 512, transcendentals=8 * rows * 256
        ),
        compiler_params=pltpu.CompilerParams(vmem_limit_bytes=VMEM),
        name="scores",
    )(meta, *blocks, qa, qb, na, nb, wa, wb)


def head_sum_kernel(meta, ea0, ea1, eb0, eb1, ra, rb, o0, o1, o2, o3, total_ref):
    i = pl.program_id(0)

    def add(parts, chunk):
        total = jnp.zeros((HALF, 256), jnp.float32)
        for e_ref, r_ref in parts:
            for h in range(8):
                total = total + e_ref[h].astype(jnp.float32) * r_ref[chunk, h]
        total_ref[...] = total

    @pl.when(i < 8)
    def _():
        add(((ea0, ra), (eb0, rb)), 0)

    @pl.when(i >= 8)
    def _():
        add(((ea1, ra), (eb1, rb)), 1)

    slot = meta[BLOCKS + i]
    quarter = meta[34]
    at = pl.ds(pl.multiple_of(slot * UNIT, UNIT), UNIT)
    extra = pl.ds(pl.multiple_of(256 + (slot >> 2) * UNIT, UNIT), UNIT)
    for k, out in enumerate((o0, o1, o2, o3)):
        unit = pl.multiple_of((quarter ^ k) * UNIT, UNIT)
        out[at, :] = total_ref[pl.ds(unit, UNIT), :].astype(jnp.bfloat16)

        @pl.when((slot & 3) == (quarter ^ k))
        def _():
            out[extra, :] = total_ref[4 * UNIT :, :].astype(jnp.bfloat16)


def head_sum_call(meta, ea, eb, ra, rb):
    early = pl.BlockSpec((8, HALF, 256), lambda i, meta: (0, jnp.minimum(i, 7), 0))
    late = pl.BlockSpec((8, HALF, 256), lambda i, meta: (0, jnp.maximum(i - 8, 0), 0))
    ratio = pl.BlockSpec((2, 8, 1, 256), lambda i, meta: (0, 0, 0, 0))
    out = pl.BlockSpec((ROWS, 256), lambda i, meta: (0, 0))
    return pl.pallas_call(
        head_sum_kernel,
        grid_spec=pltpu.PrefetchScalarGridSpec(
            num_scalar_prefetch=1,
            grid=(BLOCKS,),
            in_specs=[early, late, early, late, ratio, ratio],
            out_specs=[out] * 4,
            scratch_shapes=[pltpu.VMEM((HALF, 256), jnp.float32)],
        ),
        out_shape=[jax.ShapeDtypeStruct((ROWS, 256), jnp.bfloat16)] * 4,
        cost_estimate=pl.CostEstimate(flops=0, bytes_accessed=11 << 20, transcendentals=0),
        compiler_params=pltpu.CompilerParams(vmem_limit_bytes=VMEM),
        name="head_sum",
    )(meta, *ea, *eb, ra, rb)


def key_places(meta):
    core, half, quarter = meta[32], meta[33], meta[34]
    rows = lax.broadcasted_iota(jnp.int32, (UNIT, 256), 0)
    out = []
    for u in range(16):
        out.append(rows + ((u // 2 * 4 + (u % 2) * 2 + core) * 160 + half * HALF + quarter * UNIT))
    for e in range(4):
        z, ylo = 2 * e + (quarter >> 1), quarter & 1
        out.append(rows + ((z * 4 + ylo * 2 + core) * 160 + half * HALF + 4 * UNIT))
    return out


def inner_of(keys, ia, ib, j):
    queries = jnp.concatenate([ia[j], ib[j]], axis=0)
    return lax.dot_general(
        keys[...], queries, (((1,), (1,)), ((), ())), preferred_element_type=jnp.float32
    ), queries


JSTEP = 8


def forward_kernel(spans, meta, *refs):
    n = len(spans)
    ia, ib, wa, wb, wja, wjb, keys, logits, stats = refs[n:]
    blocks = [ref.at[at : at + HALF, 0:DI] for ref, span in zip(refs, spans) for at in range(0, span, HALF)]
    step = pl.program_id(0)

    @pl.when(step == 0)
    def _():
        quarter = meta[34]
        for i in range(BLOCKS):
            slot = meta[BLOCKS + i]
            mine = pl.ds(pl.multiple_of(quarter * UNIT, UNIT), UNIT)
            keys[pl.ds(pl.multiple_of(slot * UNIT, UNIT), UNIT), :] = blocks[i][mine, :]

            @pl.when((slot & 3) == quarter)
            def _():
                extra = pl.multiple_of(256 + (slot >> 2) * UNIT, UNIT)
                keys[pl.ds(extra, UNIT), :] = blocks[i][4 * UNIT :, :]

        logits[...] = jnp.zeros_like(logits)

    total = logits[...]
    for j in range(JSTEP):
        inner, _ = inner_of(keys, ia, ib, j)
        weight = jnp.concatenate([wja[j : j + 1, :], wjb[j : j + 1, :]], axis=1)
        total = total + weight * jnp.maximum(inner, 0.0)
    logits[...] = total

    @pl.when(step == NI // JSTEP - 1)
    def _():
        place = jnp.concatenate([wa[NI : NI + 1, :], wb[NI : NI + 1, :]], axis=1)
        places = key_places(meta)
        top = jnp.full((1, 256), NEG, jnp.float32)
        for u in range(20):
            cut = slice(u * UNIT, (u + 1) * UNIT)
            value = logits[cut, :] * INDEX_SCALE
            value = jnp.where(places[u].astype(jnp.float32) <= place, value, NEG)
            logits[cut, :] = value
            top = jnp.maximum(top, jnp.max(value, axis=0, keepdims=True))
        safe = jnp.where(top == NEG, 0.0, top)
        total = jnp.sum(jnp.exp(logits[...] - safe), axis=0, keepdims=True)
        stats[...] = jnp.zeros_like(stats)
        stats[0:1, :] = top
        stats[1:2, :] = total


def j_specs():
    whole = lambda shape: pl.BlockSpec(shape, lambda s, meta: (0,) * len(shape))
    queries = pl.BlockSpec((JSTEP, 128, DI), lambda s, meta: (s, 0, 0))
    weights = pl.BlockSpec((JSTEP, 128), lambda s, meta: (s, 0))
    return whole, [queries, queries, whole((72, 128)), whole((72, 128)), weights, weights]


def forward_call(meta, blocks, ia, ib, wa, wb):
    whole, specs = j_specs()
    spans = [block.shape[0] for block in blocks]
    return pl.pallas_call(
        lambda *refs: forward_kernel(spans, *refs),
        grid_spec=pltpu.PrefetchScalarGridSpec(
            num_scalar_prefetch=1,
            grid=(NI // JSTEP,),
            in_specs=[whole(block.shape) for block in blocks] + specs,
            out_specs=[whole((ROWS, DI)), whole((ROWS, 256)), whole((8, 256))],
        ),
        out_shape=[
            jax.ShapeDtypeStruct((ROWS, DI), jnp.bfloat16),
            jax.ShapeDtypeStruct((ROWS, 256), jnp.float32),
            jax.ShapeDtypeStruct((8, 256), jnp.float32),
        ],
        cost_estimate=pl.CostEstimate(
            flops=2 * NI * ROWS * 256 * DI, bytes_accessed=5 << 20, transcendentals=0
        ),
        compiler_params=pltpu.CompilerParams(vmem_limit_bytes=VMEM),
        name="index_forward",
    )(meta, *blocks, ia, ib, wa, wb, wa, wb)


def backward_kernel(meta, keys, logits, stats, t0, t1, t2, t3, ia, ib, wa, wb, wja, wjb, wg, div, kg, grad, acc):
    step = pl.program_id(0)

    @pl.when(step == 0)
    def _():
        tops = [stats[d, 0:1, :] for d in range(8)]
        top = tops[0]
        for d in range(1, 8):
            top = jnp.maximum(top, tops[d])
        total = jnp.zeros((1, 256), jnp.float32)
        for d in range(8):
            total = total + stats[d, 1:2, :] * jnp.exp(tops[d] - top)
        norm = top + jnp.log(total)
        goal = jnp.zeros((ROWS, 256), jnp.float32)
        for part in (t0, t1, t2, t3):
            goal = goal + part[...].astype(jnp.float32)
        goal = goal * (1.0 / 64.0)
        value = logits[...]
        seen = value != NEG
        logp = value - norm
        live = seen & (goal > 0)
        safe = jnp.where(goal > 0, goal, 1.0)
        part = jnp.where(live, goal * (jnp.log(safe) - logp), 0.0)
        div[...] = jnp.zeros_like(div)
        div[0:1, :] = jnp.sum(part, axis=0, keepdims=True)
        grad[...] = jnp.where(seen, jnp.exp(logp) - goal, 0.0) * INDEX_SCALE
        acc[...] = jnp.zeros_like(acc)

    total = acc[...]
    slope = grad[...]
    for j in range(JSTEP):
        inner, queries = inner_of(keys, ia, ib, j)
        weight = jnp.concatenate([wja[j : j + 1, :], wjb[j : j + 1, :]], axis=1)
        wg[j : j + 1, :] = jnp.sum(slope * jnp.maximum(inner, 0.0), axis=0, keepdims=True)
        coeff = jnp.where(inner > 0, slope * weight, 0.0).astype(jnp.bfloat16)
        total = total + jnp.dot(coeff, queries, preferred_element_type=jnp.float32)
    acc[...] = total

    @pl.when(step == NI // JSTEP - 1)
    def _():
        quarter = meta[34]
        for b in range(BLOCKS):
            kg[b, 0:UNIT, :] = acc[b * UNIT : (b + 1) * UNIT, :].astype(jnp.bfloat16)
            at = 256 + (b // 4) * UNIT
            extra = jnp.where(quarter == b % 4, acc[at : at + UNIT, :], 0.0)
            kg[b, UNIT:, :] = extra.astype(jnp.bfloat16)


def backward_call(meta, keys, logits, stats, target, ia, ib, wa, wb):
    whole, specs = j_specs()
    return pl.pallas_call(
        backward_kernel,
        grid_spec=pltpu.PrefetchScalarGridSpec(
            num_scalar_prefetch=1,
            grid=(NI // JSTEP,),
            in_specs=[
                whole((ROWS, DI)),
                whole((ROWS, 256)),
                whole((8, 8, 256)),
            ]
            + [whole((ROWS, 256))] * 4
            + specs,
            out_specs=[
                pl.BlockSpec((JSTEP, 256), lambda s, meta: (s, 0)),
                whole((8, 256)),
                whole((BLOCKS, 2 * UNIT, DI)),
            ],
            scratch_shapes=[
                pltpu.VMEM((ROWS, 256), jnp.float32),
                pltpu.VMEM((ROWS, DI), jnp.float32),
            ],
        ),
        out_shape=[
            jax.ShapeDtypeStruct((NI, 256), jnp.float32),
            jax.ShapeDtypeStruct((8, 256), jnp.float32),
            jax.ShapeDtypeStruct((BLOCKS, 2 * UNIT, DI), jnp.bfloat16),
        ],
        cost_estimate=pl.CostEstimate(
            flops=4 * NI * ROWS * 256 * DI, bytes_accessed=6 << 20, transcendentals=0
        ),
        compiler_params=pltpu.CompilerParams(vmem_limit_bytes=VMEM),
        name="index_backward",
    )(meta, keys, logits, stats, *target, ia, ib, wa, wb, wa, wb)


def merge(m0, l0, m1, l1):
    top = jnp.maximum(m0, m1)
    return top, l0 * jnp.exp2((m0 - top) * SCORE2) + l1 * jnp.exp2((m1 - top) * SCORE2)


def swap_halves(value):
    return jnp.concatenate([value[..., 128:], value[..., :128]], axis=-1)


def gather_head(value):
    wide = jnp.broadcast_to(value[None], (8,) + value.shape)
    return lax.all_to_all(wide, ("yhi", "xh", "xp"), 0, 0, tiled=True)


def after(value, *others):
    return lax.optimization_barrier((value,) + others)[0]


def body(main_queries, latent_keys, index_queries, index_weights, index_keys, tile_order, offset):
    z, ylo, core = lax.axis_index("z"), lax.axis_index("ylo"), lax.axis_index("core")
    half = lax.axis_index("xp")
    quarter = lax.axis_index("yhi") * 2 + lax.axis_index("xh")

    rows = jnp.arange(TILE, dtype=jnp.int32)
    place = (offset + (tile_order[:, None] * TILE + rows[None, :])).reshape(1, 128)
    wa = jnp.concatenate(
        [index_weights.T, place.astype(jnp.float32), jnp.zeros((7, 128), jnp.float32)], axis=0
    )
    own = jnp.concatenate([index_keys, latent_keys], axis=1)
    own = lax.dynamic_slice_in_dim(own, half * HALF, HALF, 0)

    queries = main_queries.transpose(0, 2, 1)
    f1, b1 = shift(own, dz=1), shift(own, dz=7)
    near_a, near_b = shift(queries[:4], dx=1), shift(queries[4:], dx=3)
    wb = swap_core(wa)
    queries_far = swap_core(queries)
    y0 = shift(own, dy=1)
    f2, b2 = shift(f1, dz=1), shift(b1, dz=7)
    y1 = shift(jnp.concatenate([f1, b1]), dy=3)
    f2, b2 = lax.optimization_barrier((f2, b2, y0))[:2]
    f3, b3 = shift(f2, dz=1), shift(b2, dz=7)
    y2 = shift(jnp.concatenate([f2, b2]), dy=1)
    near_a, near_b = lax.optimization_barrier((near_a, near_b, f2))[:2]
    near_a_far, near_b_far = swap_core(near_a), swap_core(near_b)
    f3, b3 = lax.optimization_barrier((f3, b3, y1))[:2]
    f4 = shift(f3, dz=1)
    y3 = shift(jnp.concatenate([f3, b3]), dy=3)
    y4 = shift(f4, dy=1)
    ia = after(index_queries, f4).transpose(1, 0, 2)
    ib = swap_core(ia)
    column = [(0, own), (-1, f1), (1, b1), (-2, f2), (2, b2), (-3, f3), (3, b3), (-4, f4)]
    blocks = [[block for _, block in column], [y0, y1, y2, y3, y4]]

    steps = jnp.asarray([dz for dz, _ in column] * 2, dtype=jnp.int32)
    zs = (z + 8 + steps) % 8
    ys = ylo ^ jnp.asarray([0] * 8 + [1] * 8, dtype=jnp.int32)
    bases = (zs * 4 + ys * 2 + core) * 160 + half * HALF
    meta = jnp.concatenate(
        [bases, zs * 2 + ys, jnp.stack([core, half, quarter])]
    ).astype(jnp.int32)

    near = [(near_a, near_a_far), (near_b, near_b_far)]

    def score(c, g, weights):
        return score_call(
            meta, 8 * c, blocks[c], g, queries, queries_far, *near[g], weights, wb
        )

    early = [score(0, g, wa) for g in range(2)]
    late = [score(1, 0, wa)]
    keys, logits, stats = forward_call(meta, blocks[0] + blocks[1], ia, ib, after(wa, late[0][1]), wb)
    late.append(score(1, 1, after(wa, stats)))

    ratios = []
    for g in range(2):
        (_, m0, l0), (_, m1, l1) = early[g], late[g]
        m, l = merge(m0[:, 0], l0[:, 0], m1[:, 0], l1[:, 0])
        away = swap_core(swap_halves(jnp.stack([m, l])))
        m, l = merge(m, l, away[0], away[1])
        ours = jnp.stack([m, l])
        out, back = (1, 3) if g == 0 else (3, 1)
        theirs = jnp.concatenate([shift(ours[:, 4:], dx=back), shift(ours[:, :4], dx=out)], axis=1)
        top, total = merge(m, l, theirs[0], theirs[1])
        ratios.append(jnp.stack([jnp.exp2((v - top[:, None]) * SCORE2) / total[:, None] for v in (m0, m1)]))
    sums = head_sum_call(meta, [early[0][0], late[0][0]], [early[1][0], late[1][0]], *ratios)
    target = [sums[0], shift(sums[1], dx=2), shift(sums[2], dy=2), shift(sums[3], dx=2, dy=2)]

    far = swap_core(swap_halves(stats))
    itop = jnp.maximum(stats[0], far[0])
    isum = stats[1] * jnp.exp(stats[0] - itop) + far[1] * jnp.exp(far[0] - itop)
    istats = jnp.concatenate([itop[None], isum[None], jnp.zeros((6, 256), jnp.float32)], axis=0)
    istats = gather_head(istats)

    wg, div, kg = backward_call(meta, keys, logits, istats, target, ia, ib, wa, wb)
    rows_out = jnp.concatenate([wg, div], axis=0)
    rows_out = rows_out[:, :128] + swap_core(rows_out[:, 128:])
    rows_sum = jnp.sum(gather_head(rows_out), axis=0)
    kg = lax.all_to_all(kg, ("z", "ylo"), 0, 0, tiled=True)
    kg = jnp.sum(kg.astype(jnp.float32), axis=0).astype(jnp.bfloat16)
    pieces = gather_head(kg).astype(jnp.float32).reshape(4, 2, 2 * UNIT, DI)
    main = pieces[:, :, :UNIT].transpose(1, 0, 2, 3).reshape(2, 4 * UNIT, DI)
    extra = jnp.sum(pieces[:, :, UNIT:], axis=0)
    key_grad = jnp.concatenate([main, extra], axis=1).reshape(160, DI)
    return rows_sum[NI], rows_sum[:NI].T, key_grad


def solution(mesh):
    fine = Mesh(np.asarray(mesh.devices).reshape(2, 2, 2, 8, 2, 2), ALL)
    head, ctx = ("yhi", "xh", "xp"), ("z", "ylo", "core")
    in_specs = (
        P(head, ctx, None),
        P(ctx, None),
        P(ctx, None, None),
        P(ctx, None),
        P(ctx, None),
        P(ctx),
        P(),
    )
    out_specs = (P(ctx), P(ctx, None), P(ctx, None))
    return jax.shard_map(body, mesh=fine, in_specs=in_specs, out_specs=out_specs, check_vma=False)
```

```python
import math

import jax
import jax.numpy as jnp
import numpy as np
from jax import lax
from jax.experimental import pallas as pl
from jax.experimental.pallas import tpu as pltpu
from jax.sharding import Mesh
from jax.sharding import PartitionSpec as P

TILE = 32
DQ = 576
DI = 128
NI = 64
HALF = 80
UNIT = 16
BLOCKS = 16
ROWS = 320
SCORE2 = 192.0 ** (-0.5) * math.log2(math.e)
INDEX_SCALE = DI ** (-0.5)
ALL = ("yhi", "xh", "xp", "z", "ylo", "core")
NEG = -jnp.inf
VMEM = 18 << 20


def flat(x, y, z, c):
    return ((y // 2) * 4 + x) * 32 + (z * 2 + (y % 2)) * 2 + c


def shift(value, dx=0, dy=0, dz=0, flip=0):
    pairs = [
        (flat(x, y, z, c), flat((x + dx) % 4, (y + dy) % 4, (z + dz) % 8, c ^ flip))
        for x in range(4)
        for y in range(4)
        for z in range(8)
        for c in range(2)
    ]
    return lax.ppermute(value, ALL, pairs)


def swap_core(value):
    return shift(value, flip=1)


HEADS = 16
KEYS_HERE = BLOCKS * HALF


def score_kernel(spans, meta, *refs):
    n = len(spans)
    blocks, (qa, qb, na, nb, ma, mb, wa, wb) = refs[:n], refs[n : n + 8]
    e_ref, m_ref, l_ref, ik_ref, keys, bias, raw, tops, sems = refs[n + 8 :]
    step = pl.program_id(0)
    cut = 320

    @pl.when(step == 0)
    def _():
        at = 0
        copies = []
        for i, (block, span) in enumerate(zip(blocks, spans)):
            copies.append(pltpu.make_async_copy(block, keys.at[at : at + span, :], sems.at[i]))
            copies[-1].start()
            at += span
        place = jnp.concatenate([wa[NI : NI + 1, :], wb[NI : NI + 1, :]], axis=1)
        offsets = lax.broadcasted_iota(jnp.int32, (HALF, 256), 0).astype(jnp.float32)
        for i in range(BLOCKS):
            base = meta[i].astype(jnp.float32)
            bias[i * HALF : (i + 1) * HALF, :] = jnp.where(offsets + base <= place, 0.0, NEG)
        tops[...] = jnp.zeros_like(tops)
        for copy in copies:
            copy.wait()
        quarter = meta[34]
        for i in range(BLOCKS):
            slot = meta[BLOCKS + i]
            mine = pl.ds(pl.multiple_of(i * HALF + quarter * UNIT, UNIT), UNIT)
            ik_ref[pl.ds(pl.multiple_of(slot * UNIT, UNIT), UNIT), :] = keys[mine, 0:DI]

            @pl.when((slot & 3) == quarter)
            def _():
                extra = pl.multiple_of(256 + (slot >> 2) * UNIT, UNIT)
                ik_ref[pl.ds(extra, UNIT), :] = keys[i * HALF + 4 * UNIT : (i + 1) * HALF, 0:DI]

    def work(now, last):
        own = jnp.concatenate([qa[0], qb[0]], axis=1)
        left = jnp.concatenate([na[0], nb[0]], axis=1)
        right = jnp.concatenate([ma[0], mb[0]], axis=1)
        queries = jnp.where(step < 8, own, jnp.where(step < 12, left, right))
        top = jnp.max(tops[last], axis=0, keepdims=True)
        safe = jnp.where(top == NEG, 0.0, top)
        new = jnp.full((8, 256), NEG, jnp.float32)
        total = jnp.zeros((8, 256), jnp.float32)
        for t in range(0, KEYS_HERE, cut):
            piece = slice(t, t + cut)
            scores = jnp.dot(keys[piece, DI:], queries, preferred_element_type=jnp.float32)
            scores = scores + bias[piece, :]
            raw[now, piece, :] = scores
            new = jnp.maximum(new, jnp.max(scores.reshape(cut // 8, 8, 256), axis=0))
            exps = jnp.exp2((raw[last, piece, :] - safe) * SCORE2)
            e_ref[0, piece, :] = exps.astype(jnp.bfloat16)
            total = total + jnp.sum(exps.reshape(cut // 8, 8, 256), axis=0)
        tops[now] = new
        m_ref[0] = top
        l_ref[0] = jnp.sum(total, axis=0, keepdims=True)

    @pl.when(step % 2 == 0)
    def _():
        work(0, 1)

    @pl.when(step % 2 == 1)
    def _():
        work(1, 0)


def score_call(meta, blocks, qa, qb, na, nb, ma, mb, wa, wb):
    spans = [block.shape[0] for block in blocks]
    whole = lambda shape: pl.BlockSpec(shape, lambda h, meta: (0,) * len(shape))

    def heads(first, count):
        return pl.BlockSpec((1, DQ, 128), lambda h, meta: (jnp.clip(h - first, 0, count - 1), 0, 0))

    lag = lambda shape: pl.BlockSpec((1,) + shape, lambda h, meta: (jnp.maximum(h - 1, 0), 0, 0))
    return pl.pallas_call(
        lambda *refs: score_kernel(spans, *refs),
        grid_spec=pltpu.PrefetchScalarGridSpec(
            num_scalar_prefetch=1,
            grid=(HEADS + 1,),
            in_specs=[pl.BlockSpec(memory_space=pl.ANY)] * len(blocks)
            + [heads(0, 8)] * 2
            + [heads(8, 4)] * 2
            + [heads(12, 4)] * 2
            + [whole((72, 128))] * 2,
            out_specs=[lag((KEYS_HERE, 256)), lag((1, 256)), lag((1, 256)), whole((ROWS, DI))],
            scratch_shapes=[
                pltpu.VMEM((KEYS_HERE, DI + DQ), jnp.bfloat16),
                pltpu.VMEM((KEYS_HERE, 256), jnp.float32),
                pltpu.VMEM((2, KEYS_HERE, 256), jnp.float32),
                pltpu.VMEM((2, 8, 256), jnp.float32),
                pltpu.SemaphoreType.DMA((len(blocks),)),
            ],
        ),
        out_shape=[
            jax.ShapeDtypeStruct((HEADS, KEYS_HERE, 256), jnp.bfloat16),
            jax.ShapeDtypeStruct((HEADS, 1, 256), jnp.float32),
            jax.ShapeDtypeStruct((HEADS, 1, 256), jnp.float32),
            jax.ShapeDtypeStruct((ROWS, DI), jnp.bfloat16),
        ],
        cost_estimate=pl.CostEstimate(
            flops=4 * HEADS * KEYS_HERE * 256 * DQ,
            bytes_accessed=HEADS * KEYS_HERE * 512,
            transcendentals=HEADS * KEYS_HERE * 256,
        ),
        compiler_params=pltpu.CompilerParams(vmem_limit_bytes=VMEM),
        name="scores",
    )(meta, *blocks, qa, qb, na, nb, ma, mb, wa, wb)


def head_sum_kernel(meta, e_ref, r_ref, o0, o1, o2, o3, total_ref):
    i = pl.program_id(0)
    total = jnp.zeros((HALF, 256), jnp.float32)
    for h in range(HEADS):
        total = total + e_ref[h].astype(jnp.float32) * r_ref[h]
    total_ref[...] = total
    slot = meta[BLOCKS + i]
    quarter = meta[34]
    at = pl.ds(pl.multiple_of(slot * UNIT, UNIT), UNIT)
    extra = pl.ds(pl.multiple_of(256 + (slot >> 2) * UNIT, UNIT), UNIT)
    for k, out in enumerate((o0, o1, o2, o3)):
        unit = pl.multiple_of((quarter ^ k) * UNIT, UNIT)
        out[at, :] = total_ref[pl.ds(unit, UNIT), :].astype(jnp.bfloat16)

        @pl.when((slot & 3) == (quarter ^ k))
        def _():
            out[extra, :] = total_ref[4 * UNIT :, :].astype(jnp.bfloat16)


def head_sum_call(meta, exps, ratio):
    piece = pl.BlockSpec((HEADS, HALF, 256), lambda i, meta: (0, i, 0))
    ratios = pl.BlockSpec((HEADS, 1, 256), lambda i, meta: (0, 0, 0))
    out = pl.BlockSpec((ROWS, 256), lambda i, meta: (0, 0))
    return pl.pallas_call(
        head_sum_kernel,
        grid_spec=pltpu.PrefetchScalarGridSpec(
            num_scalar_prefetch=1,
            grid=(BLOCKS,),
            in_specs=[piece, ratios],
            out_specs=[out] * 4,
            scratch_shapes=[pltpu.VMEM((HALF, 256), jnp.float32)],
        ),
        out_shape=[jax.ShapeDtypeStruct((ROWS, 256), jnp.bfloat16)] * 4,
        cost_estimate=pl.CostEstimate(flops=0, bytes_accessed=11 << 20, transcendentals=0),
        compiler_params=pltpu.CompilerParams(vmem_limit_bytes=VMEM),
        name="head_sum",
    )(meta, exps, ratio)


def key_places(meta):
    core, half, quarter = meta[32], meta[33], meta[34]
    rows = lax.broadcasted_iota(jnp.int32, (UNIT, 256), 0)
    out = []
    for u in range(16):
        out.append(rows + ((u // 2 * 4 + (u % 2) * 2 + core) * 160 + half * HALF + quarter * UNIT))
    for e in range(4):
        z, ylo = 2 * e + (quarter >> 1), quarter & 1
        out.append(rows + ((z * 4 + ylo * 2 + core) * 160 + half * HALF + 4 * UNIT))
    return out


def inner_of(keys, ia, ib, j):
    queries = jnp.concatenate([ia[j], ib[j]], axis=0)
    return lax.dot_general(
        keys[...], queries, (((1,), (1,)), ((), ())), preferred_element_type=jnp.float32
    ), queries


JSTEP = 8


def forward_kernel(meta, keys, ia, ib, wa, wb, wja, wjb, logits, stats):
    step = pl.program_id(0)

    @pl.when(step == 0)
    def _():
        logits[...] = jnp.zeros_like(logits)

    total = logits[...]
    for j in range(JSTEP):
        inner, _ = inner_of(keys, ia, ib, j)
        weight = jnp.concatenate([wja[j : j + 1, :], wjb[j : j + 1, :]], axis=1)
        total = total + weight * jnp.maximum(inner, 0.0)
    logits[...] = total

    @pl.when(step == NI // JSTEP - 1)
    def _():
        place = jnp.concatenate([wa[NI : NI + 1, :], wb[NI : NI + 1, :]], axis=1)
        places = key_places(meta)
        top = jnp.full((1, 256), NEG, jnp.float32)
        for u in range(20):
            cut = slice(u * UNIT, (u + 1) * UNIT)
            value = logits[cut, :] * INDEX_SCALE
            value = jnp.where(places[u].astype(jnp.float32) <= place, value, NEG)
            logits[cut, :] = value
            top = jnp.maximum(top, jnp.max(value, axis=0, keepdims=True))
        safe = jnp.where(top == NEG, 0.0, top)
        total = jnp.sum(jnp.exp(logits[...] - safe), axis=0, keepdims=True)
        stats[...] = jnp.zeros_like(stats)
        stats[0:1, :] = top
        stats[1:2, :] = total


def j_specs():
    whole = lambda shape: pl.BlockSpec(shape, lambda s, meta: (0,) * len(shape))
    queries = pl.BlockSpec((JSTEP, 128, DI), lambda s, meta: (s, 0, 0))
    weights = pl.BlockSpec((JSTEP, 128), lambda s, meta: (s, 0))
    return whole, [queries, queries, whole((72, 128)), whole((72, 128)), weights, weights]


def forward_call(meta, keys, ia, ib, wa, wb):
    whole, specs = j_specs()
    return pl.pallas_call(
        forward_kernel,
        grid_spec=pltpu.PrefetchScalarGridSpec(
            num_scalar_prefetch=1,
            grid=(NI // JSTEP,),
            in_specs=[whole((ROWS, DI))] + specs,
            out_specs=[whole((ROWS, 256)), whole((8, 256))],
        ),
        out_shape=[
            jax.ShapeDtypeStruct((ROWS, 256), jnp.float32),
            jax.ShapeDtypeStruct((8, 256), jnp.float32),
        ],
        cost_estimate=pl.CostEstimate(
            flops=2 * NI * ROWS * 256 * DI, bytes_accessed=5 << 20, transcendentals=0
        ),
        compiler_params=pltpu.CompilerParams(vmem_limit_bytes=VMEM),
        name="index_forward",
    )(meta, keys, ia, ib, wa, wb, wa, wb)


def backward_kernel(meta, keys, logits, s0, s1, s2, s3, t0, t1, t2, t3, ia, ib, wa, wb, wja, wjb, wg, div, kg, grad, acc):
    step = pl.program_id(0)

    @pl.when(step == 0)
    def _():
        stats = (s0, s1, s2, s3)
        tops = [part[0:1, :] for part in stats]
        top = tops[0]
        for other in tops[1:]:
            top = jnp.maximum(top, other)
        total = jnp.zeros((1, 256), jnp.float32)
        for part, other in zip(stats, tops):
            total = total + part[1:2, :] * jnp.exp(other - top)
        norm = top + jnp.log(total)
        goal = jnp.zeros((ROWS, 256), jnp.float32)
        for part in (t0, t1, t2, t3):
            goal = goal + part[...].astype(jnp.float32)
        goal = goal * (1.0 / 64.0)
        value = logits[...]
        seen = value != NEG
        logp = value - norm
        live = seen & (goal > 0)
        safe = jnp.where(goal > 0, goal, 1.0)
        part = jnp.where(live, goal * (jnp.log(safe) - logp), 0.0)
        div[...] = jnp.zeros_like(div)
        div[0:1, :] = jnp.sum(part, axis=0, keepdims=True)
        grad[...] = jnp.where(seen, jnp.exp(logp) - goal, 0.0) * INDEX_SCALE
        acc[...] = jnp.zeros_like(acc)

    total = acc[...]
    slope = grad[...]
    for j in range(JSTEP):
        inner, queries = inner_of(keys, ia, ib, j)
        weight = jnp.concatenate([wja[j : j + 1, :], wjb[j : j + 1, :]], axis=1)
        wg[j : j + 1, :] = jnp.sum(slope * jnp.maximum(inner, 0.0), axis=0, keepdims=True)
        coeff = jnp.where(inner > 0, slope * weight, 0.0).astype(jnp.bfloat16)
        total = total + jnp.dot(coeff, queries, preferred_element_type=jnp.float32)
    acc[...] = total

    @pl.when(step == NI // JSTEP - 1)
    def _():
        quarter = meta[34]
        for b in range(BLOCKS):
            kg[b, 0:UNIT, :] = acc[b * UNIT : (b + 1) * UNIT, :].astype(jnp.bfloat16)
            at = 256 + (b // 4) * UNIT
            extra = jnp.where(quarter == b % 4, acc[at : at + UNIT, :], 0.0)
            kg[b, UNIT:, :] = extra.astype(jnp.bfloat16)


def backward_call(meta, keys, logits, stats, target, ia, ib, wa, wb):
    whole, specs = j_specs()
    return pl.pallas_call(
        backward_kernel,
        grid_spec=pltpu.PrefetchScalarGridSpec(
            num_scalar_prefetch=1,
            grid=(NI // JSTEP,),
            in_specs=[
                whole((ROWS, DI)),
                whole((ROWS, 256)),
            ]
            + [whole((8, 256))] * 4
            + [whole((ROWS, 256))] * 4
            + specs,
            out_specs=[
                pl.BlockSpec((JSTEP, 256), lambda s, meta: (s, 0)),
                whole((8, 256)),
                whole((BLOCKS, 2 * UNIT, DI)),
            ],
            scratch_shapes=[
                pltpu.VMEM((ROWS, 256), jnp.float32),
                pltpu.VMEM((ROWS, DI), jnp.float32),
            ],
        ),
        out_shape=[
            jax.ShapeDtypeStruct((NI, 256), jnp.float32),
            jax.ShapeDtypeStruct((8, 256), jnp.float32),
            jax.ShapeDtypeStruct((BLOCKS, 2 * UNIT, DI), jnp.bfloat16),
        ],
        cost_estimate=pl.CostEstimate(
            flops=4 * NI * ROWS * 256 * DI, bytes_accessed=6 << 20, transcendentals=0
        ),
        compiler_params=pltpu.CompilerParams(vmem_limit_bytes=VMEM),
        name="index_backward",
    )(meta, keys, logits, *stats, *target, ia, ib, wa, wb, wa, wb)


def merge(m0, l0, m1, l1):
    top = jnp.maximum(m0, m1)
    return top, l0 * jnp.exp2((m0 - top) * SCORE2) + l1 * jnp.exp2((m1 - top) * SCORE2)


def merge_rows(a, b):
    top = jnp.maximum(a[0:1], b[0:1])
    total = a[1:2] * jnp.exp(a[0:1] - top) + b[1:2] * jnp.exp(b[0:1] - top)
    return jnp.concatenate([top, total, jnp.zeros((6, 256), jnp.float32)])


def swap_halves(value):
    return jnp.concatenate([value[..., 128:], value[..., :128]], axis=-1)


def gather_head(value):
    wide = jnp.broadcast_to(value[None], (8,) + value.shape)
    return lax.all_to_all(wide, ("yhi", "xh", "xp"), 0, 0, tiled=True)


def after(value, *others):
    return lax.optimization_barrier((value,) + others)[0]


def body(main_queries, latent_keys, index_queries, index_weights, index_keys, tile_order, offset):
    z, ylo, core = lax.axis_index("z"), lax.axis_index("ylo"), lax.axis_index("core")
    half = lax.axis_index("xp")
    quarter = lax.axis_index("yhi") * 2 + lax.axis_index("xh")

    rows = jnp.arange(TILE, dtype=jnp.int32)
    place = (offset + (tile_order[:, None] * TILE + rows[None, :])).reshape(1, 128)
    wa = jnp.concatenate(
        [index_weights.T, place.astype(jnp.float32), jnp.zeros((7, 128), jnp.float32)], axis=0
    )
    own = jnp.concatenate([index_keys, latent_keys], axis=1)
    own = lax.dynamic_slice_in_dim(own, half * HALF, HALF, 0)

    queries = main_queries.transpose(0, 2, 1)
    f1, b1 = shift(own, dz=1), shift(own, dz=7)
    left, right = shift(queries[:4], dx=1), shift(queries[4:], dx=3)
    wb = swap_core(wa)
    queries_far = swap_core(queries)
    y0 = shift(own, dy=1)
    f2, b2 = shift(f1, dz=1), shift(b1, dz=7)
    y1 = shift(jnp.concatenate([f1, b1]), dy=3)
    ia = after(index_queries, f1).transpose(1, 0, 2)
    ib = swap_core(ia)
    f3, b3 = shift(f2, dz=1), shift(b2, dz=7)
    y2 = shift(jnp.concatenate([f2, b2]), dy=1)
    left, right = lax.optimization_barrier((left, right, f3))[:2]
    left_far, right_far = swap_core(left), swap_core(right)
    f4 = shift(f3, dz=1)
    y3 = shift(jnp.concatenate([f3, b3]), dy=3)
    y4 = shift(f4, dy=1)
    column = [(0, own), (-1, f1), (1, b1), (-2, f2), (2, b2), (-3, f3), (3, b3), (-4, f4)]
    blocks = [block for _, block in column] + [y0, y1, y2, y3, y4]

    steps = jnp.asarray([dz for dz, _ in column] * 2, dtype=jnp.int32)
    zs = (z + 8 + steps) % 8
    ys = ylo ^ jnp.asarray([0] * 8 + [1] * 8, dtype=jnp.int32)
    bases = (zs * 4 + ys * 2 + core) * 160 + half * HALF
    meta = jnp.concatenate(
        [bases, zs * 2 + ys, jnp.stack([core, half, quarter])]
    ).astype(jnp.int32)

    exps, m0, l0, keys = score_call(
        meta, blocks, queries, queries_far, left, left_far, right, right_far, wa, wb
    )
    m0, l0 = m0[:, 0], l0[:, 0]

    away = swap_core(swap_halves(jnp.stack([m0, l0])))
    m, l = merge(m0, l0, away[0], away[1])
    ours = jnp.stack([m, l])
    up = shift(jnp.concatenate([ours[:, 0:4], ours[:, 12:16]], axis=1), dx=1)
    down = shift(ours[:, 4:12], dx=3)
    theirs = jnp.concatenate([down[:, 4:], up[:, 4:], up[:, :4], down[:, :4]], axis=1)
    top, total = merge(m, l, theirs[0], theirs[1])
    ratio = (jnp.exp2((m0 - top) * SCORE2) / total)[:, None]

    logits, stats = forward_call(meta, keys, ia, ib, wa, wb)
    stats = merge_rows(stats, swap_core(swap_halves(stats)))
    stats = merge_rows(stats, shift(stats, dx=3))

    sums = head_sum_call(meta, exps, ratio)
    group = (dict(dx=2), dict(dy=2), dict(dx=2, dy=2))
    target = [sums[0]] + [shift(part, **move) for part, move in zip(sums[1:], group)]
    istats = [stats] + [shift(stats, **move) for move in group]

    wg, div, kg = backward_call(meta, keys, logits, istats, target, ia, ib, wa, wb)
    rows_out = jnp.concatenate([wg, div], axis=0)
    rows_out = rows_out[:, :128] + swap_core(rows_out[:, 128:])
    rows_high = lax.reduce_precision(rows_out, 8, 7)
    tail = rows_high[NI : NI + 1]
    tail = jnp.concatenate([rows_high, rows_out[NI : NI + 1] - tail, jnp.zeros((7, 128), jnp.float32)])
    kg = lax.all_to_all(kg, ("z", "ylo"), 0, 0, tiled=True)
    kg = jnp.sum(kg.astype(jnp.float32), axis=0)
    last = gather_head(jnp.concatenate([kg, tail]).astype(jnp.bfloat16)).astype(jnp.float32)
    rows_sum = jnp.sum(last[:, 2 * UNIT :], axis=0)
    pieces = last[:, : 2 * UNIT].reshape(4, 2, 2 * UNIT, DI)
    main = pieces[:, :, :UNIT].transpose(1, 0, 2, 3).reshape(2, 4 * UNIT, DI)
    extra = jnp.sum(pieces[:, :, UNIT:], axis=0)
    key_grad = jnp.concatenate([main, extra], axis=1).reshape(160, DI)
    return rows_sum[NI] + rows_sum[NI + 8], rows_sum[:NI].T, key_grad


def solution(mesh):
    fine = Mesh(np.asarray(mesh.devices).reshape(2, 2, 2, 8, 2, 2), ALL)
    head, ctx = ("yhi", "xh", "xp"), ("z", "ylo", "core")
    in_specs = (
        P(head, ctx, None),
        P(ctx, None),
        P(ctx, None, None),
        P(ctx, None),
        P(ctx, None),
        P(ctx),
        P(),
    )
    out_specs = (P(ctx), P(ctx, None), P(ctx, None))
    return jax.shard_map(body, mesh=fine, in_specs=in_specs, out_specs=out_specs, check_vma=False)
```

```python
import math

import jax
import jax.numpy as jnp
import numpy as np
from jax import lax
from jax.experimental import pallas as pl
from jax.experimental.pallas import tpu as pltpu
from jax.sharding import Mesh
from jax.sharding import PartitionSpec as P

TILE = 32
DQ = 576
DI = 128
NI = 64
HALF = 80
UNIT = 16
BLOCKS = 16
ROWS = 320
SCORE2 = 192.0 ** (-0.5) * math.log2(math.e)
INDEX_SCALE = DI ** (-0.5)
ALL = ("yhi", "xh", "xp", "z", "ylo", "core")
NEG = -jnp.inf
VMEM = 18 << 20


def flat(x, y, z, c):
    return ((y // 2) * 4 + x) * 32 + (z * 2 + (y % 2)) * 2 + c


def shift(value, dx=0, dy=0, dz=0, flip=0):
    pairs = [
        (flat(x, y, z, c), flat((x + dx) % 4, (y + dy) % 4, (z + dz) % 8, c ^ flip))
        for x in range(4)
        for y in range(4)
        for z in range(8)
        for c in range(2)
    ]
    return lax.ppermute(value, ALL, pairs)


def swap_core(value):
    return shift(value, flip=1)


LOG2E = math.log2(math.e)


def merge(m0, l0, m1, l1, rate):
    top = jnp.maximum(m0, m1)
    return top, l0 * jnp.exp2((m0 - top) * rate) + l1 * jnp.exp2((m1 - top) * rate)


def swapped(value):
    return jnp.concatenate([value[:, 128:], value[:, :128]], axis=1)


HEADS = 16
CHUNK = 8 * HALF


def score_kernel(first, spans, others, meta, *refs):
    n, e = len(spans), len(others)
    blocks, extras = refs[:n], refs[n : n + e]
    qa, qb, na, nb, ma, mb, wa, wb = refs[n + e : n + e + 8]
    refs = refs[n + e + 8 :]
    if e:
        e_ref, m_ref, l_ref, ik_ref, keys, bias, raw, tops, sems, index, isems = refs
    else:
        e_ref, m_ref, l_ref, keys, bias, raw, tops, sems = refs
    step = pl.program_id(0)
    cut = 320

    @pl.when(step == 0)
    def _():
        copies = []
        at = 0
        for i, (block, span) in enumerate(zip(blocks, spans)):
            copies.append(pltpu.make_async_copy(block, keys.at[at : at + span, :], sems.at[i]))
            copies[-1].start()
            at += span
        at = 0
        for i, (block, span) in enumerate(zip(extras, others)):
            source, rows = block.at[:, 0:DI], index.at[at : at + span, :]
            copies.append(pltpu.make_async_copy(source, rows, isems.at[i]))
            copies[-1].start()
            at += span
        place = jnp.concatenate([wa[NI : NI + 1, :], wb[NI : NI + 1, :]], axis=1)
        offsets = lax.broadcasted_iota(jnp.int32, (HALF, 256), 0).astype(jnp.float32)
        for i in range(8):
            base = meta[first + i].astype(jnp.float32)
            bias[i * HALF : (i + 1) * HALF, :] = jnp.where(offsets + base <= place, 0.0, NEG)
        tops[...] = jnp.zeros_like(tops)
        for copy in copies:
            copy.wait()
        if e:
            quarter = meta[34]
            for i in range(BLOCKS):
                slot = meta[BLOCKS + i]
                held = index if i < 8 else keys
                row = (i % 8) * HALF
                mine = pl.ds(pl.multiple_of(row + quarter * UNIT, UNIT), UNIT)
                ik_ref[pl.ds(pl.multiple_of(slot * UNIT, UNIT), UNIT), :] = held[mine, 0:DI]

                @pl.when((slot & 3) == quarter)
                def _():
                    extra = pl.multiple_of(256 + (slot >> 2) * UNIT, UNIT)
                    ik_ref[pl.ds(extra, UNIT), :] = held[row + 4 * UNIT : row + HALF, 0:DI]

    def work(now, last):
        for k in range(2):
            own = jnp.concatenate([qa[k], qb[k]], axis=1)
            left = jnp.concatenate([na[k], nb[k]], axis=1)
            right = jnp.concatenate([ma[k], mb[k]], axis=1)
            queries = jnp.where(step < 4, own, jnp.where(step < 6, left, right))
            top = jnp.max(tops[last, k], axis=0, keepdims=True)
            safe = jnp.where(top == NEG, 0.0, top)
            new = jnp.full((8, 256), NEG, jnp.float32)
            total = jnp.zeros((8, 256), jnp.float32)
            for t in range(0, CHUNK, cut):
                piece = slice(t, t + cut)
                scores = jnp.dot(keys[piece, DI:], queries, preferred_element_type=jnp.float32)
                scores = scores + bias[piece, :]
                raw[now, k, piece, :] = scores
                new = jnp.maximum(new, jnp.max(scores.reshape(cut // 8, 8, 256), axis=0))
                exps = jnp.exp2((raw[last, k, piece, :] - safe) * SCORE2)
                e_ref[k, piece, :] = exps.astype(jnp.bfloat16)
                total = total + jnp.sum(exps.reshape(cut // 8, 8, 256), axis=0)
            tops[now, k] = new
            head = pl.ds(2 * jnp.maximum(step - 1, 0) + k, 1)
            m_ref[head, :] = top
            l_ref[head, :] = jnp.sum(total, axis=0, keepdims=True)

    @pl.when(step % 2 == 0)
    def _():
        work(0, 1)

    @pl.when(step % 2 == 1)
    def _():
        work(1, 0)


def score_call(meta, first, blocks, extras, qa, qb, na, nb, ma, mb, wa, wb):
    spans, others = [b.shape[0] for b in blocks], [b.shape[0] for b in extras]
    whole = lambda shape: pl.BlockSpec(shape, lambda h, meta: (0,) * len(shape))

    def heads(start, count):
        return pl.BlockSpec((2, DQ, 128), lambda h, meta: (jnp.clip(h - start, 0, count - 1), 0, 0))

    lag = lambda shape: pl.BlockSpec((2,) + shape, lambda h, meta: (jnp.maximum(h - 1, 0), 0, 0))
    out_specs = [lag((CHUNK, 256)), whole((HEADS, 256)), whole((HEADS, 256))]
    out_shape = [
        jax.ShapeDtypeStruct((HEADS, CHUNK, 256), jnp.bfloat16),
        jax.ShapeDtypeStruct((HEADS, 256), jnp.float32),
        jax.ShapeDtypeStruct((HEADS, 256), jnp.float32),
    ]
    scratch = [
        pltpu.VMEM((CHUNK, DI + DQ), jnp.bfloat16),
        pltpu.VMEM((CHUNK, 256), jnp.float32),
        pltpu.VMEM((2, 2, CHUNK, 256), jnp.float32),
        pltpu.VMEM((2, 2, 8, 256), jnp.float32),
        pltpu.SemaphoreType.DMA((len(blocks),)),
    ]
    if extras:
        out_specs.append(whole((ROWS, DI)))
        out_shape.append(jax.ShapeDtypeStruct((ROWS, DI), jnp.bfloat16))
        scratch.append(pltpu.VMEM((CHUNK, DI), jnp.bfloat16))
        scratch.append(pltpu.SemaphoreType.DMA((len(extras),)))
    return pl.pallas_call(
        lambda *refs: score_kernel(first, spans, others, *refs),
        grid_spec=pltpu.PrefetchScalarGridSpec(
            num_scalar_prefetch=1,
            grid=(HEADS // 2 + 1,),
            in_specs=[pl.BlockSpec(memory_space=pl.ANY)] * (len(blocks) + len(extras))
            + [heads(0, 4)] * 2
            + [heads(4, 2)] * 2
            + [heads(6, 2)] * 2
            + [whole((72, 128))] * 2,
            out_specs=out_specs,
            scratch_shapes=scratch,
        ),
        out_shape=out_shape,
        cost_estimate=pl.CostEstimate(
            flops=4 * HEADS * CHUNK * 256 * DQ,
            bytes_accessed=HEADS * CHUNK * 512,
            transcendentals=HEADS * CHUNK * 256,
        ),
        compiler_params=pltpu.CompilerParams(vmem_limit_bytes=VMEM),
        name="scores",
    )(meta, *blocks, *extras, qa, qb, na, nb, ma, mb, wa, wb)


def head_sum_kernel(meta, e0, e1, m0, m1, here, up, down, o0, o1, o2, o3, total_ref, ratio):
    i = pl.program_id(0)

    @pl.when(i == 0)
    def _():
        def side(v):
            heads = [down[v, 4:8, :], up[v, 4:8, :], up[v, 0:4, :], down[v, 0:4, :]]
            return jnp.concatenate(heads, axis=0)

        top, total = merge(here[0, 0:16, :], here[1, 0:16, :], side(0), side(1), SCORE2)
        for c, m in enumerate((m0, m1)):
            ratio[c] = jnp.exp2((m[...] - top) * SCORE2) / total
        index = slice(HEADS, HEADS + 1)
        terms = []
        for left in merge(here[0, index, :], here[1, index, :], down[0, 8:9, :], down[1, 8:9, :], LOG2E):
            for _ in range(3):
                term = left.astype(jnp.bfloat16).astype(jnp.float32)
                terms.append(term)
                left = left - term
        packed = jnp.concatenate(terms + [jnp.zeros((10, 256), jnp.float32)], axis=0)
        for out in (o0, o1, o2, o3):
            out[ROWS:, :] = packed.astype(jnp.bfloat16)

    def add(e_ref, c):
        total = jnp.zeros((HALF, 256), jnp.float32)
        for h in range(HEADS):
            total = total + e_ref[h].astype(jnp.float32) * ratio[c, h : h + 1, :]
        total_ref[...] = total

    @pl.when(i < 8)
    def _():
        add(e0, 0)

    @pl.when(i >= 8)
    def _():
        add(e1, 1)

    slot = meta[BLOCKS + i]
    quarter = meta[34]
    at = pl.ds(pl.multiple_of(slot * UNIT, UNIT), UNIT)
    extra = pl.ds(pl.multiple_of(256 + (slot >> 2) * UNIT, UNIT), UNIT)
    for k, out in enumerate((o0, o1, o2, o3)):
        unit = pl.multiple_of((quarter ^ k) * UNIT, UNIT)
        out[at, :] = total_ref[pl.ds(unit, UNIT), :].astype(jnp.bfloat16)

        @pl.when((slot & 3) == (quarter ^ k))
        def _():
            out[extra, :] = total_ref[4 * UNIT :, :].astype(jnp.bfloat16)


def head_sum_call(meta, e0, e1, *stats):
    early = pl.BlockSpec((HEADS, HALF, 256), lambda i, meta: (0, jnp.minimum(i, 7), 0))
    late = pl.BlockSpec((HEADS, HALF, 256), lambda i, meta: (0, jnp.maximum(i - 8, 0), 0))
    whole = lambda shape: pl.BlockSpec(shape, lambda i, meta: (0,) * len(shape))
    out = pl.BlockSpec((ROWS + UNIT, 256), lambda i, meta: (0, 0))
    return pl.pallas_call(
        head_sum_kernel,
        grid_spec=pltpu.PrefetchScalarGridSpec(
            num_scalar_prefetch=1,
            grid=(BLOCKS,),
            in_specs=[early, late] + [whole(part.shape) for part in stats],
            out_specs=[out] * 4,
            scratch_shapes=[
                pltpu.VMEM((HALF, 256), jnp.float32),
                pltpu.VMEM((2, HEADS, 256), jnp.float32),
            ],
        ),
        out_shape=[jax.ShapeDtypeStruct((ROWS + UNIT, 256), jnp.bfloat16)] * 4,
        cost_estimate=pl.CostEstimate(flops=0, bytes_accessed=11 << 20, transcendentals=0),
        compiler_params=pltpu.CompilerParams(vmem_limit_bytes=VMEM),
        name="head_sum",
    )(meta, e0, e1, *stats)


def key_places(meta):
    core, half, quarter = meta[32], meta[33], meta[34]
    rows = lax.broadcasted_iota(jnp.int32, (UNIT, 256), 0)
    out = []
    for u in range(16):
        out.append(rows + ((u // 2 * 4 + (u % 2) * 2 + core) * 160 + half * HALF + quarter * UNIT))
    for e in range(4):
        z, ylo = 2 * e + (quarter >> 1), quarter & 1
        out.append(rows + ((z * 4 + ylo * 2 + core) * 160 + half * HALF + 4 * UNIT))
    return out


def inner_of(keys, ia, ib, j):
    queries = jnp.concatenate([ia[j], ib[j]], axis=0)
    return lax.dot_general(
        keys[...], queries, (((1,), (1,)), ((), ())), preferred_element_type=jnp.float32
    ), queries


JSTEP = 32


def forward_kernel(meta, keys, m0, l0, m1, l1, ia, ib, wa, wb, wja, wjb, logits, here, sent):
    step = pl.program_id(0)

    @pl.when(step == 0)
    def _():
        logits[...] = jnp.zeros_like(logits)

    total = logits[...]
    for j in range(JSTEP):
        inner, _ = inner_of(keys, ia, ib, j)
        weight = jnp.concatenate([wja[j : j + 1, :], wjb[j : j + 1, :]], axis=1)
        total = total + weight * jnp.maximum(inner, 0.0)
    logits[...] = total

    @pl.when(step == NI // JSTEP - 1)
    def _():
        place = jnp.concatenate([wa[NI : NI + 1, :], wb[NI : NI + 1, :]], axis=1)
        places = key_places(meta)
        top = jnp.full((1, 256), NEG, jnp.float32)
        for u in range(20):
            cut = slice(u * UNIT, (u + 1) * UNIT)
            value = logits[cut, :] * INDEX_SCALE
            value = jnp.where(places[u].astype(jnp.float32) <= place, value, NEG)
            logits[cut, :] = value
            top = jnp.maximum(top, jnp.max(value, axis=0, keepdims=True))
        safe = jnp.where(top == NEG, 0.0, top)
        total = jnp.sum(jnp.exp(logits[...] - safe), axis=0, keepdims=True)
        tops, totals = merge(m0[...], l0[...], m1[...], l1[...], SCORE2)
        for v, (heads, index) in enumerate(((tops, top), (totals, total))):
            rows = jnp.concatenate([heads, index, jnp.zeros((7, 256), jnp.float32)], axis=0)
            here[v] = rows
            sent[v] = swapped(rows)


def pair_kernel(ours, theirs, here, up, down):
    index = slice(HEADS, HEADS + 1)
    heads = slice(0, HEADS)
    tops, totals = merge(ours[0, heads, :], ours[1, heads, :], theirs[0, heads, :], theirs[1, heads, :], SCORE2)
    top, total = merge(ours[0, index, :], ours[1, index, :], theirs[0, index, :], theirs[1, index, :], LOG2E)
    for v, (main, extra) in enumerate(((tops, top), (totals, total))):
        pad = jnp.zeros((7, 256), jnp.float32)
        here[v] = jnp.concatenate([main, extra, pad], axis=0)
        up[v] = jnp.concatenate([main[0:4], main[12:16]], axis=0)
        down[v] = jnp.concatenate([main[4:12], extra, pad], axis=0)


def pair_call(ours, theirs):
    return pl.pallas_call(
        pair_kernel,
        out_shape=[jax.ShapeDtypeStruct((2, rows, 256), jnp.float32) for rows in (24, 8, 16)],
        name="pair_statistics",
    )(ours, theirs)


def j_specs():
    whole = lambda shape: pl.BlockSpec(shape, lambda s, meta: (0,) * len(shape))
    queries = pl.BlockSpec((JSTEP, 128, DI), lambda s, meta: (s, 0, 0))
    weights = pl.BlockSpec((JSTEP, 128), lambda s, meta: (s, 0))
    return whole, [queries, queries, whole((72, 128)), whole((72, 128)), weights, weights]


def forward_call(meta, keys, stats, ia, ib, wa, wb):
    whole, specs = j_specs()
    return pl.pallas_call(
        forward_kernel,
        grid_spec=pltpu.PrefetchScalarGridSpec(
            num_scalar_prefetch=1,
            grid=(NI // JSTEP,),
            in_specs=[whole((ROWS, DI))] + [whole((HEADS, 256))] * 4 + specs,
            out_specs=[whole((ROWS, 256)), whole((2, 24, 256)), whole((2, 24, 256))],
        ),
        out_shape=[
            jax.ShapeDtypeStruct((ROWS, 256), jnp.float32),
            jax.ShapeDtypeStruct((2, 24, 256), jnp.float32),
            jax.ShapeDtypeStruct((2, 24, 256), jnp.float32),
        ],
        cost_estimate=pl.CostEstimate(
            flops=2 * NI * ROWS * 256 * DI, bytes_accessed=5 << 20, transcendentals=0
        ),
        compiler_params=pltpu.CompilerParams(vmem_limit_bytes=VMEM),
        name="index_forward",
    )(meta, keys, *stats, ia, ib, wa, wb, wa, wb)


def backward_kernel(meta, keys, logits, t0, t1, t2, t3, ia, ib, wa, wb, wja, wjb, rows_a, rows_b, kg, grad, acc):
    step = pl.program_id(0)

    @pl.when(step == 0)
    def _():
        parts = (t0, t1, t2, t3)

        def value(part, row):
            terms = part[ROWS:, :].astype(jnp.float32)
            return terms[row : row + 1] + terms[row + 1 : row + 2] + terms[row + 2 : row + 3]

        tops = [value(part, 0) for part in parts]
        top = tops[0]
        for other in tops[1:]:
            top = jnp.maximum(top, other)
        total = jnp.zeros((1, 256), jnp.float32)
        for part, other in zip(parts, tops):
            total = total + value(part, 3) * jnp.exp(other - top)
        norm = top + jnp.log(total)
        goal = jnp.zeros((ROWS, 256), jnp.float32)
        for part in parts:
            goal = goal + part[0:ROWS, :].astype(jnp.float32)
        goal = goal * (1.0 / 64.0)
        held = logits[...]
        seen = held != NEG
        logp = held - norm
        live = seen & (goal > 0)
        safe = jnp.where(goal > 0, goal, 1.0)
        part = jnp.where(live, goal * (jnp.log(safe) - logp), 0.0)
        part = jnp.sum(part, axis=0, keepdims=True)
        part = jnp.concatenate([part, jnp.zeros((15, 256), jnp.float32)], axis=0)
        rows_a[NI:, :] = part[:, :128]
        rows_b[NI:, :] = part[:, 128:]
        grad[...] = jnp.where(seen, jnp.exp(logp) - goal, 0.0) * INDEX_SCALE
        acc[...] = jnp.zeros_like(acc)

    total = acc[...]
    slope = grad[...]
    for j in range(JSTEP):
        inner, queries = inner_of(keys, ia, ib, j)
        weight = jnp.concatenate([wja[j : j + 1, :], wjb[j : j + 1, :]], axis=1)
        share = jnp.sum(slope * jnp.maximum(inner, 0.0), axis=0, keepdims=True)
        rows_a[pl.ds(step * JSTEP + j, 1), :] = share[:, :128]
        rows_b[pl.ds(step * JSTEP + j, 1), :] = share[:, 128:]
        coeff = jnp.where(inner > 0, slope * weight, 0.0).astype(jnp.bfloat16)
        total = total + jnp.dot(coeff, queries, preferred_element_type=jnp.float32)
    acc[...] = total

    @pl.when(step == NI // JSTEP - 1)
    def _():
        quarter = meta[34]
        for b in range(BLOCKS):
            kg[b, 0:UNIT, :] = acc[b * UNIT : (b + 1) * UNIT, :].astype(jnp.bfloat16)
            at = 256 + (b // 4) * UNIT
            extra = jnp.where(quarter == b % 4, acc[at : at + UNIT, :], 0.0)
            kg[b, UNIT:, :] = extra.astype(jnp.bfloat16)


def backward_call(meta, keys, logits, target, ia, ib, wa, wb):
    whole, specs = j_specs()
    return pl.pallas_call(
        backward_kernel,
        grid_spec=pltpu.PrefetchScalarGridSpec(
            num_scalar_prefetch=1,
            grid=(NI // JSTEP,),
            in_specs=[
                whole((ROWS, DI)),
                whole((ROWS, 256)),
            ]
            + [whole((ROWS + UNIT, 256))] * 4
            + specs,
            out_specs=[
                whole((NI + 16, 128)),
                whole((NI + 16, 128)),
                whole((BLOCKS, 2 * UNIT, DI)),
            ],
            scratch_shapes=[
                pltpu.VMEM((ROWS, 256), jnp.float32),
                pltpu.VMEM((ROWS, DI), jnp.float32),
            ],
        ),
        out_shape=[
            jax.ShapeDtypeStruct((NI + 16, 128), jnp.float32),
            jax.ShapeDtypeStruct((NI + 16, 128), jnp.float32),
            jax.ShapeDtypeStruct((BLOCKS, 2 * UNIT, DI), jnp.bfloat16),
        ],
        cost_estimate=pl.CostEstimate(
            flops=4 * NI * ROWS * 256 * DI, bytes_accessed=6 << 20, transcendentals=0
        ),
        compiler_params=pltpu.CompilerParams(vmem_limit_bytes=VMEM),
        name="index_backward",
    )(meta, keys, logits, *target, ia, ib, wa, wb, wa, wb)


def gather_head(value):
    wide = jnp.broadcast_to(value[None], (8,) + value.shape)
    return lax.all_to_all(wide, ("yhi", "xh", "xp"), 0, 0, tiled=True)


def after(value, *others):
    return lax.optimization_barrier((value,) + others)[0]


def body(main_queries, latent_keys, index_queries, index_weights, index_keys, tile_order, offset):
    z, ylo, core = lax.axis_index("z"), lax.axis_index("ylo"), lax.axis_index("core")
    half = lax.axis_index("xp")
    quarter = lax.axis_index("yhi") * 2 + lax.axis_index("xh")

    rows = jnp.arange(TILE, dtype=jnp.int32)
    place = (offset + (tile_order[:, None] * TILE + rows[None, :])).reshape(1, 128)
    wa = jnp.concatenate(
        [index_weights.T, place.astype(jnp.float32), jnp.zeros((7, 128), jnp.float32)], axis=0
    )
    own = jnp.concatenate([index_keys, latent_keys], axis=1)
    own = lax.dynamic_slice_in_dim(own, half * HALF, HALF, 0)

    queries = main_queries.transpose(0, 2, 1)
    f1, b1 = shift(own, dz=1), shift(own, dz=7)
    queries_far = swap_core(queries)
    halves = after(queries, f1)
    left, right = shift(halves[:4], dx=1), shift(halves[4:], dx=3)
    wb = swap_core(wa)
    f1, b1 = lax.optimization_barrier((f1, b1))
    f2, b2 = shift(f1, dz=1), shift(b1, dz=7)
    f2, b2 = lax.optimization_barrier((f2, b2))
    f3, b3 = shift(f2, dz=1), shift(b2, dz=7)
    f3, b3 = lax.optimization_barrier((f3, b3))
    left, right = lax.optimization_barrier((left, right, f3))[:2]
    left_far, right_far = swap_core(left), swap_core(right)
    f4 = shift(f3, dz=1)
    f4, ia = lax.optimization_barrier((f4, index_queries.transpose(1, 0, 2)))
    ib = swap_core(ia)
    y0 = shift(jnp.concatenate([own, f1, b1, f2]), dy=1)
    y1 = shift(jnp.concatenate([b2, f3, b3, f4]), dy=3)
    column = [(0, own), (-1, f1), (1, b1), (-2, f2), (2, b2), (-3, f3), (3, b3), (-4, f4)]

    steps = jnp.asarray([dz for dz, _ in column] * 2, dtype=jnp.int32)
    zs = (z + 8 + steps) % 8
    ys = ylo ^ jnp.asarray([0] * 8 + [1] * 8, dtype=jnp.int32)
    bases = (zs * 4 + ys * 2 + core) * 160 + half * HALF
    meta = jnp.concatenate(
        [bases, zs * 2 + ys, jnp.stack([core, half, quarter])]
    ).astype(jnp.int32)

    held = [block for _, block in column]
    sides = (queries, queries_far, left, left_far, right, right_far, wa, wb)
    e0, m0, l0 = score_call(meta, 0, held, [], *sides)
    e1, m1, l1, keys = score_call(meta, 8, [y0, y1], held, *sides)

    logits, ours, sent = forward_call(meta, keys, (m0, l0, m1, l1), ia, ib, wa, wb)
    here, up, down = pair_call(ours, swap_core(sent))
    up, down = shift(up, dx=1), shift(down, dx=3)
    sums = head_sum_call(meta, e0, e1, m0, m1, here, up, down)
    group = (dict(dx=2), dict(dy=2), dict(dx=2, dy=2))
    target = [sums[0]] + [shift(part, **move) for part, move in zip(sums[1:], group)]

    mine, other, kg = backward_call(meta, keys, logits, target, ia, ib, wa, wb)
    rows_out = mine + swap_core(other)
    rows_high = lax.reduce_precision(rows_out, 8, 7)
    low = jnp.concatenate([jnp.zeros((NI + 8, 128), jnp.float32), (rows_out - rows_high)[NI : NI + 8]])
    tail = rows_high + low
    kg = lax.all_to_all(kg, ("z", "ylo"), 0, 0, tiled=True)
    kg = jnp.sum(kg.astype(jnp.float32), axis=0)
    last = gather_head(jnp.concatenate([kg, tail]).astype(jnp.bfloat16)).astype(jnp.float32)
    rows_sum = jnp.sum(last[:, 2 * UNIT :], axis=0)
    pieces = last[:, : 2 * UNIT].reshape(4, 2, 2 * UNIT, DI)
    main = pieces[:, :, :UNIT].transpose(1, 0, 2, 3).reshape(2, 4 * UNIT, DI)
    extra = jnp.sum(pieces[:, :, UNIT:], axis=0)
    key_grad = jnp.concatenate([main, extra], axis=1).reshape(160, DI)
    return rows_sum[NI] + rows_sum[NI + 8], rows_sum[:NI].T, key_grad


def solution(mesh):
    fine = Mesh(np.asarray(mesh.devices).reshape(2, 2, 2, 8, 2, 2), ALL)
    head, ctx = ("yhi", "xh", "xp"), ("z", "ylo", "core")
    in_specs = (
        P(head, ctx, None),
        P(ctx, None),
        P(ctx, None, None),
        P(ctx, None),
        P(ctx, None),
        P(ctx),
        P(),
    )
    out_specs = (P(ctx), P(ctx, None), P(ctx, None))
    return jax.shard_map(body, mesh=fine, in_specs=in_specs, out_specs=out_specs, check_vma=False)
```

```python
import math

import jax
import jax.numpy as jnp
import numpy as np
from jax import lax
from jax.experimental import pallas as pl
from jax.experimental.pallas import tpu as pltpu
from jax.sharding import Mesh
from jax.sharding import PartitionSpec as P

TILE = 32
DQ = 576
DI = 128
NI = 64
HALF = 80
UNIT = 16
BLOCKS = 16
ROWS = 320
SCORE2 = 192.0 ** (-0.5) * math.log2(math.e)
INDEX_SCALE = DI ** (-0.5)
ALL = ("yhi", "xh", "xp", "z", "ylo", "core")
NEG = -jnp.inf
VMEM = 18 << 20


def flat(x, y, z, c):
    return ((y // 2) * 4 + x) * 32 + (z * 2 + (y % 2)) * 2 + c


def shift(value, dx=0, dy=0, dz=0, flip=0):
    pairs = [
        (flat(x, y, z, c), flat((x + dx) % 4, (y + dy) % 4, (z + dz) % 8, c ^ flip))
        for x in range(4)
        for y in range(4)
        for z in range(8)
        for c in range(2)
    ]
    return lax.ppermute(value, ALL, pairs)


def swap_core(value):
    return shift(value, flip=1)


LOG2E = math.log2(math.e)


def slot_of(meta, i):
    k = i & 7
    reach = (k + 1) >> 1
    step = reach * (1 - 2 * (k & 1))
    return ((meta[0] + 8 + step) & 7) * 2 + (meta[1] ^ (i >> 3))


def place_of(pa, pb):
    return jnp.concatenate([pa[...], pb[...]], axis=1)


def merge(m0, l0, m1, l1, rate):
    top = jnp.maximum(m0, m1)
    return top, l0 * jnp.exp2((m0 - top) * rate) + l1 * jnp.exp2((m1 - top) * rate)


def swapped(value):
    return jnp.concatenate([value[:, 128:], value[:, :128]], axis=1)


HEADS = 16
CHUNK = 8 * HALF


def score_kernel(chunk, spans, meta, *refs):
    n = len(spans)
    blocks, refs = refs[:n], refs[n:]
    if chunk:
        _, ik_before, refs = refs[0], refs[1], refs[2:]
    qa, qb, na, nb, ma, mb, pa, pb = refs[:8]
    e_ref, m_ref, l_ref, ik_ref, keys, bias, raw, tops, sems = refs[8:]
    step = pl.program_id(0)
    cut = 320

    @pl.when(step == 0)
    def _():
        copies = []
        at = 0
        for i, (block, span) in enumerate(zip(blocks, spans)):
            copies.append(pltpu.make_async_copy(block, keys.at[at : at + span, :], sems.at[i]))
            copies[-1].start()
            at += span
        place = place_of(pa, pb)
        offsets = lax.broadcasted_iota(jnp.int32, (HALF, 256), 0).astype(jnp.float32)
        slots = [slot_of(meta, 8 * chunk + i) for i in range(8)]
        for i in range(8):
            base = ((slots[i] * 2 + meta[2]) * 160 + meta[3] * HALF).astype(jnp.float32)
            bias[i * HALF : (i + 1) * HALF, :] = jnp.where(offsets + base <= place, 0.0, NEG)
        tops[...] = jnp.zeros_like(tops)
        ik_ref[...] = ik_before[...] if chunk else jnp.zeros_like(ik_ref)
        for copy in copies:
            copy.wait()
        quarter = meta[4]
        for i in range(8):
            slot = slots[i]
            mine = pl.ds(pl.multiple_of(i * HALF + quarter * UNIT, UNIT), UNIT)
            ik_ref[pl.ds(pl.multiple_of(slot * UNIT, UNIT), UNIT), :] = keys[mine, 0:DI]

            @pl.when((slot & 3) == quarter)
            def _():
                extra = pl.multiple_of(256 + (slot >> 2) * UNIT, UNIT)
                ik_ref[pl.ds(extra, UNIT), :] = keys[i * HALF + 4 * UNIT : (i + 1) * HALF, 0:DI]

    def work(now, last):
        for k in range(2):
            own = jnp.concatenate([qa[k], qb[k]], axis=1)
            left = jnp.concatenate([na[k], nb[k]], axis=1)
            right = jnp.concatenate([ma[k], mb[k]], axis=1)
            queries = jnp.where(step < 4, own, jnp.where(step < 6, left, right))
            top = jnp.max(tops[last, k], axis=0, keepdims=True)
            safe = jnp.where(top == NEG, 0.0, top)
            new = jnp.full((8, 256), NEG, jnp.float32)
            total = jnp.zeros((8, 256), jnp.float32)
            for t in range(0, CHUNK, cut):
                piece = slice(t, t + cut)
                scores = jnp.dot(keys[piece, DI:], queries, preferred_element_type=jnp.float32)
                scores = scores + bias[piece, :]
                raw[now, k, piece, :] = scores
                new = jnp.maximum(new, jnp.max(scores.reshape(cut // 8, 8, 256), axis=0))
                exps = jnp.exp2((raw[last, k, piece, :] - safe) * SCORE2)
                e_ref[k, piece, :] = exps.astype(jnp.bfloat16)
                total = total + jnp.sum(exps.reshape(cut // 8, 8, 256), axis=0)
            tops[now, k] = new
            head = pl.ds(2 * jnp.maximum(step - 1, 0) + k, 1)
            m_ref[head, :] = top
            l_ref[head, :] = jnp.sum(total, axis=0, keepdims=True)

    @pl.when(step % 2 == 0)
    def _():
        work(0, 1)

    @pl.when(step % 2 == 1)
    def _():
        work(1, 0)


def score_call(meta, chunk, blocks, before, qa, qb, na, nb, ma, mb, pa, pb):
    spans = [b.shape[0] for b in blocks]
    whole = lambda shape: pl.BlockSpec(shape, lambda h, meta: (0,) * len(shape))

    def heads(start, count):
        return pl.BlockSpec((2, DQ, 128), lambda h, meta: (jnp.clip(h - start, 0, count - 1), 0, 0))

    anywhere = pl.BlockSpec(memory_space=pl.ANY)
    exps = pl.BlockSpec((2, CHUNK, 256), lambda h, meta: (jnp.maximum(h - 1, 0), chunk, 0))
    return pl.pallas_call(
        lambda *refs: score_kernel(chunk, spans, *refs),
        grid_spec=pltpu.PrefetchScalarGridSpec(
            num_scalar_prefetch=1,
            grid=(HEADS // 2 + 1,),
            in_specs=[anywhere] * len(blocks)
            + ([anywhere, whole((ROWS, DI))] if chunk else [])
            + [heads(0, 4)] * 2
            + [heads(4, 2)] * 2
            + [heads(6, 2)] * 2
            + [whole((1, 128))] * 2,
            out_specs=[exps, whole((HEADS, 256)), whole((HEADS, 256)), whole((ROWS, DI))],
            scratch_shapes=[
                pltpu.VMEM((CHUNK, DI + DQ), jnp.bfloat16),
                pltpu.VMEM((CHUNK, 256), jnp.float32),
                pltpu.VMEM((2, 2, CHUNK, 256), jnp.float32),
                pltpu.VMEM((2, 2, 8, 256), jnp.float32),
                pltpu.SemaphoreType.DMA((len(blocks),)),
            ],
        ),
        out_shape=[
            jax.ShapeDtypeStruct((HEADS, 2 * CHUNK, 256), jnp.bfloat16),
            jax.ShapeDtypeStruct((HEADS, 256), jnp.float32),
            jax.ShapeDtypeStruct((HEADS, 256), jnp.float32),
            jax.ShapeDtypeStruct((ROWS, DI), jnp.bfloat16),
        ],
        input_output_aliases={1 + len(blocks): 0} if chunk else {},
        cost_estimate=pl.CostEstimate(
            flops=4 * HEADS * CHUNK * 256 * DQ,
            bytes_accessed=HEADS * CHUNK * 512,
            transcendentals=HEADS * CHUNK * 256,
        ),
        compiler_params=pltpu.CompilerParams(vmem_limit_bytes=VMEM),
        name="scores",
    )(meta, *blocks, *before, qa, qb, na, nb, ma, mb, pa, pb)


def head_sum_kernel(meta, e_ref, m0, m1, here, up, down, o0, o1, o2, o3, total_ref, ratio):
    i = pl.program_id(0)

    @pl.when(i == 0)
    def _():
        def side(v):
            heads = [down[v, 4:8, :], up[v, 4:8, :], up[v, 0:4, :], down[v, 0:4, :]]
            return jnp.concatenate(heads, axis=0)

        top, total = merge(here[0, 0:16, :], here[1, 0:16, :], side(0), side(1), SCORE2)
        for c, m in enumerate((m0, m1)):
            ratio[c] = jnp.exp2((m[...] - top) * SCORE2) / total
        index = slice(HEADS, HEADS + 1)
        terms = []
        for left in merge(here[0, index, :], here[1, index, :], down[0, 8:9, :], down[1, 8:9, :], LOG2E):
            for _ in range(3):
                term = left.astype(jnp.bfloat16).astype(jnp.float32)
                terms.append(term)
                left = left - term
        packed = jnp.concatenate(terms + [jnp.zeros((10, 256), jnp.float32)], axis=0)
        for out in (o0, o1, o2, o3):
            out[ROWS:, :] = packed.astype(jnp.bfloat16)

    chunk = i // 8
    total = jnp.zeros((HALF, 256), jnp.float32)
    for h in range(HEADS):
        total = total + e_ref[h].astype(jnp.float32) * ratio[chunk, h : h + 1, :]
    total_ref[...] = total
    slot = slot_of(meta, i)
    quarter = meta[4]
    at = pl.ds(pl.multiple_of(slot * UNIT, UNIT), UNIT)
    extra = pl.ds(pl.multiple_of(256 + (slot >> 2) * UNIT, UNIT), UNIT)
    for k, out in enumerate((o0, o1, o2, o3)):
        unit = pl.multiple_of((quarter ^ k) * UNIT, UNIT)
        out[at, :] = total_ref[pl.ds(unit, UNIT), :].astype(jnp.bfloat16)

        @pl.when((slot & 3) == (quarter ^ k))
        def _():
            out[extra, :] = total_ref[4 * UNIT :, :].astype(jnp.bfloat16)


def head_sum_call(meta, exps, *stats):
    piece = pl.BlockSpec((HEADS, HALF, 256), lambda i, meta: (0, i, 0))
    whole = lambda shape: pl.BlockSpec(shape, lambda i, meta: (0,) * len(shape))
    out = pl.BlockSpec((ROWS + UNIT, 256), lambda i, meta: (0, 0))
    return pl.pallas_call(
        head_sum_kernel,
        grid_spec=pltpu.PrefetchScalarGridSpec(
            num_scalar_prefetch=1,
            grid=(BLOCKS,),
            in_specs=[piece] + [whole(part.shape) for part in stats],
            out_specs=[out] * 4,
            scratch_shapes=[
                pltpu.VMEM((HALF, 256), jnp.float32),
                pltpu.VMEM((2, HEADS, 256), jnp.float32),
            ],
        ),
        out_shape=[jax.ShapeDtypeStruct((ROWS + UNIT, 256), jnp.bfloat16)] * 4,
        cost_estimate=pl.CostEstimate(flops=0, bytes_accessed=11 << 20, transcendentals=0),
        compiler_params=pltpu.CompilerParams(vmem_limit_bytes=VMEM),
        name="head_sum",
    )(meta, exps, *stats)


def key_places(meta):
    core, half, quarter = meta[2], meta[3], meta[4]
    rows = lax.broadcasted_iota(jnp.int32, (UNIT, 256), 0)
    out = []
    for u in range(16):
        out.append(rows + ((u // 2 * 4 + (u % 2) * 2 + core) * 160 + half * HALF + quarter * UNIT))
    for e in range(4):
        z, ylo = 2 * e + (quarter >> 1), quarter & 1
        out.append(rows + ((z * 4 + ylo * 2 + core) * 160 + half * HALF + 4 * UNIT))
    return out


def inner_of(keys, ia, ib, j):
    queries = jnp.concatenate([ia[j], ib[j]], axis=0)
    return lax.dot_general(
        keys[...], queries, (((1,), (1,)), ((), ())), preferred_element_type=jnp.float32
    ), queries


JSTEP = 32


def forward_kernel(meta, keys, m0, l0, m1, l1, ia, ib, pa, pb, wja, wjb, logits, here, sent):
    step = pl.program_id(0)

    @pl.when(step == 0)
    def _():
        logits[...] = jnp.zeros_like(logits)

    total = logits[...]
    for j in range(JSTEP):
        inner, _ = inner_of(keys, ia, ib, j)
        weight = jnp.concatenate([wja[j : j + 1, :], wjb[j : j + 1, :]], axis=1)
        total = total + weight * jnp.maximum(inner, 0.0)
    logits[...] = total

    @pl.when(step == NI // JSTEP - 1)
    def _():
        place = place_of(pa, pb)
        places = key_places(meta)
        top = jnp.full((1, 256), NEG, jnp.float32)
        for u in range(20):
            cut = slice(u * UNIT, (u + 1) * UNIT)
            value = logits[cut, :] * INDEX_SCALE
            value = jnp.where(places[u].astype(jnp.float32) <= place, value, NEG)
            logits[cut, :] = value
            top = jnp.maximum(top, jnp.max(value, axis=0, keepdims=True))
        safe = jnp.where(top == NEG, 0.0, top)
        total = jnp.sum(jnp.exp(logits[...] - safe), axis=0, keepdims=True)
        tops, totals = merge(m0[...], l0[...], m1[...], l1[...], SCORE2)
        for v, (heads, index) in enumerate(((tops, top), (totals, total))):
            rows = jnp.concatenate([heads, index, jnp.zeros((7, 256), jnp.float32)], axis=0)
            here[v] = rows
            sent[v] = swapped(rows)


def pair_kernel(ours, theirs, here, up, down):
    index = slice(HEADS, HEADS + 1)
    heads = slice(0, HEADS)
    tops, totals = merge(ours[0, heads, :], ours[1, heads, :], theirs[0, heads, :], theirs[1, heads, :], SCORE2)
    top, total = merge(ours[0, index, :], ours[1, index, :], theirs[0, index, :], theirs[1, index, :], LOG2E)
    for v, (main, extra) in enumerate(((tops, top), (totals, total))):
        pad = jnp.zeros((7, 256), jnp.float32)
        here[v] = jnp.concatenate([main, extra, pad], axis=0)
        up[v] = jnp.concatenate([main[0:4], main[12:16]], axis=0)
        down[v] = jnp.concatenate([main[4:12], extra, pad], axis=0)


def pair_call(ours, theirs):
    return pl.pallas_call(
        pair_kernel,
        out_shape=[jax.ShapeDtypeStruct((2, rows, 256), jnp.float32) for rows in (24, 8, 16)],
        name="pair_statistics",
    )(ours, theirs)


def j_specs():
    whole = lambda shape: pl.BlockSpec(shape, lambda s, meta: (0,) * len(shape))
    queries = pl.BlockSpec((JSTEP, 128, DI), lambda s, meta: (s, 0, 0))
    weights = pl.BlockSpec((JSTEP, 128), lambda s, meta: (s, 0))
    return whole, [queries, queries], [weights, weights]


def forward_call(meta, keys, stats, ia, ib, pa, pb, wa, wb):
    whole, queries, weights = j_specs()
    return pl.pallas_call(
        forward_kernel,
        grid_spec=pltpu.PrefetchScalarGridSpec(
            num_scalar_prefetch=1,
            grid=(NI // JSTEP,),
            in_specs=[whole((ROWS, DI))] + [whole((HEADS, 256))] * 4 + queries + [whole((1, 128))] * 2 + weights,
            out_specs=[whole((ROWS, 256)), whole((2, 24, 256)), whole((2, 24, 256))],
        ),
        out_shape=[
            jax.ShapeDtypeStruct((ROWS, 256), jnp.float32),
            jax.ShapeDtypeStruct((2, 24, 256), jnp.float32),
            jax.ShapeDtypeStruct((2, 24, 256), jnp.float32),
        ],
        cost_estimate=pl.CostEstimate(
            flops=2 * NI * ROWS * 256 * DI, bytes_accessed=5 << 20, transcendentals=0
        ),
        compiler_params=pltpu.CompilerParams(vmem_limit_bytes=VMEM),
        name="index_forward",
    )(meta, keys, *stats, ia, ib, pa, pb, wa, wb)


def backward_kernel(meta, keys, logits, t0, t1, t2, t3, ia, ib, wja, wjb, rows_a, rows_b, kg, grad, acc):
    step = pl.program_id(0)

    @pl.when(step == 0)
    def _():
        parts = (t0, t1, t2, t3)

        def value(part, row):
            terms = part[ROWS:, :].astype(jnp.float32)
            return terms[row : row + 1] + terms[row + 1 : row + 2] + terms[row + 2 : row + 3]

        tops = [value(part, 0) for part in parts]
        top = tops[0]
        for other in tops[1:]:
            top = jnp.maximum(top, other)
        total = jnp.zeros((1, 256), jnp.float32)
        for part, other in zip(parts, tops):
            total = total + value(part, 3) * jnp.exp(other - top)
        norm = top + jnp.log(total)
        goal = jnp.zeros((ROWS, 256), jnp.float32)
        for part in parts:
            goal = goal + part[0:ROWS, :].astype(jnp.float32)
        goal = goal * (1.0 / 64.0)
        held = logits[...]
        seen = held != NEG
        logp = held - norm
        live = seen & (goal > 0)
        safe = jnp.where(goal > 0, goal, 1.0)
        part = jnp.where(live, goal * (jnp.log(safe) - logp), 0.0)
        part = jnp.sum(part, axis=0, keepdims=True)
        part = jnp.concatenate([part, jnp.zeros((15, 256), jnp.float32)], axis=0)
        rows_a[NI:, :] = part[:, :128]
        rows_b[NI:, :] = part[:, 128:]
        grad[...] = jnp.where(seen, jnp.exp(logp) - goal, 0.0) * INDEX_SCALE
        acc[...] = jnp.zeros_like(acc)

    total = acc[...]
    slope = grad[...]
    for j in range(JSTEP):
        inner, queries = inner_of(keys, ia, ib, j)
        weight = jnp.concatenate([wja[j : j + 1, :], wjb[j : j + 1, :]], axis=1)
        share = jnp.sum(slope * jnp.maximum(inner, 0.0), axis=0, keepdims=True)
        rows_a[pl.ds(step * JSTEP + j, 1), :] = share[:, :128]
        rows_b[pl.ds(step * JSTEP + j, 1), :] = share[:, 128:]
        coeff = jnp.where(inner > 0, slope * weight, 0.0).astype(jnp.bfloat16)
        total = total + jnp.dot(coeff, queries, preferred_element_type=jnp.float32)
    acc[...] = total

    @pl.when(step == NI // JSTEP - 1)
    def _():
        quarter = meta[4]
        for b in range(BLOCKS):
            kg[b, 0:UNIT, :] = acc[b * UNIT : (b + 1) * UNIT, :].astype(jnp.bfloat16)
            at = 256 + (b // 4) * UNIT
            extra = jnp.where(quarter == b % 4, acc[at : at + UNIT, :], 0.0)
            kg[b, UNIT:, :] = extra.astype(jnp.bfloat16)


def backward_call(meta, keys, logits, target, ia, ib, wa, wb):
    whole, queries, weights = j_specs()
    return pl.pallas_call(
        backward_kernel,
        grid_spec=pltpu.PrefetchScalarGridSpec(
            num_scalar_prefetch=1,
            grid=(NI // JSTEP,),
            in_specs=[
                whole((ROWS, DI)),
                whole((ROWS, 256)),
            ]
            + [whole((ROWS + UNIT, 256))] * 4
            + queries
            + weights,
            out_specs=[
                whole((NI + 16, 128)),
                whole((NI + 16, 128)),
                whole((BLOCKS, 2 * UNIT, DI)),
            ],
            scratch_shapes=[
                pltpu.VMEM((ROWS, 256), jnp.float32),
                pltpu.VMEM((ROWS, DI), jnp.float32),
            ],
        ),
        out_shape=[
            jax.ShapeDtypeStruct((NI + 16, 128), jnp.float32),
            jax.ShapeDtypeStruct((NI + 16, 128), jnp.float32),
            jax.ShapeDtypeStruct((BLOCKS, 2 * UNIT, DI), jnp.bfloat16),
        ],
        cost_estimate=pl.CostEstimate(
            flops=4 * NI * ROWS * 256 * DI, bytes_accessed=6 << 20, transcendentals=0
        ),
        compiler_params=pltpu.CompilerParams(vmem_limit_bytes=VMEM),
        name="index_backward",
    )(meta, keys, logits, *target, ia, ib, wa, wb)


def gather_head(value):
    wide = jnp.broadcast_to(value[None], (8,) + value.shape)
    return lax.all_to_all(wide, ("yhi", "xh", "xp"), 0, 0, tiled=True)


def after(value, *others):
    return lax.optimization_barrier((value,) + others)[0]


def body(main_queries, latent_keys, index_queries, index_weights, index_keys, tile_order, offset):
    z, ylo, core = lax.axis_index("z"), lax.axis_index("ylo"), lax.axis_index("core")
    half = lax.axis_index("xp")
    quarter = lax.axis_index("yhi") * 2 + lax.axis_index("xh")

    rows = jnp.arange(TILE, dtype=jnp.int32)
    place = (offset + (tile_order[:, None] * TILE + rows[None, :])).reshape(1, 128)
    pa, wa = place.astype(jnp.float32), index_weights.T
    own = jnp.concatenate([index_keys, latent_keys], axis=1)
    own = lax.dynamic_slice_in_dim(own, half * HALF, HALF, 0)

    queries = main_queries.transpose(0, 2, 1)
    f1, b1 = shift(own, dz=1), shift(own, dz=7)
    queries_far = swap_core(queries)
    left, right = shift(queries[:4], dx=1), shift(queries[4:], dx=3)
    f1, b1 = lax.optimization_barrier((f1, b1))
    f2, b2 = shift(f1, dz=1), shift(b1, dz=7)
    f2, b2 = lax.optimization_barrier((f2, b2))
    f3, b3 = shift(f2, dz=1), shift(b2, dz=7)
    f3, b3 = lax.optimization_barrier((f3, b3))
    f4 = shift(f3, dz=1)
    ia = index_queries.transpose(1, 0, 2)
    pb = swap_core(pa)
    f4, ia, pb, left, right = lax.optimization_barrier((f4, ia, pb, left, right))
    y0, y1 = jnp.concatenate([own, f1, b1, f2]), jnp.concatenate([b2, f3, b3, f4])
    y0, y1, left, right = lax.optimization_barrier((y0, y1, left, right))
    y0, y1 = shift(y0, dy=1), shift(y1, dy=3)
    left_far, right_far = swap_core(left), swap_core(right)
    ia, wa = lax.optimization_barrier((ia, wa, left_far, right_far))[:2]
    ib, wb = swap_core(ia), swap_core(wa)
    meta = jnp.stack([z, ylo, core, half, quarter]).astype(jnp.int32)

    sides = (queries, queries_far, left, left_far, right, right_far, pa, pb)
    exps, m0, l0, keys = score_call(meta, 0, [own, f1, b1, f2, b2, f3, b3, f4], [], *sides)
    exps, m1, l1, keys = score_call(meta, 1, [y0, y1], [exps, keys], *sides)

    logits, ours, sent = forward_call(meta, keys, (m0, l0, m1, l1), ia, ib, pa, pb, wa, wb)
    here, up, down = pair_call(ours, swap_core(sent))
    up, down = shift(up, dx=1), shift(down, dx=3)
    sums = head_sum_call(meta, exps, m0, m1, here, up, down)
    group = (dict(dx=2), dict(dy=2), dict(dx=2, dy=2))
    target = [sums[0]] + [shift(part, **move) for part, move in zip(sums[1:], group)]

    mine, other, kg = backward_call(meta, keys, logits, target, ia, ib, wa, wb)
    rows_out = mine + swap_core(other)
    rows_high = lax.reduce_precision(rows_out, 8, 7)
    low = jnp.concatenate([jnp.zeros((NI + 8, 128), jnp.float32), (rows_out - rows_high)[NI : NI + 8]])
    tail = rows_high + low
    kg = lax.all_to_all(kg, ("z", "ylo"), 0, 0, tiled=True)
    kg = jnp.sum(kg.astype(jnp.float32), axis=0)
    last = gather_head(jnp.concatenate([kg, tail]).astype(jnp.bfloat16)).astype(jnp.float32)
    rows_sum = jnp.sum(last[:, 2 * UNIT :], axis=0)
    pieces = last[:, : 2 * UNIT].reshape(4, 2, 2 * UNIT, DI)
    main = pieces[:, :, :UNIT].transpose(1, 0, 2, 3).reshape(2, 4 * UNIT, DI)
    extra = jnp.sum(pieces[:, :, UNIT:], axis=0)
    key_grad = jnp.concatenate([main, extra], axis=1).reshape(160, DI)
    return rows_sum[NI] + rows_sum[NI + 8], rows_sum[:NI].T, key_grad


def solution(mesh):
    fine = Mesh(np.asarray(mesh.devices).reshape(2, 2, 2, 8, 2, 2), ALL)
    head, ctx = ("yhi", "xh", "xp"), ("z", "ylo", "core")
    in_specs = (
        P(head, ctx, None),
        P(ctx, None),
        P(ctx, None, None),
        P(ctx, None),
        P(ctx, None),
        P(ctx),
        P(),
    )
    out_specs = (P(ctx), P(ctx, None), P(ctx, None))
    return jax.shard_map(body, mesh=fine, in_specs=in_specs, out_specs=out_specs, check_vma=False)
```

```python
import math

import jax
import jax.numpy as jnp
import numpy as np
from jax import lax
from jax.experimental import pallas as pl
from jax.experimental.pallas import tpu as pltpu
from jax.sharding import Mesh
from jax.sharding import PartitionSpec as P

TILE = 32
DQ = 576
DI = 128
NI = 64
HALF = 80
UNIT = 16
BLOCKS = 16
ROWS = 320
SCORE2 = 192.0 ** (-0.5) * math.log2(math.e)
INDEX_SCALE = DI ** (-0.5)
ALL = ("yhi", "xh", "xp", "z", "ylo", "core")
NEG = -jnp.inf
VMEM = 18 << 20


def flat(x, y, z, c):
    return ((y // 2) * 4 + x) * 32 + (z * 2 + (y % 2)) * 2 + c


def shift(value, dx=0, dy=0, dz=0, flip=0):
    pairs = [
        (flat(x, y, z, c), flat((x + dx) % 4, (y + dy) % 4, (z + dz) % 8, c ^ flip))
        for x in range(4)
        for y in range(4)
        for z in range(8)
        for c in range(2)
    ]
    return lax.ppermute(value, ALL, pairs)


def swap_core(value):
    return shift(value, flip=1)


LOG2E = math.log2(math.e)


def in_vmem(*values):
    return [pltpu.with_memory_space_constraint(value, pltpu.VMEM) for value in values]


def slot_of(meta, i):
    k = i & 7
    reach = (k + 1) >> 1
    step = reach * (1 - 2 * (k & 1))
    return ((meta[0] + 8 + step) & 7) * 2 + (meta[1] ^ (i >> 3))


def place_of(pa, pb):
    return jnp.concatenate([pa[...], pb[...]], axis=1)


def merge(m0, l0, m1, l1, rate):
    top = jnp.maximum(m0, m1)
    return top, l0 * jnp.exp2((m0 - top) * rate) + l1 * jnp.exp2((m1 - top) * rate)


def swapped(value):
    return jnp.concatenate([value[:, 128:], value[:, :128]], axis=1)


HEADS = 16
CHUNK = 8 * HALF


def score_kernel(chunk, spans, meta, *refs):
    n = len(spans)
    blocks, refs = refs[:n], refs[n:]
    if chunk:
        _, ik_before, refs = refs[0], refs[1], refs[2:]
    qa, qb, na, nb, ma, mb, pa, pb = refs[:8]
    e_ref, m_ref, l_ref, ik_ref, keys, bias, raw, tops, sems = refs[8:]
    step = pl.program_id(0)
    cut = 320

    @pl.when(step == 0)
    def _():
        copies = []
        at = 0
        for i, (block, span) in enumerate(zip(blocks, spans)):
            copies.append(pltpu.make_async_copy(block, keys.at[at : at + span, :], sems.at[i]))
            copies[-1].start()
            at += span
        place = place_of(pa, pb)
        offsets = lax.broadcasted_iota(jnp.int32, (HALF, 256), 0).astype(jnp.float32)
        slots = [slot_of(meta, 8 * chunk + i) for i in range(8)]
        for i in range(8):
            base = ((slots[i] * 2 + meta[2]) * 160 + meta[3] * HALF).astype(jnp.float32)
            bias[i * HALF : (i + 1) * HALF, :] = jnp.where(offsets + base <= place, 0.0, NEG)
        tops[...] = jnp.zeros_like(tops)
        ik_ref[...] = ik_before[...] if chunk else jnp.zeros_like(ik_ref)
        for copy in copies:
            copy.wait()
        quarter = meta[4]
        for i in range(8):
            slot = slots[i]
            mine = pl.ds(pl.multiple_of(i * HALF + quarter * UNIT, UNIT), UNIT)
            ik_ref[pl.ds(pl.multiple_of(slot * UNIT, UNIT), UNIT), :] = keys[mine, 0:DI]

            @pl.when((slot & 3) == quarter)
            def _():
                extra = pl.multiple_of(256 + (slot >> 2) * UNIT, UNIT)
                ik_ref[pl.ds(extra, UNIT), :] = keys[i * HALF + 4 * UNIT : (i + 1) * HALF, 0:DI]

    def work(now, last):
        for k in range(2):
            own = jnp.concatenate([qa[k], qb[k]], axis=1)
            left = jnp.concatenate([na[k], nb[k]], axis=1)
            right = jnp.concatenate([ma[k], mb[k]], axis=1)
            queries = jnp.where(step < 4, own, jnp.where(step < 6, left, right))
            top = jnp.max(tops[last, k], axis=0, keepdims=True)
            safe = jnp.where(top == NEG, 0.0, top)
            head = 2 * jnp.maximum(step - 1, 0) + k
            new = jnp.full((8, 256), NEG, jnp.float32)
            total = jnp.zeros((8, 256), jnp.float32)
            for t in range(0, CHUNK, cut):
                piece, rows = slice(t, t + cut), slice(chunk * CHUNK + t, chunk * CHUNK + t + cut)
                scores = jnp.dot(keys[piece, DI:], queries, preferred_element_type=jnp.float32)
                scores = scores + bias[piece, :]
                raw[now, k, piece, :] = scores
                new = jnp.maximum(new, jnp.max(scores.reshape(cut // 8, 8, 256), axis=0))
                exps = jnp.exp2((raw[last, k, piece, :] - safe) * SCORE2)
                e_ref[head, rows, :] = exps.astype(jnp.bfloat16)
                total = total + jnp.sum(exps.reshape(cut // 8, 8, 256), axis=0)
            tops[now, k] = new
            m_ref[pl.ds(head, 1), :] = top
            l_ref[pl.ds(head, 1), :] = jnp.sum(total, axis=0, keepdims=True)

    @pl.when(step % 2 == 0)
    def _():
        work(0, 1)

    @pl.when(step % 2 == 1)
    def _():
        work(1, 0)


def score_call(meta, chunk, blocks, before, qa, qb, na, nb, ma, mb, pa, pb):
    spans = [b.shape[0] for b in blocks]
    whole = lambda shape: pl.BlockSpec(shape, lambda h, meta: (0,) * len(shape))

    def heads(start, count):
        return pl.BlockSpec((2, DQ, 128), lambda h, meta: (jnp.clip(h - start, 0, count - 1), 0, 0))

    anywhere = pl.BlockSpec(memory_space=pl.ANY)
    exps = pl.BlockSpec(memory_space=pltpu.VMEM)
    return pl.pallas_call(
        lambda *refs: score_kernel(chunk, spans, *refs),
        grid_spec=pltpu.PrefetchScalarGridSpec(
            num_scalar_prefetch=1,
            grid=(HEADS // 2 + 1,),
            in_specs=[anywhere] * len(blocks)
            + ([exps, whole((ROWS, DI))] if chunk else [])
            + [heads(0, 4)] * 2
            + [heads(4, 2)] * 2
            + [heads(6, 2)] * 2
            + [whole((1, 128))] * 2,
            out_specs=[exps, whole((HEADS, 256)), whole((HEADS, 256)), whole((ROWS, DI))],
            scratch_shapes=[
                pltpu.VMEM((CHUNK, DI + DQ), jnp.bfloat16),
                pltpu.VMEM((CHUNK, 256), jnp.float32),
                pltpu.VMEM((2, 2, CHUNK, 256), jnp.float32),
                pltpu.VMEM((2, 2, 8, 256), jnp.float32),
                pltpu.SemaphoreType.DMA((len(blocks),)),
            ],
        ),
        out_shape=[
            pltpu.VMEM((HEADS, 2 * CHUNK, 256), jnp.bfloat16),
            pltpu.VMEM((HEADS, 256), jnp.float32),
            pltpu.VMEM((HEADS, 256), jnp.float32),
            pltpu.VMEM((ROWS, DI), jnp.bfloat16),
        ],
        input_output_aliases={1 + len(blocks): 0} if chunk else {},
        cost_estimate=pl.CostEstimate(
            flops=4 * HEADS * CHUNK * 256 * DQ,
            bytes_accessed=HEADS * CHUNK * 512,
            transcendentals=HEADS * CHUNK * 256,
        ),
        compiler_params=pltpu.CompilerParams(vmem_limit_bytes=VMEM),
        name="scores",
    )(meta, *in_vmem(*blocks), *before, *in_vmem(qa, qb, na, nb, ma, mb, pa, pb))


def head_sum_kernel(meta, e_ref, m0, m1, here, up, down, o0, o1, o2, o3, total_ref, ratio):
    i = pl.program_id(0)

    @pl.when(i == 0)
    def _():
        def side(v):
            heads = [down[v, 4:8, :], up[v, 4:8, :], up[v, 0:4, :], down[v, 0:4, :]]
            return jnp.concatenate(heads, axis=0)

        top, total = merge(here[0, 0:16, :], here[1, 0:16, :], side(0), side(1), SCORE2)
        for c, m in enumerate((m0, m1)):
            ratio[c] = jnp.exp2((m[...] - top) * SCORE2) / total
        index = slice(HEADS, HEADS + 1)
        terms = []
        for left in merge(here[0, index, :], here[1, index, :], down[0, 8:9, :], down[1, 8:9, :], LOG2E):
            for _ in range(3):
                term = left.astype(jnp.bfloat16).astype(jnp.float32)
                terms.append(term)
                left = left - term
        packed = jnp.concatenate(terms + [jnp.zeros((10, 256), jnp.float32)], axis=0)
        for out in (o0, o1, o2, o3):
            out[ROWS:, :] = packed.astype(jnp.bfloat16)

    chunk = i // 8
    total = jnp.zeros((HALF, 256), jnp.float32)
    for h in range(HEADS):
        part = e_ref[h, pl.ds(pl.multiple_of(i * HALF, HALF), HALF), :]
        total = total + part.astype(jnp.float32) * ratio[chunk, h : h + 1, :]
    total_ref[...] = total
    slot = slot_of(meta, i)
    quarter = meta[4]
    at = pl.ds(pl.multiple_of(slot * UNIT, UNIT), UNIT)
    extra = pl.ds(pl.multiple_of(256 + (slot >> 2) * UNIT, UNIT), UNIT)
    for k, out in enumerate((o0, o1, o2, o3)):
        unit = pl.multiple_of((quarter ^ k) * UNIT, UNIT)
        out[at, :] = total_ref[pl.ds(unit, UNIT), :].astype(jnp.bfloat16)

        @pl.when((slot & 3) == (quarter ^ k))
        def _():
            out[extra, :] = total_ref[4 * UNIT :, :].astype(jnp.bfloat16)


def head_sum_call(meta, exps, *stats):
    piece = pl.BlockSpec(memory_space=pltpu.VMEM)
    whole = lambda shape: pl.BlockSpec(shape, lambda i, meta: (0,) * len(shape))
    out = pl.BlockSpec((ROWS + UNIT, 256), lambda i, meta: (0, 0))
    return pl.pallas_call(
        head_sum_kernel,
        grid_spec=pltpu.PrefetchScalarGridSpec(
            num_scalar_prefetch=1,
            grid=(BLOCKS,),
            in_specs=[piece] + [whole(part.shape) for part in stats],
            out_specs=[out] * 4,
            scratch_shapes=[
                pltpu.VMEM((HALF, 256), jnp.float32),
                pltpu.VMEM((2, HEADS, 256), jnp.float32),
            ],
        ),
        out_shape=[pltpu.VMEM((ROWS + UNIT, 256), jnp.bfloat16)] * 4,
        cost_estimate=pl.CostEstimate(flops=0, bytes_accessed=11 << 20, transcendentals=0),
        compiler_params=pltpu.CompilerParams(vmem_limit_bytes=VMEM),
        name="head_sum",
    )(meta, *in_vmem(exps, *stats))


def key_places(meta):
    core, half, quarter = meta[2], meta[3], meta[4]
    rows = lax.broadcasted_iota(jnp.int32, (UNIT, 256), 0)
    out = []
    for u in range(16):
        out.append(rows + ((u // 2 * 4 + (u % 2) * 2 + core) * 160 + half * HALF + quarter * UNIT))
    for e in range(4):
        z, ylo = 2 * e + (quarter >> 1), quarter & 1
        out.append(rows + ((z * 4 + ylo * 2 + core) * 160 + half * HALF + 4 * UNIT))
    return out


def inner_of(keys, ia, ib, j):
    queries = jnp.concatenate([ia[j], ib[j]], axis=0)
    return lax.dot_general(
        keys[...], queries, (((1,), (1,)), ((), ())), preferred_element_type=jnp.float32
    ), queries


JSTEP = 32


def forward_kernel(meta, keys, m0, l0, m1, l1, ia, ib, pa, pb, wja, wjb, logits, here, sent):
    step = pl.program_id(0)

    @pl.when(step == 0)
    def _():
        logits[...] = jnp.zeros_like(logits)

    total = logits[...]
    for j in range(JSTEP):
        inner, _ = inner_of(keys, ia, ib, j)
        weight = jnp.concatenate([wja[j : j + 1, :], wjb[j : j + 1, :]], axis=1)
        total = total + weight * jnp.maximum(inner, 0.0)
    logits[...] = total

    @pl.when(step == NI // JSTEP - 1)
    def _():
        place = place_of(pa, pb)
        places = key_places(meta)
        top = jnp.full((1, 256), NEG, jnp.float32)
        for u in range(20):
            cut = slice(u * UNIT, (u + 1) * UNIT)
            value = logits[cut, :] * INDEX_SCALE
            value = jnp.where(places[u].astype(jnp.float32) <= place, value, NEG)
            logits[cut, :] = value
            top = jnp.maximum(top, jnp.max(value, axis=0, keepdims=True))
        safe = jnp.where(top == NEG, 0.0, top)
        total = jnp.sum(jnp.exp(logits[...] - safe), axis=0, keepdims=True)
        tops, totals = merge(m0[...], l0[...], m1[...], l1[...], SCORE2)
        for v, (heads, index) in enumerate(((tops, top), (totals, total))):
            rows = jnp.concatenate([heads, index, jnp.zeros((7, 256), jnp.float32)], axis=0)
            here[v] = rows
            sent[v] = swapped(rows)


def pair_kernel(ours, theirs, here, up, down):
    index = slice(HEADS, HEADS + 1)
    heads = slice(0, HEADS)
    tops, totals = merge(ours[0, heads, :], ours[1, heads, :], theirs[0, heads, :], theirs[1, heads, :], SCORE2)
    top, total = merge(ours[0, index, :], ours[1, index, :], theirs[0, index, :], theirs[1, index, :], LOG2E)
    for v, (main, extra) in enumerate(((tops, top), (totals, total))):
        pad = jnp.zeros((7, 256), jnp.float32)
        here[v] = jnp.concatenate([main, extra, pad], axis=0)
        up[v] = jnp.concatenate([main[0:4], main[12:16]], axis=0)
        down[v] = jnp.concatenate([main[4:12], extra, pad], axis=0)


def pair_call(ours, theirs):
    return pl.pallas_call(
        pair_kernel,
        out_shape=[pltpu.VMEM((2, rows, 256), jnp.float32) for rows in (24, 8, 16)],
        name="pair_statistics",
    )(*in_vmem(ours, theirs))


def j_specs():
    whole = lambda shape: pl.BlockSpec(shape, lambda s, meta: (0,) * len(shape))
    queries = pl.BlockSpec((JSTEP, 128, DI), lambda s, meta: (s, 0, 0))
    weights = pl.BlockSpec((JSTEP, 128), lambda s, meta: (s, 0))
    return whole, [queries, queries], [weights, weights]


def forward_call(meta, keys, stats, ia, ib, pa, pb, wa, wb):
    whole, queries, weights = j_specs()
    return pl.pallas_call(
        forward_kernel,
        grid_spec=pltpu.PrefetchScalarGridSpec(
            num_scalar_prefetch=1,
            grid=(NI // JSTEP,),
            in_specs=[whole((ROWS, DI))] + [whole((HEADS, 256))] * 4 + queries + [whole((1, 128))] * 2 + weights,
            out_specs=[whole((ROWS, 256)), whole((2, 24, 256)), whole((2, 24, 256))],
        ),
        out_shape=[
            pltpu.VMEM((ROWS, 256), jnp.float32),
            pltpu.VMEM((2, 24, 256), jnp.float32),
            pltpu.VMEM((2, 24, 256), jnp.float32),
        ],
        cost_estimate=pl.CostEstimate(
            flops=2 * NI * ROWS * 256 * DI, bytes_accessed=5 << 20, transcendentals=0
        ),
        compiler_params=pltpu.CompilerParams(vmem_limit_bytes=VMEM),
        name="index_forward",
    )(meta, *in_vmem(keys, *stats, ia, ib, pa, pb, wa, wb))


def backward_kernel(meta, keys, logits, t0, t1, t2, t3, ia, ib, wja, wjb, rows_a, rows_b, kg, grad, acc):
    step = pl.program_id(0)

    @pl.when(step == 0)
    def _():
        parts = (t0, t1, t2, t3)

        def value(part, row):
            terms = part[ROWS:, :].astype(jnp.float32)
            return terms[row : row + 1] + terms[row + 1 : row + 2] + terms[row + 2 : row + 3]

        tops = [value(part, 0) for part in parts]
        top = tops[0]
        for other in tops[1:]:
            top = jnp.maximum(top, other)
        total = jnp.zeros((1, 256), jnp.float32)
        for part, other in zip(parts, tops):
            total = total + value(part, 3) * jnp.exp(other - top)
        norm = top + jnp.log(total)
        goal = jnp.zeros((ROWS, 256), jnp.float32)
        for part in parts:
            goal = goal + part[0:ROWS, :].astype(jnp.float32)
        goal = goal * (1.0 / 64.0)
        held = logits[...]
        seen = held != NEG
        logp = held - norm
        live = seen & (goal > 0)
        safe = jnp.where(goal > 0, goal, 1.0)
        part = jnp.where(live, goal * (jnp.log(safe) - logp), 0.0)
        part = jnp.sum(part, axis=0, keepdims=True)
        part = jnp.concatenate([part, jnp.zeros((15, 256), jnp.float32)], axis=0)
        rows_a[NI:, :] = part[:, :128]
        rows_b[NI:, :] = part[:, 128:]
        grad[...] = jnp.where(seen, jnp.exp(logp) - goal, 0.0) * INDEX_SCALE
        acc[...] = jnp.zeros_like(acc)

    total = acc[...]
    slope = grad[...]
    for j in range(JSTEP):
        inner, queries = inner_of(keys, ia, ib, j)
        weight = jnp.concatenate([wja[j : j + 1, :], wjb[j : j + 1, :]], axis=1)
        share = jnp.sum(slope * jnp.maximum(inner, 0.0), axis=0, keepdims=True)
        rows_a[pl.ds(step * JSTEP + j, 1), :] = share[:, :128]
        rows_b[pl.ds(step * JSTEP + j, 1), :] = share[:, 128:]
        coeff = jnp.where(inner > 0, slope * weight, 0.0).astype(jnp.bfloat16)
        total = total + jnp.dot(coeff, queries, preferred_element_type=jnp.float32)
    acc[...] = total

    @pl.when(step == NI // JSTEP - 1)
    def _():
        quarter = meta[4]
        for b in range(BLOCKS):
            kg[b, 0:UNIT, :] = acc[b * UNIT : (b + 1) * UNIT, :].astype(jnp.bfloat16)
            at = 256 + (b // 4) * UNIT
            extra = jnp.where(quarter == b % 4, acc[at : at + UNIT, :], 0.0)
            kg[b, UNIT:, :] = extra.astype(jnp.bfloat16)


def backward_call(meta, keys, logits, target, ia, ib, wa, wb):
    whole, queries, weights = j_specs()
    return pl.pallas_call(
        backward_kernel,
        grid_spec=pltpu.PrefetchScalarGridSpec(
            num_scalar_prefetch=1,
            grid=(NI // JSTEP,),
            in_specs=[
                whole((ROWS, DI)),
                whole((ROWS, 256)),
            ]
            + [whole((ROWS + UNIT, 256))] * 4
            + queries
            + weights,
            out_specs=[
                whole((NI + 16, 128)),
                whole((NI + 16, 128)),
                whole((BLOCKS, 2 * UNIT, DI)),
            ],
            scratch_shapes=[
                pltpu.VMEM((ROWS, 256), jnp.float32),
                pltpu.VMEM((ROWS, DI), jnp.float32),
            ],
        ),
        out_shape=[
            pltpu.VMEM((NI + 16, 128), jnp.float32),
            pltpu.VMEM((NI + 16, 128), jnp.float32),
            pltpu.VMEM((BLOCKS, 2 * UNIT, DI), jnp.bfloat16),
        ],
        cost_estimate=pl.CostEstimate(
            flops=4 * NI * ROWS * 256 * DI, bytes_accessed=6 << 20, transcendentals=0
        ),
        compiler_params=pltpu.CompilerParams(vmem_limit_bytes=VMEM),
        name="index_backward",
    )(meta, *in_vmem(keys, logits, *target, ia, ib, wa, wb))


def gather_head(value):
    wide = jnp.broadcast_to(value[None], (8,) + value.shape)
    return lax.all_to_all(wide, ("yhi", "xh", "xp"), 0, 0, tiled=True)


def after(value, *others):
    return lax.optimization_barrier((value,) + others)[0]


def body(main_queries, latent_keys, index_queries, index_weights, index_keys, tile_order, offset):
    z, ylo, core = lax.axis_index("z"), lax.axis_index("ylo"), lax.axis_index("core")
    half = lax.axis_index("xp")
    quarter = lax.axis_index("yhi") * 2 + lax.axis_index("xh")

    rows = jnp.arange(TILE, dtype=jnp.int32)
    place = (offset + (tile_order[:, None] * TILE + rows[None, :])).reshape(1, 128)
    pa, wa = place.astype(jnp.float32), index_weights.T
    own = jnp.concatenate([index_keys, latent_keys], axis=1)
    own = lax.dynamic_slice_in_dim(own, half * HALF, HALF, 0)

    queries = main_queries.transpose(0, 2, 1)
    f1, b1 = shift(own, dz=1), shift(own, dz=7)
    queries_far = swap_core(queries)
    left, right = shift(queries[:4], dx=1), shift(queries[4:], dx=3)
    f1, b1 = lax.optimization_barrier((f1, b1))
    f2, b2 = shift(f1, dz=1), shift(b1, dz=7)
    f2, b2 = lax.optimization_barrier((f2, b2))
    f3, b3 = shift(f2, dz=1), shift(b2, dz=7)
    f3, b3 = lax.optimization_barrier((f3, b3))
    f4 = shift(f3, dz=1)
    ia = index_queries.transpose(1, 0, 2)
    pb = swap_core(pa)
    f4, ia, pb, left, right = lax.optimization_barrier((f4, ia, pb, left, right))
    y0, y1 = jnp.concatenate([own, f1, b1, f2]), jnp.concatenate([b2, f3, b3, f4])
    y0, y1, left, right = lax.optimization_barrier((y0, y1, left, right))
    y0, y1 = shift(y0, dy=1), shift(y1, dy=3)
    left_far, right_far = swap_core(left), swap_core(right)
    meta = jnp.stack([z, ylo, core, half, quarter]).astype(jnp.int32)

    sides = (queries, queries_far, left, left_far, right, right_far, pa, pb)
    exps, m0, l0, keys = score_call(meta, 0, [own, f1, b1, f2, b2, f3, b3, f4], [], *sides)
    ia, wa = lax.optimization_barrier((ia, wa, m0))[:2]
    ib, wb = swap_core(ia), swap_core(wa)
    exps, m1, l1, keys = score_call(meta, 1, [y0, y1], in_vmem(exps, keys), *sides)

    logits, ours, sent = forward_call(meta, keys, (m0, l0, m1, l1), ia, ib, pa, pb, wa, wb)
    here, up, down = pair_call(ours, swap_core(sent))
    up, down = shift(up, dx=1), shift(down, dx=3)
    sums = head_sum_call(meta, exps, m0, m1, here, up, down)
    group = (dict(dx=2), dict(dy=2), dict(dx=2, dy=2))
    target = [sums[0]] + [shift(part, **move) for part, move in zip(sums[1:], group)]

    mine, other, kg = backward_call(meta, keys, logits, target, ia, ib, wa, wb)
    rows_out = mine + swap_core(other)
    rows_high = lax.reduce_precision(rows_out, 8, 7)
    low = jnp.concatenate([jnp.zeros((NI + 8, 128), jnp.float32), (rows_out - rows_high)[NI : NI + 8]])
    tail = rows_high + low
    kg = lax.all_to_all(kg, ("z", "ylo"), 0, 0, tiled=True)
    kg = jnp.sum(kg.astype(jnp.float32), axis=0)
    last = gather_head(jnp.concatenate([kg, tail]).astype(jnp.bfloat16)).astype(jnp.float32)
    rows_sum = jnp.sum(last[:, 2 * UNIT :], axis=0)
    pieces = last[:, : 2 * UNIT].reshape(4, 2, 2 * UNIT, DI)
    main = pieces[:, :, :UNIT].transpose(1, 0, 2, 3).reshape(2, 4 * UNIT, DI)
    extra = jnp.sum(pieces[:, :, UNIT:], axis=0)
    key_grad = jnp.concatenate([main, extra], axis=1).reshape(160, DI)
    return rows_sum[NI] + rows_sum[NI + 8], rows_sum[:NI].T, key_grad


def solution(mesh):
    fine = Mesh(np.asarray(mesh.devices).reshape(2, 2, 2, 8, 2, 2), ALL)
    head, ctx = ("yhi", "xh", "xp"), ("z", "ylo", "core")
    in_specs = (
        P(head, ctx, None),
        P(ctx, None),
        P(ctx, None, None),
        P(ctx, None),
        P(ctx, None),
        P(ctx),
        P(),
    )
    out_specs = (P(ctx), P(ctx, None), P(ctx, None))
    return jax.shard_map(body, mesh=fine, in_specs=in_specs, out_specs=out_specs, check_vma=False)
```

```python
import math

import jax
import jax.numpy as jnp
import numpy as np
from jax import lax
from jax.experimental import pallas as pl
from jax.experimental.pallas import tpu as pltpu
from jax.sharding import Mesh
from jax.sharding import PartitionSpec as P

TILE = 32
DQ = 576
DI = 128
NI = 64
HALF = 80
UNIT = 16
BLOCKS = 16
ROWS = 320
SCORE2 = 192.0 ** (-0.5) * math.log2(math.e)
INDEX_SCALE = DI ** (-0.5)
ALL = ("yhi", "xh", "xp", "z", "ylo", "core")
NEG = -jnp.inf
VMEM = 18 << 20


def flat(x, y, z, c):
    return ((y // 2) * 4 + x) * 32 + (z * 2 + (y % 2)) * 2 + c


def shift(value, dx=0, dy=0, dz=0, flip=0):
    pairs = [
        (flat(x, y, z, c), flat((x + dx) % 4, (y + dy) % 4, (z + dz) % 8, c ^ flip))
        for x in range(4)
        for y in range(4)
        for z in range(8)
        for c in range(2)
    ]
    return lax.ppermute(value, ALL, pairs)


def swap_core(value):
    return shift(value, flip=1)


LOG2E = math.log2(math.e)


def in_vmem(*values):
    return [pltpu.with_memory_space_constraint(value, pltpu.VMEM) for value in values]


def slot_of(meta, i):
    k = i & 7
    reach = (k + 1) >> 1
    step = reach * (1 - 2 * (k & 1))
    return ((meta[0] + 8 + step) & 7) * 2 + (meta[1] ^ (i >> 3))


def place_of(pa, pb):
    return jnp.concatenate([pa[...], pb[...]], axis=1)


def merge(m0, l0, m1, l1, rate):
    top = jnp.maximum(m0, m1)
    return top, l0 * jnp.exp2((m0 - top) * rate) + l1 * jnp.exp2((m1 - top) * rate)


def swapped(value):
    return jnp.concatenate([value[:, 128:], value[:, :128]], axis=1)


HEADS = 16
CHUNK = 8 * HALF


def score_kernel(chunk, spans, meta, *refs):
    n = len(spans)
    blocks, refs = refs[:n], refs[n:]
    if chunk:
        _, ik_before, refs = refs[0], refs[1], refs[2:]
    qa, qb, na, nb, ma, mb, pa, pb = refs[:8]
    e_ref, m_ref, l_ref, ik_ref, keys, bias, raw, tops, sems = refs[8:]
    step = pl.program_id(0)
    cut = 320

    @pl.when(step == 0)
    def _():
        copies = []
        at = 0
        for i, (block, span) in enumerate(zip(blocks, spans)):
            copies.append(pltpu.make_async_copy(block, keys.at[at : at + span, :], sems.at[i]))
            copies[-1].start()
            at += span
        place = place_of(pa, pb)
        offsets = lax.broadcasted_iota(jnp.int32, (HALF, 256), 0).astype(jnp.float32)
        slots = [slot_of(meta, 8 * chunk + i) for i in range(8)]
        for i in range(8):
            base = ((slots[i] * 2 + meta[2]) * 160 + meta[3] * HALF).astype(jnp.float32)
            bias[i * HALF : (i + 1) * HALF, :] = jnp.where(offsets + base <= place, 0.0, NEG)
        tops[...] = jnp.zeros_like(tops)
        ik_ref[...] = ik_before[...] if chunk else jnp.zeros_like(ik_ref)
        for copy in copies:
            copy.wait()
        quarter = meta[4]
        for i in range(8):
            slot = slots[i]
            mine = pl.ds(pl.multiple_of(i * HALF + quarter * UNIT, UNIT), UNIT)
            ik_ref[pl.ds(pl.multiple_of(slot * UNIT, UNIT), UNIT), :] = keys[mine, 0:DI]

            @pl.when((slot & 3) == quarter)
            def _():
                extra = pl.multiple_of(256 + (slot >> 2) * UNIT, UNIT)
                ik_ref[pl.ds(extra, UNIT), :] = keys[i * HALF + 4 * UNIT : (i + 1) * HALF, 0:DI]

    def work(now, last):
        for k in range(2):
            own = jnp.concatenate([qa[k], qb[k]], axis=1)
            left = jnp.concatenate([na[k], nb[k]], axis=1)
            right = jnp.concatenate([ma[k], mb[k]], axis=1)
            queries = jnp.where(step < 4, own, jnp.where(step < 6, left, right))
            top = jnp.max(tops[last, k], axis=0, keepdims=True)
            safe = jnp.where(top == NEG, 0.0, top)
            head = 2 * jnp.maximum(step - 1, 0) + k
            new = jnp.full((8, 256), NEG, jnp.float32)
            total = jnp.zeros((8, 256), jnp.float32)
            for t in range(0, CHUNK, cut):
                piece, rows = slice(t, t + cut), slice(chunk * CHUNK + t, chunk * CHUNK + t + cut)
                scores = jnp.dot(keys[piece, DI:], queries, preferred_element_type=jnp.float32)
                scores = scores + bias[piece, :]
                raw[now, k, piece, :] = scores
                new = jnp.maximum(new, jnp.max(scores.reshape(cut // 8, 8, 256), axis=0))
                exps = jnp.exp2((raw[last, k, piece, :] - safe) * SCORE2)
                e_ref[head, rows, :] = exps.astype(jnp.bfloat16)
                total = total + jnp.sum(exps.reshape(cut // 8, 8, 256), axis=0)
            tops[now, k] = new
            m_ref[pl.ds(head, 1), :] = top
            l_ref[pl.ds(head, 1), :] = jnp.sum(total, axis=0, keepdims=True)

    @pl.when(step % 2 == 0)
    def _():
        work(0, 1)

    @pl.when(step % 2 == 1)
    def _():
        work(1, 0)


def score_call(meta, chunk, blocks, before, qa, qb, na, nb, ma, mb, pa, pb):
    spans = [b.shape[0] for b in blocks]
    whole = lambda shape: pl.BlockSpec(shape, lambda h, meta: (0,) * len(shape))

    def heads(start, count):
        return pl.BlockSpec((2, DQ, 128), lambda h, meta: (jnp.clip(h - start, 0, count - 1), 0, 0))

    anywhere = pl.BlockSpec(memory_space=pl.ANY)
    exps = pl.BlockSpec(memory_space=pltpu.VMEM)
    return pl.pallas_call(
        lambda *refs: score_kernel(chunk, spans, *refs),
        grid_spec=pltpu.PrefetchScalarGridSpec(
            num_scalar_prefetch=1,
            grid=(HEADS // 2 + 1,),
            in_specs=[anywhere] * len(blocks)
            + ([exps, whole((ROWS, DI))] if chunk else [])
            + [heads(0, 4)] * 2
            + [heads(4, 2)] * 2
            + [heads(6, 2)] * 2
            + [whole((1, 128))] * 2,
            out_specs=[exps, whole((HEADS, 256)), whole((HEADS, 256)), whole((ROWS, DI))],
            scratch_shapes=[
                pltpu.VMEM((CHUNK, DI + DQ), jnp.bfloat16),
                pltpu.VMEM((CHUNK, 256), jnp.float32),
                pltpu.VMEM((2, 2, CHUNK, 256), jnp.float32),
                pltpu.VMEM((2, 2, 8, 256), jnp.float32),
                pltpu.SemaphoreType.DMA((len(blocks),)),
            ],
        ),
        out_shape=[
            pltpu.VMEM((HEADS, 2 * CHUNK, 256), jnp.bfloat16),
            pltpu.VMEM((HEADS, 256), jnp.float32),
            pltpu.VMEM((HEADS, 256), jnp.float32),
            pltpu.VMEM((ROWS, DI), jnp.bfloat16),
        ],
        input_output_aliases={1 + len(blocks): 0} if chunk else {},
        cost_estimate=pl.CostEstimate(
            flops=4 * HEADS * CHUNK * 256 * DQ,
            bytes_accessed=HEADS * CHUNK * 512,
            transcendentals=HEADS * CHUNK * 256,
        ),
        compiler_params=pltpu.CompilerParams(vmem_limit_bytes=VMEM),
        name="scores",
    )(meta, *in_vmem(*blocks), *before, *in_vmem(qa, qb, na, nb, ma, mb, pa, pb))


def head_sum_kernel(meta, e_ref, m0, m1, here, up, down, o0, o1, o2, o3, total_ref, ratio):
    i = pl.program_id(0)

    @pl.when(i == 0)
    def _():
        def side(v):
            heads = [down[v, 4:8, :], up[v, 4:8, :], up[v, 0:4, :], down[v, 0:4, :]]
            return jnp.concatenate(heads, axis=0)

        top, total = merge(here[0, 0:16, :], here[1, 0:16, :], side(0), side(1), SCORE2)
        for c, m in enumerate((m0, m1)):
            ratio[c] = jnp.exp2((m[...] - top) * SCORE2) / total
        index = slice(HEADS, HEADS + 1)
        terms = []
        for left in merge(here[0, index, :], here[1, index, :], down[0, 8:9, :], down[1, 8:9, :], LOG2E):
            for _ in range(3):
                term = left.astype(jnp.bfloat16).astype(jnp.float32)
                terms.append(term)
                left = left - term
        packed = jnp.concatenate(terms + [jnp.zeros((10, 256), jnp.float32)], axis=0)
        for out in (o0, o1, o2, o3):
            out[ROWS:, :] = packed.astype(jnp.bfloat16)

    chunk = i // 8
    total = jnp.zeros((HALF, 256), jnp.float32)
    for h in range(HEADS):
        part = e_ref[h, pl.ds(pl.multiple_of(i * HALF, HALF), HALF), :]
        total = total + part.astype(jnp.float32) * ratio[chunk, h : h + 1, :]
    total_ref[...] = total
    slot = slot_of(meta, i)
    quarter = meta[4]
    at = pl.ds(pl.multiple_of(slot * UNIT, UNIT), UNIT)
    extra = pl.ds(pl.multiple_of(256 + (slot >> 2) * UNIT, UNIT), UNIT)
    for k, out in enumerate((o0, o1, o2, o3)):
        unit = pl.multiple_of((quarter ^ k) * UNIT, UNIT)
        out[at, :] = total_ref[pl.ds(unit, UNIT), :].astype(jnp.bfloat16)

        @pl.when((slot & 3) == (quarter ^ k))
        def _():
            out[extra, :] = total_ref[4 * UNIT :, :].astype(jnp.bfloat16)


def head_sum_call(meta, exps, *stats):
    piece = pl.BlockSpec(memory_space=pltpu.VMEM)
    whole = lambda shape: pl.BlockSpec(shape, lambda i, meta: (0,) * len(shape))
    out = pl.BlockSpec((ROWS + UNIT, 256), lambda i, meta: (0, 0))
    return pl.pallas_call(
        head_sum_kernel,
        grid_spec=pltpu.PrefetchScalarGridSpec(
            num_scalar_prefetch=1,
            grid=(BLOCKS,),
            in_specs=[piece] + [whole(part.shape) for part in stats],
            out_specs=[out] * 4,
            scratch_shapes=[
                pltpu.VMEM((HALF, 256), jnp.float32),
                pltpu.VMEM((2, HEADS, 256), jnp.float32),
            ],
        ),
        out_shape=[pltpu.VMEM((ROWS + UNIT, 256), jnp.bfloat16)] * 4,
        cost_estimate=pl.CostEstimate(flops=0, bytes_accessed=11 << 20, transcendentals=0),
        compiler_params=pltpu.CompilerParams(vmem_limit_bytes=VMEM),
        name="head_sum",
    )(meta, *in_vmem(exps, *stats))


def key_places(meta):
    core, half, quarter = meta[2], meta[3], meta[4]
    rows = lax.broadcasted_iota(jnp.int32, (UNIT, 256), 0)
    out = []
    for u in range(16):
        out.append(rows + ((u // 2 * 4 + (u % 2) * 2 + core) * 160 + half * HALF + quarter * UNIT))
    for e in range(4):
        z, ylo = 2 * e + (quarter >> 1), quarter & 1
        out.append(rows + ((z * 4 + ylo * 2 + core) * 160 + half * HALF + 4 * UNIT))
    return out


def inner_of(keys, ia, ib, j):
    queries = jnp.concatenate([ia[j], ib[j]], axis=0)
    return lax.dot_general(
        keys[...], queries, (((1,), (1,)), ((), ())), preferred_element_type=jnp.float32
    ), queries


JSTEP = 32


def forward_kernel(meta, keys, m0, l0, m1, l1, ia, ib, pa, pb, wja, wjb, logits, here, sent):
    step = pl.program_id(0)

    @pl.when(step == 0)
    def _():
        logits[...] = jnp.zeros_like(logits)

    total = logits[...]
    for j in range(JSTEP):
        inner, _ = inner_of(keys, ia, ib, j)
        weight = jnp.concatenate([wja[j : j + 1, :], wjb[j : j + 1, :]], axis=1)
        total = total + weight * jnp.maximum(inner, 0.0)
    logits[...] = total

    @pl.when(step == NI // JSTEP - 1)
    def _():
        place = place_of(pa, pb)
        places = key_places(meta)
        top = jnp.full((1, 256), NEG, jnp.float32)
        for u in range(20):
            cut = slice(u * UNIT, (u + 1) * UNIT)
            value = logits[cut, :] * INDEX_SCALE
            value = jnp.where(places[u].astype(jnp.float32) <= place, value, NEG)
            logits[cut, :] = value
            top = jnp.maximum(top, jnp.max(value, axis=0, keepdims=True))
        safe = jnp.where(top == NEG, 0.0, top)
        total = jnp.sum(jnp.exp(logits[...] - safe), axis=0, keepdims=True)
        tops, totals = merge(m0[...], l0[...], m1[...], l1[...], SCORE2)
        for v, (heads, index) in enumerate(((tops, top), (totals, total))):
            rows = jnp.concatenate([heads, index, jnp.zeros((7, 256), jnp.float32)], axis=0)
            here[v] = rows
            sent[v] = swapped(rows)


def pair_kernel(ours, theirs, here, up, down):
    index = slice(HEADS, HEADS + 1)
    heads = slice(0, HEADS)
    tops, totals = merge(ours[0, heads, :], ours[1, heads, :], theirs[0, heads, :], theirs[1, heads, :], SCORE2)
    top, total = merge(ours[0, index, :], ours[1, index, :], theirs[0, index, :], theirs[1, index, :], LOG2E)
    for v, (main, extra) in enumerate(((tops, top), (totals, total))):
        pad = jnp.zeros((7, 256), jnp.float32)
        here[v] = jnp.concatenate([main, extra, pad], axis=0)
        up[v] = jnp.concatenate([main[0:4], main[12:16]], axis=0)
        down[v] = jnp.concatenate([main[4:12], extra, pad], axis=0)


def pair_call(ours, theirs):
    return pl.pallas_call(
        pair_kernel,
        out_shape=[pltpu.VMEM((2, rows, 256), jnp.float32) for rows in (24, 8, 16)],
        compiler_params=pltpu.CompilerParams(vmem_limit_bytes=1 << 20),
        name="pair_statistics",
    )(*in_vmem(ours, theirs))


def j_specs():
    whole = lambda shape: pl.BlockSpec(shape, lambda s, meta: (0,) * len(shape))
    queries = pl.BlockSpec((JSTEP, 128, DI), lambda s, meta: (s, 0, 0))
    weights = pl.BlockSpec((JSTEP, 128), lambda s, meta: (s, 0))
    return whole, [queries, queries], [weights, weights]


def forward_call(meta, keys, stats, ia, ib, pa, pb, wa, wb):
    whole, queries, weights = j_specs()
    return pl.pallas_call(
        forward_kernel,
        grid_spec=pltpu.PrefetchScalarGridSpec(
            num_scalar_prefetch=1,
            grid=(NI // JSTEP,),
            in_specs=[whole((ROWS, DI))] + [whole((HEADS, 256))] * 4 + queries + [whole((1, 128))] * 2 + weights,
            out_specs=[whole((ROWS, 256)), whole((2, 24, 256)), whole((2, 24, 256))],
        ),
        out_shape=[
            pltpu.VMEM((ROWS, 256), jnp.float32),
            pltpu.VMEM((2, 24, 256), jnp.float32),
            pltpu.VMEM((2, 24, 256), jnp.float32),
        ],
        cost_estimate=pl.CostEstimate(
            flops=2 * NI * ROWS * 256 * DI, bytes_accessed=5 << 20, transcendentals=0
        ),
        compiler_params=pltpu.CompilerParams(vmem_limit_bytes=VMEM),
        name="index_forward",
    )(meta, *in_vmem(keys, *stats, ia, ib, pa, pb, wa, wb))


def backward_kernel(meta, keys, logits, t0, t1, t2, t3, ia, ib, wja, wjb, rows_a, rows_b, kg, grad, acc):
    step = pl.program_id(0)

    @pl.when(step == 0)
    def _():
        parts = (t0, t1, t2, t3)

        def value(part, row):
            terms = part[ROWS:, :].astype(jnp.float32)
            return terms[row : row + 1] + terms[row + 1 : row + 2] + terms[row + 2 : row + 3]

        tops = [value(part, 0) for part in parts]
        top = tops[0]
        for other in tops[1:]:
            top = jnp.maximum(top, other)
        total = jnp.zeros((1, 256), jnp.float32)
        for part, other in zip(parts, tops):
            total = total + value(part, 3) * jnp.exp(other - top)
        norm = top + jnp.log(total)
        goal = jnp.zeros((ROWS, 256), jnp.float32)
        for part in parts:
            goal = goal + part[0:ROWS, :].astype(jnp.float32)
        goal = goal * (1.0 / 64.0)
        held = logits[...]
        seen = held != NEG
        logp = held - norm
        live = seen & (goal > 0)
        safe = jnp.where(goal > 0, goal, 1.0)
        part = jnp.where(live, goal * (jnp.log(safe) - logp), 0.0)
        part = jnp.sum(part, axis=0, keepdims=True)
        part = jnp.concatenate([part, jnp.zeros((15, 256), jnp.float32)], axis=0)
        rows_a[NI:, :] = part[:, :128]
        rows_b[NI:, :] = part[:, 128:]
        grad[...] = jnp.where(seen, jnp.exp(logp) - goal, 0.0) * INDEX_SCALE
        acc[...] = jnp.zeros_like(acc)

    total = acc[...]
    slope = grad[...]
    for j in range(JSTEP):
        inner, queries = inner_of(keys, ia, ib, j)
        weight = jnp.concatenate([wja[j : j + 1, :], wjb[j : j + 1, :]], axis=1)
        share = jnp.sum(slope * jnp.maximum(inner, 0.0), axis=0, keepdims=True)
        rows_a[pl.ds(step * JSTEP + j, 1), :] = share[:, :128]
        rows_b[pl.ds(step * JSTEP + j, 1), :] = share[:, 128:]
        coeff = jnp.where(inner > 0, slope * weight, 0.0).astype(jnp.bfloat16)
        total = total + jnp.dot(coeff, queries, preferred_element_type=jnp.float32)
    acc[...] = total

    @pl.when(step == NI // JSTEP - 1)
    def _():
        quarter = meta[4]
        for b in range(BLOCKS):
            kg[b, 0:UNIT, :] = acc[b * UNIT : (b + 1) * UNIT, :].astype(jnp.bfloat16)
            at = 256 + (b // 4) * UNIT
            extra = jnp.where(quarter == b % 4, acc[at : at + UNIT, :], 0.0)
            kg[b, UNIT:, :] = extra.astype(jnp.bfloat16)


def backward_call(meta, keys, logits, target, ia, ib, wa, wb):
    whole, queries, weights = j_specs()
    return pl.pallas_call(
        backward_kernel,
        grid_spec=pltpu.PrefetchScalarGridSpec(
            num_scalar_prefetch=1,
            grid=(NI // JSTEP,),
            in_specs=[
                whole((ROWS, DI)),
                whole((ROWS, 256)),
            ]
            + [whole((ROWS + UNIT, 256))] * 4
            + queries
            + weights,
            out_specs=[
                whole((NI + 16, 128)),
                whole((NI + 16, 128)),
                whole((BLOCKS, 2 * UNIT, DI)),
            ],
            scratch_shapes=[
                pltpu.VMEM((ROWS, 256), jnp.float32),
                pltpu.VMEM((ROWS, DI), jnp.float32),
            ],
        ),
        out_shape=[
            pltpu.VMEM((NI + 16, 128), jnp.float32),
            pltpu.VMEM((NI + 16, 128), jnp.float32),
            pltpu.VMEM((BLOCKS, 2 * UNIT, DI), jnp.bfloat16),
        ],
        cost_estimate=pl.CostEstimate(
            flops=4 * NI * ROWS * 256 * DI, bytes_accessed=6 << 20, transcendentals=0
        ),
        compiler_params=pltpu.CompilerParams(vmem_limit_bytes=VMEM),
        name="index_backward",
    )(meta, *in_vmem(keys, logits, *target, ia, ib, wa, wb))


def gather_head(value):
    wide = jnp.broadcast_to(value[None], (8,) + value.shape)
    return lax.all_to_all(wide, ("yhi", "xh", "xp"), 0, 0, tiled=True)


def after(value, *others):
    return lax.optimization_barrier((value,) + others)[0]


def body(main_queries, latent_keys, index_queries, index_weights, index_keys, tile_order, offset):
    z, ylo, core = lax.axis_index("z"), lax.axis_index("ylo"), lax.axis_index("core")
    half = lax.axis_index("xp")
    quarter = lax.axis_index("yhi") * 2 + lax.axis_index("xh")

    rows = jnp.arange(TILE, dtype=jnp.int32)
    place = (offset + (tile_order[:, None] * TILE + rows[None, :])).reshape(1, 128)
    pa, wa = place.astype(jnp.float32), index_weights.T
    own = jnp.concatenate([index_keys, latent_keys], axis=1)
    own = lax.dynamic_slice_in_dim(own, half * HALF, HALF, 0)
    meta = jnp.stack([z, ylo, core, half, quarter]).astype(jnp.int32)
    own, meta = lax.optimization_barrier((own, meta))

    queries = main_queries.transpose(0, 2, 1)
    f1, b1 = shift(own, dz=1), shift(own, dz=7)
    queries_far = swap_core(queries)
    halves = after(queries, own)
    left, right = shift(halves[:4], dx=1), shift(halves[4:], dx=3)
    f1, b1 = lax.optimization_barrier((f1, b1))
    f2, b2 = shift(f1, dz=1), shift(b1, dz=7)
    f2, b2 = lax.optimization_barrier((f2, b2))
    f3, b3 = shift(f2, dz=1), shift(b2, dz=7)
    pb = swap_core(pa)
    ia = index_queries.transpose(1, 0, 2)
    f3, b3, left, right, ia, pb = lax.optimization_barrier((f3, b3, left, right, ia, pb))
    f4 = shift(f3, dz=1)
    left_far, right_far = swap_core(left), swap_core(right)
    y0, y1 = jnp.concatenate([own, f1, b1, f2]), jnp.concatenate([b2, f3, b3, f4])
    y0, y1 = shift(y0, dy=1), shift(y1, dy=3)
    ia, wa = lax.optimization_barrier((ia, wa, f4, left_far, right_far))[:2]
    ib, wb = swap_core(ia), swap_core(wa)

    sides = (queries, queries_far, left, left_far, right, right_far, pa, pb)
    exps, m0, l0, keys = score_call(meta, 0, [own, f1, b1, f2, b2, f3, b3, f4], [], *sides)
    exps, m1, l1, keys = score_call(meta, 1, [y0, y1], in_vmem(exps, keys), *sides)

    logits, ours, sent = forward_call(meta, keys, (m0, l0, m1, l1), ia, ib, pa, pb, wa, wb)
    here, up, down = pair_call(ours, swap_core(sent))
    up, down = shift(up, dx=1), shift(down, dx=3)
    sums = head_sum_call(meta, exps, m0, m1, here, up, down)
    group = (dict(dx=2), dict(dy=2), dict(dx=2, dy=2))
    target = [sums[0]] + [shift(part, **move) for part, move in zip(sums[1:], group)]

    mine, other, kg = backward_call(meta, keys, logits, target, ia, ib, wa, wb)
    rows_out = mine + swap_core(other)
    rows_high = lax.reduce_precision(rows_out, 8, 7)
    low = jnp.concatenate([jnp.zeros((NI + 8, 128), jnp.float32), (rows_out - rows_high)[NI : NI + 8]])
    tail = rows_high + low
    kg = lax.all_to_all(kg, ("z", "ylo"), 0, 0, tiled=True)
    kg = jnp.sum(kg.astype(jnp.float32), axis=0)
    last = gather_head(jnp.concatenate([kg, tail]).astype(jnp.bfloat16)).astype(jnp.float32)
    rows_sum = jnp.sum(last[:, 2 * UNIT :], axis=0)
    pieces = last[:, : 2 * UNIT].reshape(4, 2, 2 * UNIT, DI)
    main = pieces[:, :, :UNIT].transpose(1, 0, 2, 3).reshape(2, 4 * UNIT, DI)
    extra = jnp.sum(pieces[:, :, UNIT:], axis=0)
    key_grad = jnp.concatenate([main, extra], axis=1).reshape(160, DI)
    return rows_sum[NI] + rows_sum[NI + 8], rows_sum[:NI].T, key_grad


def solution(mesh):
    fine = Mesh(np.asarray(mesh.devices).reshape(2, 2, 2, 8, 2, 2), ALL)
    head, ctx = ("yhi", "xh", "xp"), ("z", "ylo", "core")
    in_specs = (
        P(head, ctx, None),
        P(ctx, None),
        P(ctx, None, None),
        P(ctx, None),
        P(ctx, None),
        P(ctx),
        P(),
    )
    out_specs = (P(ctx), P(ctx, None), P(ctx, None))
    return jax.shard_map(body, mesh=fine, in_specs=in_specs, out_specs=out_specs, check_vma=False)
```

```python
import math

import jax
import jax.numpy as jnp
import numpy as np
from jax import lax
from jax.experimental import pallas as pl
from jax.experimental.pallas import tpu as pltpu
from jax.sharding import Mesh
from jax.sharding import PartitionSpec as P

TILE = 32
DQ = 576
DI = 128
NI = 64
HALF = 80
UNIT = 16
BLOCKS = 16
ROWS = 320
SCORE2 = 192.0 ** (-0.5) * math.log2(math.e)
INDEX_SCALE = DI ** (-0.5)
ALL = ("yhi", "xh", "xp", "z", "ylo", "core")
NEG = -jnp.inf
VMEM = 18 << 20


def flat(x, y, z, c):
    return ((y // 2) * 4 + x) * 32 + (z * 2 + (y % 2)) * 2 + c


def shift(value, dx=0, dy=0, dz=0, flip=0):
    pairs = [
        (flat(x, y, z, c), flat((x + dx) % 4, (y + dy) % 4, (z + dz) % 8, c ^ flip))
        for x in range(4)
        for y in range(4)
        for z in range(8)
        for c in range(2)
    ]
    return lax.ppermute(value, ALL, pairs)


def swap_core(value):
    return shift(value, flip=1)


LOG2E = math.log2(math.e)


def in_vmem(*values):
    return [pltpu.with_memory_space_constraint(value, pltpu.VMEM) for value in values]


def slot_of(meta, i):
    k = i & 7
    reach = (k + 1) >> 1
    step = reach * (1 - 2 * (k & 1))
    return ((meta[0] + 8 + step) & 7) * 2 + (meta[1] ^ (i >> 3))


def place_of(pa, pb):
    return jnp.concatenate([pa[...], pb[...]], axis=1)


def merge(m0, l0, m1, l1, rate):
    top = jnp.maximum(m0, m1)
    return top, l0 * jnp.exp2((m0 - top) * rate) + l1 * jnp.exp2((m1 - top) * rate)


def swapped(value):
    return jnp.concatenate([value[:, 128:], value[:, :128]], axis=1)


HEADS = 16
CHUNK = 8 * HALF


def score_kernel(chunk, spans, meta, *refs):
    n = len(spans)
    blocks, refs = refs[:n], refs[n:]
    if chunk:
        _, ik_before, refs = refs[0], refs[1], refs[2:]
    qa, qb, na, nb, ma, mb, pa, pb = refs[:8]
    e_ref, m_ref, l_ref, ik_ref, keys, bias, raw, tops, sems = refs[8:]
    step = pl.program_id(0)
    cut = 320

    @pl.when(step == 0)
    def _():
        copies = []
        at = 0
        for i, (block, span) in enumerate(zip(blocks, spans)):
            copies.append(pltpu.make_async_copy(block, keys.at[at : at + span, :], sems.at[i]))
            copies[-1].start()
            at += span
        place = place_of(pa, pb)
        offsets = lax.broadcasted_iota(jnp.int32, (HALF, 256), 0).astype(jnp.float32)
        slots = [slot_of(meta, 8 * chunk + i) for i in range(8)]
        for i in range(8):
            base = ((slots[i] * 2 + meta[2]) * 160 + meta[3] * HALF).astype(jnp.float32)
            bias[i * HALF : (i + 1) * HALF, :] = jnp.where(offsets + base <= place, 0.0, NEG)
        tops[...] = jnp.zeros_like(tops)
        ik_ref[...] = ik_before[...] if chunk else jnp.zeros_like(ik_ref)
        for copy in copies:
            copy.wait()
        quarter = meta[4]
        for i in range(8):
            slot = slots[i]
            mine = pl.ds(pl.multiple_of(i * HALF + quarter * UNIT, UNIT), UNIT)
            ik_ref[pl.ds(pl.multiple_of(slot * UNIT, UNIT), UNIT), :] = keys[mine, 0:DI]

            @pl.when((slot & 3) == quarter)
            def _():
                extra = pl.multiple_of(256 + (slot >> 2) * UNIT, UNIT)
                ik_ref[pl.ds(extra, UNIT), :] = keys[i * HALF + 4 * UNIT : (i + 1) * HALF, 0:DI]

    def work(now, last):
        for k in range(2):
            own = jnp.concatenate([qa[k], qb[k]], axis=1)
            left = jnp.concatenate([na[k], nb[k]], axis=1)
            right = jnp.concatenate([ma[k], mb[k]], axis=1)
            queries = jnp.where(step < 4, own, jnp.where(step < 6, left, right))
            top = jnp.max(tops[last, k], axis=0, keepdims=True)
            safe = jnp.where(top == NEG, 0.0, top)
            head = 2 * jnp.maximum(step - 1, 0) + k
            new = jnp.full((8, 256), NEG, jnp.float32)
            total = jnp.zeros((8, 256), jnp.float32)
            for t in range(0, CHUNK, cut):
                piece, rows = slice(t, t + cut), slice(chunk * CHUNK + t, chunk * CHUNK + t + cut)
                scores = jnp.dot(keys[piece, DI:], queries, preferred_element_type=jnp.float32)
                scores = scores + bias[piece, :]
                raw[now, k, piece, :] = scores
                new = jnp.maximum(new, jnp.max(scores.reshape(cut // 8, 8, 256), axis=0))
                exps = jnp.exp2((raw[last, k, piece, :] - safe) * SCORE2)
                e_ref[head, rows, :] = exps.astype(jnp.bfloat16)
                total = total + jnp.sum(exps.reshape(cut // 8, 8, 256), axis=0)
            tops[now, k] = new
            m_ref[pl.ds(head, 1), :] = top
            l_ref[pl.ds(head, 1), :] = jnp.sum(total, axis=0, keepdims=True)

    @pl.when(step % 2 == 0)
    def _():
        work(0, 1)

    @pl.when(step % 2 == 1)
    def _():
        work(1, 0)


def score_call(meta, chunk, blocks, before, qa, qb, na, nb, ma, mb, pa, pb):
    spans = [b.shape[0] for b in blocks]
    whole = lambda shape: pl.BlockSpec(shape, lambda h, meta: (0,) * len(shape))

    def heads(start, count):
        return pl.BlockSpec((2, DQ, 128), lambda h, meta: (jnp.clip(h - start, 0, count - 1), 0, 0))

    anywhere = pl.BlockSpec(memory_space=pl.ANY)
    exps = pl.BlockSpec(memory_space=pltpu.VMEM)
    return pl.pallas_call(
        lambda *refs: score_kernel(chunk, spans, *refs),
        grid_spec=pltpu.PrefetchScalarGridSpec(
            num_scalar_prefetch=1,
            grid=(HEADS // 2 + 1,),
            in_specs=[anywhere] * len(blocks)
            + ([exps, whole((ROWS, DI))] if chunk else [])
            + [heads(0, 4)] * 2
            + [heads(4, 2)] * 2
            + [heads(6, 2)] * 2
            + [whole((1, 128))] * 2,
            out_specs=[exps, whole((HEADS, 256)), whole((HEADS, 256)), whole((ROWS, DI))],
            scratch_shapes=[
                pltpu.VMEM((CHUNK, DI + DQ), jnp.bfloat16),
                pltpu.VMEM((CHUNK, 256), jnp.float32),
                pltpu.VMEM((2, 2, CHUNK, 256), jnp.float32),
                pltpu.VMEM((2, 2, 8, 256), jnp.float32),
                pltpu.SemaphoreType.DMA((len(blocks),)),
            ],
        ),
        out_shape=[
            pltpu.VMEM((HEADS, 2 * CHUNK, 256), jnp.bfloat16),
            pltpu.VMEM((HEADS, 256), jnp.float32),
            pltpu.VMEM((HEADS, 256), jnp.float32),
            pltpu.VMEM((ROWS, DI), jnp.bfloat16),
        ],
        input_output_aliases={1 + len(blocks): 0} if chunk else {},
        cost_estimate=pl.CostEstimate(
            flops=4 * HEADS * CHUNK * 256 * DQ,
            bytes_accessed=HEADS * CHUNK * 512,
            transcendentals=HEADS * CHUNK * 256,
        ),
        compiler_params=pltpu.CompilerParams(vmem_limit_bytes=VMEM),
        name="scores",
    )(meta, *in_vmem(*blocks), *before, *in_vmem(qa, qb, na, nb, ma, mb, pa, pb))


def head_sum_kernel(meta, e_ref, m0, m1, here, up, down, o0, o1, o2, o3, total_ref, ratio):
    i = pl.program_id(0)

    @pl.when(i == 0)
    def _():
        def side(v):
            heads = [down[v, 4:8, :], up[v, 4:8, :], up[v, 0:4, :], down[v, 0:4, :]]
            return jnp.concatenate(heads, axis=0)

        top, total = merge(here[0, 0:16, :], here[1, 0:16, :], side(0), side(1), SCORE2)
        for c, m in enumerate((m0, m1)):
            ratio[c] = jnp.exp2((m[...] - top) * SCORE2) / total
        index = slice(HEADS, HEADS + 1)
        terms = []
        for left in merge(here[0, index, :], here[1, index, :], down[0, 8:9, :], down[1, 8:9, :], LOG2E):
            for _ in range(3):
                term = left.astype(jnp.bfloat16).astype(jnp.float32)
                terms.append(term)
                left = left - term
        packed = jnp.concatenate(terms + [jnp.zeros((10, 256), jnp.float32)], axis=0)
        for out in (o0, o1, o2, o3):
            out[ROWS:, :] = packed.astype(jnp.bfloat16)

    chunk = i // 8
    total = jnp.zeros((HALF, 256), jnp.float32)
    for h in range(HEADS):
        part = e_ref[h, pl.ds(pl.multiple_of(i * HALF, HALF), HALF), :]
        total = total + part.astype(jnp.float32) * ratio[chunk, h : h + 1, :]
    total_ref[...] = total
    slot = slot_of(meta, i)
    quarter = meta[4]
    at = pl.ds(pl.multiple_of(slot * UNIT, UNIT), UNIT)
    extra = pl.ds(pl.multiple_of(256 + (slot >> 2) * UNIT, UNIT), UNIT)
    for k, out in enumerate((o0, o1, o2, o3)):
        unit = pl.multiple_of((quarter ^ k) * UNIT, UNIT)
        out[at, :] = total_ref[pl.ds(unit, UNIT), :].astype(jnp.bfloat16)

        @pl.when((slot & 3) == (quarter ^ k))
        def _():
            out[extra, :] = total_ref[4 * UNIT :, :].astype(jnp.bfloat16)


def head_sum_call(meta, exps, *stats):
    piece = pl.BlockSpec(memory_space=pltpu.VMEM)
    whole = lambda shape: pl.BlockSpec(shape, lambda i, meta: (0,) * len(shape))
    out = pl.BlockSpec((ROWS + UNIT, 256), lambda i, meta: (0, 0))
    return pl.pallas_call(
        head_sum_kernel,
        grid_spec=pltpu.PrefetchScalarGridSpec(
            num_scalar_prefetch=1,
            grid=(BLOCKS,),
            in_specs=[piece] + [whole(part.shape) for part in stats],
            out_specs=[out] * 4,
            scratch_shapes=[
                pltpu.VMEM((HALF, 256), jnp.float32),
                pltpu.VMEM((2, HEADS, 256), jnp.float32),
            ],
        ),
        out_shape=[pltpu.VMEM((ROWS + UNIT, 256), jnp.bfloat16)] * 4,
        cost_estimate=pl.CostEstimate(flops=0, bytes_accessed=11 << 20, transcendentals=0),
        compiler_params=pltpu.CompilerParams(vmem_limit_bytes=VMEM),
        name="head_sum",
    )(meta, *in_vmem(exps, *stats))


def key_places(meta):
    core, half, quarter = meta[2], meta[3], meta[4]
    rows = lax.broadcasted_iota(jnp.int32, (UNIT, 256), 0)
    out = []
    for u in range(16):
        out.append(rows + ((u // 2 * 4 + (u % 2) * 2 + core) * 160 + half * HALF + quarter * UNIT))
    for e in range(4):
        z, ylo = 2 * e + (quarter >> 1), quarter & 1
        out.append(rows + ((z * 4 + ylo * 2 + core) * 160 + half * HALF + 4 * UNIT))
    return out


def inner_of(keys, ia, ib, j):
    queries = jnp.concatenate([ia[j], ib[j]], axis=0)
    return lax.dot_general(
        keys[...], queries, (((1,), (1,)), ((), ())), preferred_element_type=jnp.float32
    ), queries


JSTEP = 32


def forward_kernel(meta, keys, m0, l0, m1, l1, ia, ib, pa, pb, wja, wjb, logits, here, sent):
    step = pl.program_id(0)

    @pl.when(step == 0)
    def _():
        logits[...] = jnp.zeros_like(logits)

    total = logits[...]
    for j in range(JSTEP):
        inner, _ = inner_of(keys, ia, ib, j)
        weight = jnp.concatenate([wja[j : j + 1, :], wjb[j : j + 1, :]], axis=1)
        total = total + weight * jnp.maximum(inner, 0.0)
    logits[...] = total

    @pl.when(step == NI // JSTEP - 1)
    def _():
        place = place_of(pa, pb)
        places = key_places(meta)
        top = jnp.full((1, 256), NEG, jnp.float32)
        for u in range(20):
            cut = slice(u * UNIT, (u + 1) * UNIT)
            value = logits[cut, :] * INDEX_SCALE
            value = jnp.where(places[u].astype(jnp.float32) <= place, value, NEG)
            logits[cut, :] = value
            top = jnp.maximum(top, jnp.max(value, axis=0, keepdims=True))
        safe = jnp.where(top == NEG, 0.0, top)
        total = jnp.sum(jnp.exp(logits[...] - safe), axis=0, keepdims=True)
        tops, totals = merge(m0[...], l0[...], m1[...], l1[...], SCORE2)
        for v, (heads, index) in enumerate(((tops, top), (totals, total))):
            rows = jnp.concatenate([heads, index, jnp.zeros((7, 256), jnp.float32)], axis=0)
            here[v] = rows
            sent[v] = swapped(rows)


def pair_kernel(ours, theirs, here, up, down):
    index = slice(HEADS, HEADS + 1)
    heads = slice(0, HEADS)
    tops, totals = merge(ours[0, heads, :], ours[1, heads, :], theirs[0, heads, :], theirs[1, heads, :], SCORE2)
    top, total = merge(ours[0, index, :], ours[1, index, :], theirs[0, index, :], theirs[1, index, :], LOG2E)
    for v, (main, extra) in enumerate(((tops, top), (totals, total))):
        pad = jnp.zeros((7, 256), jnp.float32)
        here[v] = jnp.concatenate([main, extra, pad], axis=0)
        up[v] = jnp.concatenate([main[0:4], main[12:16]], axis=0)
        down[v] = jnp.concatenate([main[4:12], extra, pad], axis=0)


def pair_call(ours, theirs):
    return pl.pallas_call(
        pair_kernel,
        out_shape=[pltpu.VMEM((2, rows, 256), jnp.float32) for rows in (24, 8, 16)],
        compiler_params=pltpu.CompilerParams(vmem_limit_bytes=1 << 20),
        name="pair_statistics",
    )(*in_vmem(ours, theirs))


def j_specs():
    whole = lambda shape: pl.BlockSpec(shape, lambda s, meta: (0,) * len(shape))
    queries = pl.BlockSpec((JSTEP, 128, DI), lambda s, meta: (s, 0, 0))
    weights = pl.BlockSpec((JSTEP, 128), lambda s, meta: (s, 0))
    return whole, [queries, queries], [weights, weights]


def forward_call(meta, keys, stats, ia, ib, pa, pb, wa, wb):
    whole, queries, weights = j_specs()
    return pl.pallas_call(
        forward_kernel,
        grid_spec=pltpu.PrefetchScalarGridSpec(
            num_scalar_prefetch=1,
            grid=(NI // JSTEP,),
            in_specs=[whole((ROWS, DI))] + [whole((HEADS, 256))] * 4 + queries + [whole((1, 128))] * 2 + weights,
            out_specs=[whole((ROWS, 256)), whole((2, 24, 256)), whole((2, 24, 256))],
        ),
        out_shape=[
            pltpu.VMEM((ROWS, 256), jnp.float32),
            pltpu.VMEM((2, 24, 256), jnp.float32),
            pltpu.VMEM((2, 24, 256), jnp.float32),
        ],
        cost_estimate=pl.CostEstimate(
            flops=2 * NI * ROWS * 256 * DI, bytes_accessed=5 << 20, transcendentals=0
        ),
        compiler_params=pltpu.CompilerParams(vmem_limit_bytes=VMEM),
        name="index_forward",
    )(meta, *in_vmem(keys, *stats, ia, ib, pa, pb, wa, wb))


def backward_kernel(meta, keys, logits, t0, t1, t2, t3, ia, ib, wja, wjb, rows_a, rows_b, kg, grad, acc):
    step = pl.program_id(0)

    @pl.when(step == 0)
    def _():
        parts = (t0, t1, t2, t3)

        def value(part, row):
            terms = part[ROWS:, :].astype(jnp.float32)
            return terms[row : row + 1] + terms[row + 1 : row + 2] + terms[row + 2 : row + 3]

        tops = [value(part, 0) for part in parts]
        top = tops[0]
        for other in tops[1:]:
            top = jnp.maximum(top, other)
        total = jnp.zeros((1, 256), jnp.float32)
        for part, other in zip(parts, tops):
            total = total + value(part, 3) * jnp.exp(other - top)
        norm = top + jnp.log(total)
        goal = jnp.zeros((ROWS, 256), jnp.float32)
        for part in parts:
            goal = goal + part[0:ROWS, :].astype(jnp.float32)
        goal = goal * (1.0 / 64.0)
        held = logits[...]
        seen = held != NEG
        logp = held - norm
        live = seen & (goal > 0)
        safe = jnp.where(goal > 0, goal, 1.0)
        part = jnp.where(live, goal * (jnp.log(safe) - logp), 0.0)
        part = jnp.sum(part, axis=0, keepdims=True)
        part = jnp.concatenate([part, jnp.zeros((15, 256), jnp.float32)], axis=0)
        rows_a[NI:, :] = part[:, :128]
        rows_b[NI:, :] = part[:, 128:]
        grad[...] = jnp.where(seen, jnp.exp(logp) - goal, 0.0) * INDEX_SCALE
        acc[...] = jnp.zeros_like(acc)

    total = acc[...]
    slope = grad[...]
    for j in range(JSTEP):
        inner, queries = inner_of(keys, ia, ib, j)
        weight = jnp.concatenate([wja[j : j + 1, :], wjb[j : j + 1, :]], axis=1)
        share = jnp.sum(slope * jnp.maximum(inner, 0.0), axis=0, keepdims=True)
        rows_a[pl.ds(step * JSTEP + j, 1), :] = share[:, :128]
        rows_b[pl.ds(step * JSTEP + j, 1), :] = share[:, 128:]
        coeff = jnp.where(inner > 0, slope * weight, 0.0).astype(jnp.bfloat16)
        total = total + jnp.dot(coeff, queries, preferred_element_type=jnp.float32)
    acc[...] = total

    @pl.when(step == NI // JSTEP - 1)
    def _():
        quarter = meta[4]
        for b in range(BLOCKS):
            kg[b, 0:UNIT, :] = acc[b * UNIT : (b + 1) * UNIT, :].astype(jnp.bfloat16)
            at = 256 + (b // 4) * UNIT
            extra = jnp.where(quarter == b % 4, acc[at : at + UNIT, :], 0.0)
            kg[b, UNIT:, :] = extra.astype(jnp.bfloat16)


def backward_call(meta, keys, logits, target, ia, ib, wa, wb):
    whole, queries, weights = j_specs()
    return pl.pallas_call(
        backward_kernel,
        grid_spec=pltpu.PrefetchScalarGridSpec(
            num_scalar_prefetch=1,
            grid=(NI // JSTEP,),
            in_specs=[
                whole((ROWS, DI)),
                whole((ROWS, 256)),
            ]
            + [whole((ROWS + UNIT, 256))] * 4
            + queries
            + weights,
            out_specs=[
                whole((NI + 16, 128)),
                whole((NI + 16, 128)),
                whole((BLOCKS, 2 * UNIT, DI)),
            ],
            scratch_shapes=[
                pltpu.VMEM((ROWS, 256), jnp.float32),
                pltpu.VMEM((ROWS, DI), jnp.float32),
            ],
        ),
        out_shape=[
            pltpu.VMEM((NI + 16, 128), jnp.float32),
            pltpu.VMEM((NI + 16, 128), jnp.float32),
            pltpu.VMEM((BLOCKS, 2 * UNIT, DI), jnp.bfloat16),
        ],
        cost_estimate=pl.CostEstimate(
            flops=4 * NI * ROWS * 256 * DI, bytes_accessed=6 << 20, transcendentals=0
        ),
        compiler_params=pltpu.CompilerParams(vmem_limit_bytes=VMEM),
        name="index_backward",
    )(meta, *in_vmem(keys, logits, *target, ia, ib, wa, wb))


def gather_head(value):
    wide = jnp.broadcast_to(value[None], (8,) + value.shape)
    return lax.all_to_all(wide, ("yhi", "xh", "xp"), 0, 0, tiled=True)


def after(value, *others):
    return lax.optimization_barrier((value,) + others)[0]


def body(main_queries, latent_keys, index_queries, index_weights, index_keys, tile_order, offset):
    z, ylo, core = lax.axis_index("z"), lax.axis_index("ylo"), lax.axis_index("core")
    half = lax.axis_index("xp")
    quarter = lax.axis_index("yhi") * 2 + lax.axis_index("xh")

    rows = jnp.arange(TILE, dtype=jnp.int32)
    place = (offset + (tile_order[:, None] * TILE + rows[None, :])).reshape(1, 128)
    pa, wa = place.astype(jnp.float32), index_weights.T
    own = jnp.concatenate([index_keys, latent_keys], axis=1)
    own = lax.dynamic_slice_in_dim(own, half * HALF, HALF, 0)
    meta = jnp.stack([z, ylo, core, half, quarter]).astype(jnp.int32)
    own, meta = lax.optimization_barrier((own, meta))

    queries = main_queries.transpose(0, 2, 1)
    f1, b1 = shift(own, dz=1), shift(own, dz=7)
    queries_far = swap_core(queries)
    halves = after(queries, own)
    left, right = shift(halves[:4], dx=1), shift(halves[4:], dx=3)
    f4 = shift(own, dz=4)
    f1, b1 = lax.optimization_barrier((f1, b1))
    f2, b2 = shift(f1, dz=1), shift(b1, dz=7)
    ia = index_queries.transpose(1, 0, 2)
    pb = swap_core(pa)
    f2, b2, ia, pb = lax.optimization_barrier((f2, b2, ia, pb))
    f3, b3 = shift(f2, dz=1), shift(b2, dz=7)
    f3, b3, left, right, f4 = lax.optimization_barrier((f3, b3, left, right, f4))
    left_far, right_far = swap_core(left), swap_core(right)
    y0, y1 = jnp.concatenate([own, f1, b1, f2]), jnp.concatenate([b2, f3, b3, f4])
    y0, y1 = shift(y0, dy=1), shift(y1, dy=3)
    ia, wa = lax.optimization_barrier((ia, wa, f4, left_far, right_far))[:2]
    ib, wb = swap_core(ia), swap_core(wa)

    sides = (queries, queries_far, left, left_far, right, right_far, pa, pb)
    exps, m0, l0, keys = score_call(meta, 0, [own, f1, b1, f2, b2, f3, b3, f4], [], *sides)
    exps, m1, l1, keys = score_call(meta, 1, [y0, y1], in_vmem(exps, keys), *sides)

    logits, ours, sent = forward_call(meta, keys, (m0, l0, m1, l1), ia, ib, pa, pb, wa, wb)
    here, up, down = pair_call(ours, swap_core(sent))
    up, down = shift(up, dx=1), shift(down, dx=3)
    sums = head_sum_call(meta, exps, m0, m1, here, up, down)
    group = (dict(dx=2), dict(dy=2), dict(dx=2, dy=2))
    far = shift(sums[3], **group[2])
    target = [sums[0]] + [shift(part, **move) for part, move in zip(sums[1:3], group)] + [far]

    mine, other, kg = backward_call(meta, keys, logits, target, ia, ib, wa, wb)
    rows_out = mine + swap_core(other)
    rows_high = lax.reduce_precision(rows_out, 8, 7)
    low = jnp.concatenate([jnp.zeros((NI + 8, 128), jnp.float32), (rows_out - rows_high)[NI : NI + 8]])
    tail = rows_high + low
    kg = lax.all_to_all(kg, ("z", "ylo"), 0, 0, tiled=True)
    kg = jnp.sum(kg.astype(jnp.float32), axis=0)
    last = gather_head(jnp.concatenate([kg, tail]).astype(jnp.bfloat16)).astype(jnp.float32)
    rows_sum = jnp.sum(last[:, 2 * UNIT :], axis=0)
    pieces = last[:, : 2 * UNIT].reshape(4, 2, 2 * UNIT, DI)
    main = pieces[:, :, :UNIT].transpose(1, 0, 2, 3).reshape(2, 4 * UNIT, DI)
    extra = jnp.sum(pieces[:, :, UNIT:], axis=0)
    key_grad = jnp.concatenate([main, extra], axis=1).reshape(160, DI)
    return rows_sum[NI] + rows_sum[NI + 8], rows_sum[:NI].T, key_grad


def solution(mesh):
    fine = Mesh(np.asarray(mesh.devices).reshape(2, 2, 2, 8, 2, 2), ALL)
    head, ctx = ("yhi", "xh", "xp"), ("z", "ylo", "core")
    in_specs = (
        P(head, ctx, None),
        P(ctx, None),
        P(ctx, None, None),
        P(ctx, None),
        P(ctx, None),
        P(ctx),
        P(),
    )
    out_specs = (P(ctx), P(ctx, None), P(ctx, None))
    return jax.shard_map(body, mesh=fine, in_specs=in_specs, out_specs=out_specs, check_vma=False)
```

```python
import math

import jax
import jax.numpy as jnp
import numpy as np
from jax import lax
from jax.experimental import pallas as pl
from jax.experimental.pallas import tpu as pltpu
from jax.sharding import Mesh
from jax.sharding import PartitionSpec as P

TILE = 32
DQ = 576
DI = 128
NI = 64
HALF = 80
UNIT = 16
BLOCKS = 16
ROWS = 320
SCORE2 = 192.0 ** (-0.5) * math.log2(math.e)
INDEX_SCALE = DI ** (-0.5)
ALL = ("yhi", "xh", "xp", "z", "ylo", "core")
NEG = -jnp.inf
VMEM = 18 << 20


def flat(x, y, z, c):
    return ((y // 2) * 4 + x) * 32 + (z * 2 + (y % 2)) * 2 + c


def shift(value, dx=0, dy=0, dz=0, flip=0):
    pairs = [
        (flat(x, y, z, c), flat((x + dx) % 4, (y + dy) % 4, (z + dz) % 8, c ^ flip))
        for x in range(4)
        for y in range(4)
        for z in range(8)
        for c in range(2)
    ]
    return lax.ppermute(value, ALL, pairs)


def ring(value):
    pairs = [
        (flat(x, y, z, c), flat(x, y, (z + (7 if c else 1)) % 8, c))
        for x in range(4)
        for y in range(4)
        for z in range(8)
        for c in range(2)
    ]
    return lax.ppermute(value, ALL, pairs)


def swap_core(value):
    return shift(value, flip=1)


LOG2E = math.log2(math.e)


def in_vmem(*values):
    return [pltpu.with_memory_space_constraint(value, pltpu.VMEM) for value in values]


def slot_of(meta, i):
    k = i & 7
    reach = (k + 1) >> 1
    step = reach * (1 - 2 * ((k & 1) ^ meta[2]))
    return ((meta[0] + 8 + step) & 7) * 2 + (meta[1] ^ (i >> 3))


def place_of(pa, pb):
    return jnp.concatenate([pa[...], pb[...]], axis=1)


def merge(m0, l0, m1, l1, rate):
    top = jnp.maximum(m0, m1)
    return top, l0 * jnp.exp2((m0 - top) * rate) + l1 * jnp.exp2((m1 - top) * rate)


def swapped(value):
    return jnp.concatenate([value[:, 128:], value[:, :128]], axis=1)


HEADS = 16
CHUNK = 8 * HALF


def score_kernel(chunk, spans, meta, *refs):
    n = len(spans)
    blocks, refs = refs[:n], refs[n:]
    if chunk:
        _, ik_before, refs = refs[0], refs[1], refs[2:]
    qa, qb, na, nb, ma, mb, pa, pb = refs[:8]
    e_ref, m_ref, l_ref, ik_ref, keys, bias, raw, tops, sems = refs[8:]
    step = pl.program_id(0)
    cut = 320

    @pl.when(step == 0)
    def _():
        copies = []
        at = 0
        for i, (block, (row, span)) in enumerate(zip(blocks, spans)):
            source = block.at[row : row + span, :]
            copies.append(pltpu.make_async_copy(source, keys.at[at : at + span, :], sems.at[i]))
            copies[-1].start()
            at += span
        place = place_of(pa, pb)
        offsets = lax.broadcasted_iota(jnp.int32, (HALF, 256), 0).astype(jnp.float32)
        slots = [slot_of(meta, 8 * chunk + i) for i in range(8)]
        for i in range(8):
            base = ((slots[i] * 2 + meta[2]) * 160 + meta[3] * HALF).astype(jnp.float32)
            bias[i * HALF : (i + 1) * HALF, :] = jnp.where(offsets + base <= place, 0.0, NEG)
        tops[...] = jnp.zeros_like(tops)
        ik_ref[...] = ik_before[...] if chunk else jnp.zeros_like(ik_ref)
        for copy in copies:
            copy.wait()
        quarter = meta[4]
        for i in range(8):
            slot = slots[i]
            mine = pl.ds(pl.multiple_of(i * HALF + quarter * UNIT, UNIT), UNIT)
            ik_ref[pl.ds(pl.multiple_of(slot * UNIT, UNIT), UNIT), :] = keys[mine, 0:DI]

            @pl.when((slot & 3) == quarter)
            def _():
                extra = pl.multiple_of(256 + (slot >> 2) * UNIT, UNIT)
                ik_ref[pl.ds(extra, UNIT), :] = keys[i * HALF + 4 * UNIT : (i + 1) * HALF, 0:DI]

    def work(now, last):
        for k in range(2):
            own = jnp.concatenate([qa[k], qb[k]], axis=1)
            left = jnp.concatenate([na[k], nb[k]], axis=1)
            right = jnp.concatenate([ma[k], mb[k]], axis=1)
            queries = jnp.where(step < 4, own, jnp.where(step < 6, left, right))
            top = jnp.max(tops[last, k], axis=0, keepdims=True)
            safe = jnp.where(top == NEG, 0.0, top)
            head = 2 * jnp.maximum(step - 1, 0) + k
            new = jnp.full((8, 256), NEG, jnp.float32)
            total = jnp.zeros((8, 256), jnp.float32)
            for t in range(0, CHUNK, cut):
                piece, rows = slice(t, t + cut), slice(chunk * CHUNK + t, chunk * CHUNK + t + cut)
                scores = jnp.dot(keys[piece, DI:], queries, preferred_element_type=jnp.float32)
                scores = scores + bias[piece, :]
                raw[now, k, piece, :] = scores
                new = jnp.maximum(new, jnp.max(scores.reshape(cut // 8, 8, 256), axis=0))
                exps = jnp.exp2((raw[last, k, piece, :] - safe) * SCORE2)
                e_ref[head, rows, :] = exps.astype(jnp.bfloat16)
                total = total + jnp.sum(exps.reshape(cut // 8, 8, 256), axis=0)
            tops[now, k] = new
            m_ref[pl.ds(head, 1), :] = top
            l_ref[pl.ds(head, 1), :] = jnp.sum(total, axis=0, keepdims=True)

    @pl.when(step % 2 == 0)
    def _():
        work(0, 1)

    @pl.when(step % 2 == 1)
    def _():
        work(1, 0)


def score_call(meta, chunk, blocks, before, qa, qb, na, nb, ma, mb, pa, pb):
    spans, blocks = [cut for _, cut in blocks], [block for block, _ in blocks]
    whole = lambda shape: pl.BlockSpec(shape, lambda h, meta: (0,) * len(shape))

    def heads(start, count):
        return pl.BlockSpec((2, DQ, 128), lambda h, meta: (jnp.clip(h - start, 0, count - 1), 0, 0))

    anywhere = pl.BlockSpec(memory_space=pl.ANY)
    exps = pl.BlockSpec(memory_space=pltpu.VMEM)
    return pl.pallas_call(
        lambda *refs: score_kernel(chunk, spans, *refs),
        grid_spec=pltpu.PrefetchScalarGridSpec(
            num_scalar_prefetch=1,
            grid=(HEADS // 2 + 1,),
            in_specs=[anywhere] * len(blocks)
            + ([exps, whole((ROWS, DI))] if chunk else [])
            + [heads(0, 4)] * 2
            + [heads(4, 2)] * 2
            + [heads(6, 2)] * 2
            + [whole((1, 128))] * 2,
            out_specs=[exps, whole((HEADS, 256)), whole((HEADS, 256)), whole((ROWS, DI))],
            scratch_shapes=[
                pltpu.VMEM((CHUNK, DI + DQ), jnp.bfloat16),
                pltpu.VMEM((CHUNK, 256), jnp.float32),
                pltpu.VMEM((2, 2, CHUNK, 256), jnp.float32),
                pltpu.VMEM((2, 2, 8, 256), jnp.float32),
                pltpu.SemaphoreType.DMA((len(blocks),)),
            ],
        ),
        out_shape=[
            pltpu.VMEM((HEADS, 2 * CHUNK, 256), jnp.bfloat16),
            pltpu.VMEM((HEADS, 256), jnp.float32),
            pltpu.VMEM((HEADS, 256), jnp.float32),
            pltpu.VMEM((ROWS, DI), jnp.bfloat16),
        ],
        input_output_aliases={1 + len(blocks): 0} if chunk else {},
        cost_estimate=pl.CostEstimate(
            flops=4 * HEADS * CHUNK * 256 * DQ,
            bytes_accessed=HEADS * CHUNK * 512,
            transcendentals=HEADS * CHUNK * 256,
        ),
        compiler_params=pltpu.CompilerParams(vmem_limit_bytes=VMEM),
        name="scores",
    )(meta, *in_vmem(*blocks), *before, *in_vmem(qa, qb, na, nb, ma, mb, pa, pb))


def head_sum_kernel(meta, e_ref, m0, m1, here, up, down, o0, o1, o2, o3, total_ref, ratio):
    i = pl.program_id(0)

    @pl.when(i == 0)
    def _():
        def side(v):
            heads = [down[v, 4:8, :], up[v, 4:8, :], up[v, 0:4, :], down[v, 0:4, :]]
            return jnp.concatenate(heads, axis=0)

        top, total = merge(here[0, 0:16, :], here[1, 0:16, :], side(0), side(1), SCORE2)
        for c, m in enumerate((m0, m1)):
            ratio[c] = jnp.exp2((m[...] - top) * SCORE2) / total
        index = slice(HEADS, HEADS + 1)
        terms = []
        for left in merge(here[0, index, :], here[1, index, :], down[0, 8:9, :], down[1, 8:9, :], LOG2E):
            for _ in range(3):
                term = left.astype(jnp.bfloat16).astype(jnp.float32)
                terms.append(term)
                left = left - term
        packed = jnp.concatenate(terms + [jnp.zeros((10, 256), jnp.float32)], axis=0)
        for out in (o0, o1, o2, o3):
            out[ROWS:, :] = packed.astype(jnp.bfloat16)

    chunk = i // 8
    total = jnp.zeros((HALF, 256), jnp.float32)
    for h in range(HEADS):
        part = e_ref[h, pl.ds(pl.multiple_of(i * HALF, HALF), HALF), :]
        total = total + part.astype(jnp.float32) * ratio[chunk, h : h + 1, :]
    total_ref[...] = total
    slot = slot_of(meta, i)
    quarter = meta[4]
    at = pl.ds(pl.multiple_of(slot * UNIT, UNIT), UNIT)
    extra = pl.ds(pl.multiple_of(256 + (slot >> 2) * UNIT, UNIT), UNIT)
    for k, out in enumerate((o0, o1, o2, o3)):
        unit = pl.multiple_of((quarter ^ k) * UNIT, UNIT)
        out[at, :] = total_ref[pl.ds(unit, UNIT), :].astype(jnp.bfloat16)

        @pl.when((slot & 3) == (quarter ^ k))
        def _():
            out[extra, :] = total_ref[4 * UNIT :, :].astype(jnp.bfloat16)


def head_sum_call(meta, exps, *stats):
    piece = pl.BlockSpec(memory_space=pltpu.VMEM)
    whole = lambda shape: pl.BlockSpec(shape, lambda i, meta: (0,) * len(shape))
    out = pl.BlockSpec((ROWS + UNIT, 256), lambda i, meta: (0, 0))
    return pl.pallas_call(
        head_sum_kernel,
        grid_spec=pltpu.PrefetchScalarGridSpec(
            num_scalar_prefetch=1,
            grid=(BLOCKS,),
            in_specs=[piece] + [whole(part.shape) for part in stats],
            out_specs=[out] * 4,
            scratch_shapes=[
                pltpu.VMEM((HALF, 256), jnp.float32),
                pltpu.VMEM((2, HEADS, 256), jnp.float32),
            ],
        ),
        out_shape=[pltpu.VMEM((ROWS + UNIT, 256), jnp.bfloat16)] * 4,
        cost_estimate=pl.CostEstimate(flops=0, bytes_accessed=11 << 20, transcendentals=0),
        compiler_params=pltpu.CompilerParams(vmem_limit_bytes=VMEM),
        name="head_sum",
    )(meta, *in_vmem(exps, *stats))


def key_places(meta):
    core, half, quarter = meta[2], meta[3], meta[4]
    rows = lax.broadcasted_iota(jnp.int32, (UNIT, 256), 0)
    out = []
    for u in range(16):
        out.append(rows + ((u // 2 * 4 + (u % 2) * 2 + core) * 160 + half * HALF + quarter * UNIT))
    for e in range(4):
        z, ylo = 2 * e + (quarter >> 1), quarter & 1
        out.append(rows + ((z * 4 + ylo * 2 + core) * 160 + half * HALF + 4 * UNIT))
    return out


def inner_of(keys, ia, ib, j):
    queries = jnp.concatenate([ia[j], ib[j]], axis=0)
    return lax.dot_general(
        keys[...], queries, (((1,), (1,)), ((), ())), preferred_element_type=jnp.float32
    ), queries


JSTEP = 32


def forward_kernel(meta, keys, m0, l0, m1, l1, ia, ib, pa, pb, wja, wjb, logits, here, sent):
    step = pl.program_id(0)

    @pl.when(step == 0)
    def _():
        logits[...] = jnp.zeros_like(logits)

    total = logits[...]
    for j in range(JSTEP):
        inner, _ = inner_of(keys, ia, ib, j)
        weight = jnp.concatenate([wja[j : j + 1, :], wjb[j : j + 1, :]], axis=1)
        total = total + weight * jnp.maximum(inner, 0.0)
    logits[...] = total

    @pl.when(step == NI // JSTEP - 1)
    def _():
        place = place_of(pa, pb)
        places = key_places(meta)
        top = jnp.full((1, 256), NEG, jnp.float32)
        for u in range(20):
            cut = slice(u * UNIT, (u + 1) * UNIT)
            value = logits[cut, :] * INDEX_SCALE
            value = jnp.where(places[u].astype(jnp.float32) <= place, value, NEG)
            logits[cut, :] = value
            top = jnp.maximum(top, jnp.max(value, axis=0, keepdims=True))
        safe = jnp.where(top == NEG, 0.0, top)
        total = jnp.sum(jnp.exp(logits[...] - safe), axis=0, keepdims=True)
        tops, totals = merge(m0[...], l0[...], m1[...], l1[...], SCORE2)
        for v, (heads, index) in enumerate(((tops, top), (totals, total))):
            rows = jnp.concatenate([heads, index, jnp.zeros((7, 256), jnp.float32)], axis=0)
            here[v] = rows
            sent[v] = swapped(rows)


def pair_kernel(ours, theirs, here, up, down):
    index = slice(HEADS, HEADS + 1)
    heads = slice(0, HEADS)
    tops, totals = merge(ours[0, heads, :], ours[1, heads, :], theirs[0, heads, :], theirs[1, heads, :], SCORE2)
    top, total = merge(ours[0, index, :], ours[1, index, :], theirs[0, index, :], theirs[1, index, :], LOG2E)
    for v, (main, extra) in enumerate(((tops, top), (totals, total))):
        pad = jnp.zeros((7, 256), jnp.float32)
        here[v] = jnp.concatenate([main, extra, pad], axis=0)
        up[v] = jnp.concatenate([main[0:4], main[12:16]], axis=0)
        down[v] = jnp.concatenate([main[4:12], extra, pad], axis=0)


def pair_call(ours, theirs):
    return pl.pallas_call(
        pair_kernel,
        out_shape=[pltpu.VMEM((2, rows, 256), jnp.float32) for rows in (24, 8, 16)],
        compiler_params=pltpu.CompilerParams(vmem_limit_bytes=1 << 20),
        name="pair_statistics",
    )(*in_vmem(ours, theirs))


def j_specs():
    whole = lambda shape: pl.BlockSpec(shape, lambda s, meta: (0,) * len(shape))
    queries = pl.BlockSpec((JSTEP, 128, DI), lambda s, meta: (s, 0, 0))
    weights = pl.BlockSpec((JSTEP, 128), lambda s, meta: (s, 0))
    return whole, [queries, queries], [weights, weights]


def forward_call(meta, keys, stats, ia, ib, pa, pb, wa, wb):
    whole, queries, weights = j_specs()
    return pl.pallas_call(
        forward_kernel,
        grid_spec=pltpu.PrefetchScalarGridSpec(
            num_scalar_prefetch=1,
            grid=(NI // JSTEP,),
            in_specs=[whole((ROWS, DI))] + [whole((HEADS, 256))] * 4 + queries + [whole((1, 128))] * 2 + weights,
            out_specs=[whole((ROWS, 256)), whole((2, 24, 256)), whole((2, 24, 256))],
        ),
        out_shape=[
            pltpu.VMEM((ROWS, 256), jnp.float32),
            pltpu.VMEM((2, 24, 256), jnp.float32),
            pltpu.VMEM((2, 24, 256), jnp.float32),
        ],
        cost_estimate=pl.CostEstimate(
            flops=2 * NI * ROWS * 256 * DI, bytes_accessed=5 << 20, transcendentals=0
        ),
        compiler_params=pltpu.CompilerParams(vmem_limit_bytes=VMEM),
        name="index_forward",
    )(meta, *in_vmem(keys, *stats, ia, ib, pa, pb, wa, wb))


def backward_kernel(meta, keys, logits, t0, t1, t2, t3, ia, ib, wja, wjb, rows_a, rows_b, kg, grad, acc):
    step = pl.program_id(0)

    @pl.when(step == 0)
    def _():
        parts = (t0, t1, t2, t3)

        def value(part, row):
            terms = part[ROWS:, :].astype(jnp.float32)
            return terms[row : row + 1] + terms[row + 1 : row + 2] + terms[row + 2 : row + 3]

        tops = [value(part, 0) for part in parts]
        top = tops[0]
        for other in tops[1:]:
            top = jnp.maximum(top, other)
        total = jnp.zeros((1, 256), jnp.float32)
        for part, other in zip(parts, tops):
            total = total + value(part, 3) * jnp.exp(other - top)
        norm = top + jnp.log(total)
        goal = jnp.zeros((ROWS, 256), jnp.float32)
        for part in parts:
            goal = goal + part[0:ROWS, :].astype(jnp.float32)
        goal = goal * (1.0 / 64.0)
        held = logits[...]
        seen = held != NEG
        logp = held - norm
        live = seen & (goal > 0)
        safe = jnp.where(goal > 0, goal, 1.0)
        part = jnp.where(live, goal * (jnp.log(safe) - logp), 0.0)
        part = jnp.sum(part, axis=0, keepdims=True)
        part = jnp.concatenate([part, jnp.zeros((15, 256), jnp.float32)], axis=0)
        rows_a[NI:, :] = part[:, :128]
        rows_b[NI:, :] = part[:, 128:]
        grad[...] = jnp.where(seen, jnp.exp(logp) - goal, 0.0) * INDEX_SCALE
        acc[...] = jnp.zeros_like(acc)

    total = acc[...]
    slope = grad[...]
    for j in range(JSTEP):
        inner, queries = inner_of(keys, ia, ib, j)
        weight = jnp.concatenate([wja[j : j + 1, :], wjb[j : j + 1, :]], axis=1)
        share = jnp.sum(slope * jnp.maximum(inner, 0.0), axis=0, keepdims=True)
        rows_a[pl.ds(step * JSTEP + j, 1), :] = share[:, :128]
        rows_b[pl.ds(step * JSTEP + j, 1), :] = share[:, 128:]
        coeff = jnp.where(inner > 0, slope * weight, 0.0).astype(jnp.bfloat16)
        total = total + jnp.dot(coeff, queries, preferred_element_type=jnp.float32)
    acc[...] = total

    @pl.when(step == NI // JSTEP - 1)
    def _():
        quarter = meta[4]
        for b in range(BLOCKS):
            kg[b, 0:UNIT, :] = acc[b * UNIT : (b + 1) * UNIT, :].astype(jnp.bfloat16)
            at = 256 + (b // 4) * UNIT
            extra = jnp.where(quarter == b % 4, acc[at : at + UNIT, :], 0.0)
            kg[b, UNIT:, :] = extra.astype(jnp.bfloat16)


def backward_call(meta, keys, logits, target, ia, ib, wa, wb):
    whole, queries, weights = j_specs()
    return pl.pallas_call(
        backward_kernel,
        grid_spec=pltpu.PrefetchScalarGridSpec(
            num_scalar_prefetch=1,
            grid=(NI // JSTEP,),
            in_specs=[
                whole((ROWS, DI)),
                whole((ROWS, 256)),
            ]
            + [whole((ROWS + UNIT, 256))] * 4
            + queries
            + weights,
            out_specs=[
                whole((NI + 16, 128)),
                whole((NI + 16, 128)),
                whole((BLOCKS, 2 * UNIT, DI)),
            ],
            scratch_shapes=[
                pltpu.VMEM((ROWS, 256), jnp.float32),
                pltpu.VMEM((ROWS, DI), jnp.float32),
            ],
        ),
        out_shape=[
            pltpu.VMEM((NI + 16, 128), jnp.float32),
            pltpu.VMEM((NI + 16, 128), jnp.float32),
            pltpu.VMEM((BLOCKS, 2 * UNIT, DI), jnp.bfloat16),
        ],
        cost_estimate=pl.CostEstimate(
            flops=4 * NI * ROWS * 256 * DI, bytes_accessed=6 << 20, transcendentals=0
        ),
        compiler_params=pltpu.CompilerParams(vmem_limit_bytes=VMEM),
        name="index_backward",
    )(meta, *in_vmem(keys, logits, *target, ia, ib, wa, wb))


def gather_head(value):
    wide = jnp.broadcast_to(value[None], (8,) + value.shape)
    return lax.all_to_all(wide, ("yhi", "xh", "xp"), 0, 0, tiled=True)


def after(value, *others):
    return lax.optimization_barrier((value,) + others)[0]


def body(main_queries, latent_keys, index_queries, index_weights, index_keys, tile_order, offset):
    z, ylo, core = lax.axis_index("z"), lax.axis_index("ylo"), lax.axis_index("core")
    half = lax.axis_index("xp")
    quarter = lax.axis_index("yhi") * 2 + lax.axis_index("xh")

    rows = jnp.arange(TILE, dtype=jnp.int32)
    place = (offset + (tile_order[:, None] * TILE + rows[None, :])).reshape(1, 128)
    pa, wa = place.astype(jnp.float32), index_weights.T
    own = jnp.concatenate([index_keys, latent_keys], axis=1)
    own = lax.dynamic_slice_in_dim(own, half * HALF, HALF, 0)
    meta = jnp.stack([z, ylo, core, half, quarter]).astype(jnp.int32)
    own, meta = lax.optimization_barrier((own, meta))

    queries = main_queries.transpose(0, 2, 1)
    start = jnp.concatenate([own, swap_core(own)])
    r1 = ring(start)
    queries_far = swap_core(queries)
    halves = after(queries, start)
    left, right = shift(halves[:4], dx=1), shift(halves[4:], dx=3)
    r2 = ring(r1)
    ia = index_queries.transpose(1, 0, 2)
    pb = swap_core(pa)
    r2, ia, pb = lax.optimization_barrier((r2, ia, pb))
    r3 = ring(r2)
    x1, x2 = swap_core(r1), swap_core(r2)
    r3, left, right, x1, x2 = lax.optimization_barrier((r3, left, right, x1, x2))
    x3 = swap_core(r3)
    r4 = ring(r3[:HALF])
    r4, x3 = lax.optimization_barrier((r4, x3))
    left_far, right_far = swap_core(left), swap_core(right)
    y0 = jnp.concatenate([own, r1[:HALF], x1[HALF:], r2[:HALF]])
    y1 = jnp.concatenate([x2[HALF:], r3[:HALF], x3[HALF:], r4])
    y0, y1 = shift(y0, dy=1), shift(y1, dy=3)
    ia, wa = lax.optimization_barrier((ia, wa, r4, left_far, right_far))[:2]
    ib, wb = swap_core(ia), swap_core(wa)

    sides = (queries, queries_far, left, left_far, right, right_far, pa, pb)
    low, high = (0, HALF), (HALF, HALF)
    column = [(own, low), (r1, low), (x1, high), (r2, low), (x2, high), (r3, low), (x3, high), (r4, low)]
    exps, m0, l0, keys = score_call(meta, 0, column, [], *sides)
    exps, m1, l1, keys = score_call(meta, 1, [(y0, (0, 4 * HALF)), (y1, (0, 4 * HALF))], in_vmem(exps, keys), *sides)

    logits, ours, sent = forward_call(meta, keys, (m0, l0, m1, l1), ia, ib, pa, pb, wa, wb)
    here, up, down = pair_call(ours, swap_core(sent))
    up, down = shift(up, dx=1), shift(down, dx=3)
    sums = head_sum_call(meta, exps, m0, m1, here, up, down)
    group = (dict(dx=2), dict(dy=2), dict(dx=2, dy=2))
    far = shift(sums[3], **group[2])
    target = [sums[0]] + [shift(part, **move) for part, move in zip(sums[1:3], group)] + [far]

    mine, other, kg = backward_call(meta, keys, logits, target, ia, ib, wa, wb)
    rows_out = mine + swap_core(other)
    rows_high = lax.reduce_precision(rows_out, 8, 7)
    low = jnp.concatenate([jnp.zeros((NI + 8, 128), jnp.float32), (rows_out - rows_high)[NI : NI + 8]])
    tail = rows_high + low
    kg = lax.all_to_all(kg, ("z", "ylo"), 0, 0, tiled=True)
    kg = jnp.sum(kg.astype(jnp.float32), axis=0)
    last = gather_head(jnp.concatenate([kg, tail]).astype(jnp.bfloat16)).astype(jnp.float32)
    rows_sum = jnp.sum(last[:, 2 * UNIT :], axis=0)
    pieces = last[:, : 2 * UNIT].reshape(4, 2, 2 * UNIT, DI)
    main = pieces[:, :, :UNIT].transpose(1, 0, 2, 3).reshape(2, 4 * UNIT, DI)
    extra = jnp.sum(pieces[:, :, UNIT:], axis=0)
    key_grad = jnp.concatenate([main, extra], axis=1).reshape(160, DI)
    return rows_sum[NI] + rows_sum[NI + 8], rows_sum[:NI].T, key_grad


def solution(mesh):
    fine = Mesh(np.asarray(mesh.devices).reshape(2, 2, 2, 8, 2, 2), ALL)
    head, ctx = ("yhi", "xh", "xp"), ("z", "ylo", "core")
    in_specs = (
        P(head, ctx, None),
        P(ctx, None),
        P(ctx, None, None),
        P(ctx, None),
        P(ctx, None),
        P(ctx),
        P(),
    )
    out_specs = (P(ctx), P(ctx, None), P(ctx, None))
    return jax.shard_map(body, mesh=fine, in_specs=in_specs, out_specs=out_specs, check_vma=False)
```

```python
import math

import jax
import jax.numpy as jnp
import numpy as np
from jax import lax
from jax.experimental import pallas as pl
from jax.experimental.pallas import tpu as pltpu
from jax.sharding import Mesh
from jax.sharding import PartitionSpec as P

TILE = 32
DQ = 576
DI = 128
NI = 64
HALF = 80
UNIT = 16
BLOCKS = 16
ROWS = 320
SCORE2 = 192.0 ** (-0.5) * math.log2(math.e)
INDEX_SCALE = DI ** (-0.5)
ALL = ("yhi", "xh", "xp", "z", "ylo", "core")
NEG = -jnp.inf
VMEM = 12 << 20
HERE = pl.BlockSpec(memory_space=pltpu.VMEM)


def flat(x, y, z, c):
    return ((y // 2) * 4 + x) * 32 + (z * 2 + (y % 2)) * 2 + c


def shift(value, dx=0, dy=0, dz=0, flip=0):
    pairs = [
        (flat(x, y, z, c), flat((x + dx) % 4, (y + dy) % 4, (z + dz) % 8, c ^ flip))
        for x in range(4)
        for y in range(4)
        for z in range(8)
        for c in range(2)
    ]
    return lax.ppermute(value, ALL, pairs)


def swap_core(value):
    return shift(value, flip=1)


LOG2E = math.log2(math.e)


def in_vmem(*values):
    return [pltpu.with_memory_space_constraint(value, pltpu.VMEM) for value in values]


def slot_of(meta, i):
    k = i & 7
    reach = (k + 1) >> 1
    step = reach * (1 - 2 * (k & 1))
    return ((meta[0] + 8 + step) & 7) * 2 + (meta[1] ^ (i >> 3))


def place_of(pa, pb):
    return jnp.concatenate([pa[...], pb[...]], axis=1)


def merge(m0, l0, m1, l1, rate):
    top = jnp.maximum(m0, m1)
    return top, l0 * jnp.exp2((m0 - top) * rate) + l1 * jnp.exp2((m1 - top) * rate)


def swapped(value):
    return jnp.concatenate([value[:, 128:], value[:, :128]], axis=1)


HEADS = 16
CHUNK = 8 * HALF


def score_kernel(chunk, spans, meta, *refs):
    n = len(spans)
    blocks, refs = refs[:n], refs[n:]
    if chunk:
        _, ik_before, refs = refs[0], refs[1], refs[2:]
    qa, qb, na, nb, ma, mb, pa, pb = refs[:8]
    e_ref, m_ref, l_ref, ik_ref, keys, bias, raw, tops, sems = refs[8:]
    step = pl.program_id(0)
    cut = 320

    @pl.when(step == 0)
    def _():
        copies = []
        at = 0
        for i, (block, span) in enumerate(zip(blocks, spans)):
            copies.append(pltpu.make_async_copy(block, keys.at[at : at + span, :], sems.at[i]))
            copies[-1].start()
            at += span
        place = place_of(pa, pb)
        offsets = lax.broadcasted_iota(jnp.int32, (HALF, 256), 0).astype(jnp.float32)
        slots = [slot_of(meta, 8 * chunk + i) for i in range(8)]
        for i in range(8):
            base = ((slots[i] * 2 + meta[2]) * 160 + meta[3] * HALF).astype(jnp.float32)
            bias[i * HALF : (i + 1) * HALF, :] = jnp.where(offsets + base <= place, 0.0, NEG)
        tops[...] = jnp.zeros_like(tops)
        ik_ref[...] = ik_before[...] if chunk else jnp.zeros_like(ik_ref)
        for copy in copies:
            copy.wait()
        quarter = meta[4]
        for i in range(8):
            slot = slots[i]
            mine = pl.ds(pl.multiple_of(i * HALF + quarter * UNIT, UNIT), UNIT)
            ik_ref[pl.ds(pl.multiple_of(slot * UNIT, UNIT), UNIT), :] = keys[mine, 0:DI]

            @pl.when((slot & 3) == quarter)
            def _():
                extra = pl.multiple_of(256 + (slot >> 2) * UNIT, UNIT)
                ik_ref[pl.ds(extra, UNIT), :] = keys[i * HALF + 4 * UNIT : (i + 1) * HALF, 0:DI]

    def work(now, last):
        for k in range(2):
            own, left, right = (
                jnp.concatenate([a[at], b[at]], axis=1)
                for a, b, at in (
                    (qa, qb, 2 * jnp.minimum(step, 3) + k),
                    (na, nb, 2 * jnp.clip(step - 4, 0, 1) + k),
                    (ma, mb, 2 * jnp.clip(step - 6, 0, 1) + k),
                )
            )
            queries = jnp.where(step < 4, own, jnp.where(step < 6, left, right))
            top = jnp.max(tops[last, k], axis=0, keepdims=True)
            safe = jnp.where(top == NEG, 0.0, top)
            head = 2 * jnp.maximum(step - 1, 0) + k
            new = jnp.full((8, 256), NEG, jnp.float32)
            total = jnp.zeros((8, 256), jnp.float32)
            for t in range(0, CHUNK, cut):
                piece, rows = slice(t, t + cut), slice(chunk * CHUNK + t, chunk * CHUNK + t + cut)
                scores = jnp.dot(keys[piece, DI:], queries, preferred_element_type=jnp.float32)
                scores = scores + bias[piece, :]
                raw[now, k, piece, :] = scores
                new = jnp.maximum(new, jnp.max(scores.reshape(cut // 8, 8, 256), axis=0))
                exps = jnp.exp2((raw[last, k, piece, :] - safe) * SCORE2)
                e_ref[head, rows, :] = exps.astype(jnp.bfloat16)
                total = total + jnp.sum(exps.reshape(cut // 8, 8, 256), axis=0)
            tops[now, k] = new
            m_ref[pl.ds(head, 1), :] = top
            l_ref[pl.ds(head, 1), :] = jnp.sum(total, axis=0, keepdims=True)

    @pl.when(step % 2 == 0)
    def _():
        work(0, 1)

    @pl.when(step % 2 == 1)
    def _():
        work(1, 0)


def score_call(meta, chunk, blocks, before, qa, qb, na, nb, ma, mb, pa, pb):
    spans = [b.shape[0] for b in blocks]
    anywhere = pl.BlockSpec(memory_space=pl.ANY)
    return pl.pallas_call(
        lambda *refs: score_kernel(chunk, spans, *refs),
        grid_spec=pltpu.PrefetchScalarGridSpec(
            num_scalar_prefetch=1,
            grid=(HEADS // 2 + 1,),
            in_specs=[anywhere] * len(blocks)
            + [HERE] * (len(before) + 8),
            out_specs=[HERE] * 4,
            scratch_shapes=[
                pltpu.VMEM((CHUNK, DI + DQ), jnp.bfloat16),
                pltpu.VMEM((CHUNK, 256), jnp.float32),
                pltpu.VMEM((2, 2, CHUNK, 256), jnp.float32),
                pltpu.VMEM((2, 2, 8, 256), jnp.float32),
                pltpu.SemaphoreType.DMA((len(blocks),)),
            ],
        ),
        out_shape=[
            pltpu.VMEM((HEADS, 2 * CHUNK, 256), jnp.bfloat16),
            pltpu.VMEM((HEADS, 256), jnp.float32),
            pltpu.VMEM((HEADS, 256), jnp.float32),
            pltpu.VMEM((ROWS, DI), jnp.bfloat16),
        ],
        input_output_aliases={1 + len(blocks): 0} if chunk else {},
        cost_estimate=pl.CostEstimate(
            flops=4 * HEADS * CHUNK * 256 * DQ,
            bytes_accessed=HEADS * CHUNK * 512,
            transcendentals=HEADS * CHUNK * 256,
        ),
        compiler_params=pltpu.CompilerParams(vmem_limit_bytes=VMEM),
        name="scores",
    )(meta, *in_vmem(*blocks), *before, *in_vmem(qa, qb, na, nb, ma, mb, pa, pb))


def head_sum_kernel(meta, e_ref, m0, m1, here, up, down, o0, o1, o2, o3, total_ref, ratio):
    i = pl.program_id(0)

    @pl.when(i == 0)
    def _():
        def side(v):
            heads = [down[v, 4:8, :], up[v, 4:8, :], up[v, 0:4, :], down[v, 0:4, :]]
            return jnp.concatenate(heads, axis=0)

        top, total = merge(here[0, 0:16, :], here[1, 0:16, :], side(0), side(1), SCORE2)
        for c, m in enumerate((m0, m1)):
            ratio[c] = jnp.exp2((m[...] - top) * SCORE2) / total
        index = slice(HEADS, HEADS + 1)
        terms = []
        for left in merge(here[0, index, :], here[1, index, :], down[0, 8:9, :], down[1, 8:9, :], LOG2E):
            for _ in range(3):
                term = left.astype(jnp.bfloat16).astype(jnp.float32)
                terms.append(term)
                left = left - term
        packed = jnp.concatenate(terms + [jnp.zeros((10, 256), jnp.float32)], axis=0)
        for out in (o0, o1, o2, o3):
            out[ROWS:, :] = packed.astype(jnp.bfloat16)

    chunk = i // 8
    total = jnp.zeros((HALF, 256), jnp.float32)
    for h in range(HEADS):
        part = e_ref[h, pl.ds(pl.multiple_of(i * HALF, HALF), HALF), :]
        total = total + part.astype(jnp.float32) * ratio[chunk, h : h + 1, :]
    total_ref[...] = total
    slot = slot_of(meta, i)
    quarter = meta[4]
    at = pl.ds(pl.multiple_of(slot * UNIT, UNIT), UNIT)
    extra = pl.ds(pl.multiple_of(256 + (slot >> 2) * UNIT, UNIT), UNIT)
    for k, out in enumerate((o0, o1, o2, o3)):
        unit = pl.multiple_of((quarter ^ k) * UNIT, UNIT)
        out[at, :] = total_ref[pl.ds(unit, UNIT), :].astype(jnp.bfloat16)

        @pl.when((slot & 3) == (quarter ^ k))
        def _():
            out[extra, :] = total_ref[4 * UNIT :, :].astype(jnp.bfloat16)


def head_sum_call(meta, exps, *stats):
    return pl.pallas_call(
        head_sum_kernel,
        grid_spec=pltpu.PrefetchScalarGridSpec(
            num_scalar_prefetch=1,
            grid=(BLOCKS,),
            in_specs=[HERE] * (1 + len(stats)),
            out_specs=[HERE] * 4,
            scratch_shapes=[
                pltpu.VMEM((HALF, 256), jnp.float32),
                pltpu.VMEM((2, HEADS, 256), jnp.float32),
            ],
        ),
        out_shape=[pltpu.VMEM((ROWS + UNIT, 256), jnp.bfloat16)] * 4,
        cost_estimate=pl.CostEstimate(flops=0, bytes_accessed=11 << 20, transcendentals=0),
        compiler_params=pltpu.CompilerParams(vmem_limit_bytes=VMEM),
        name="head_sum",
    )(meta, *in_vmem(exps, *stats))


def key_places(meta):
    core, half, quarter = meta[2], meta[3], meta[4]
    rows = lax.broadcasted_iota(jnp.int32, (UNIT, 256), 0)
    out = []
    for u in range(16):
        out.append(rows + ((u // 2 * 4 + (u % 2) * 2 + core) * 160 + half * HALF + quarter * UNIT))
    for e in range(4):
        z, ylo = 2 * e + (quarter >> 1), quarter & 1
        out.append(rows + ((z * 4 + ylo * 2 + core) * 160 + half * HALF + 4 * UNIT))
    return out


def inner_of(keys, ia, ib, j):
    queries = jnp.concatenate([ia[j], ib[j]], axis=0)
    return lax.dot_general(
        keys[...], queries, (((1,), (1,)), ((), ())), preferred_element_type=jnp.float32
    ), queries


JSTEP = 32


def forward_kernel(meta, keys, m0, l0, m1, l1, ia, ib, pa, pb, wja, wjb, logits, here, sent):
    step = pl.program_id(0)

    @pl.when(step == 0)
    def _():
        logits[...] = jnp.zeros_like(logits)

    total = logits[...]
    for j in range(JSTEP):
        at = step * JSTEP + j
        inner, _ = inner_of(keys, ia, ib, at)
        weight = jnp.concatenate([wja[pl.ds(at, 1), :], wjb[pl.ds(at, 1), :]], axis=1)
        total = total + weight * jnp.maximum(inner, 0.0)
    logits[...] = total

    @pl.when(step == NI // JSTEP - 1)
    def _():
        place = place_of(pa, pb)
        places = key_places(meta)
        top = jnp.full((1, 256), NEG, jnp.float32)
        for u in range(20):
            cut = slice(u * UNIT, (u + 1) * UNIT)
            value = logits[cut, :] * INDEX_SCALE
            value = jnp.where(places[u].astype(jnp.float32) <= place, value, NEG)
            logits[cut, :] = value
            top = jnp.maximum(top, jnp.max(value, axis=0, keepdims=True))
        safe = jnp.where(top == NEG, 0.0, top)
        total = jnp.sum(jnp.exp(logits[...] - safe), axis=0, keepdims=True)
        tops, totals = merge(m0[...], l0[...], m1[...], l1[...], SCORE2)
        for v, (heads, index) in enumerate(((tops, top), (totals, total))):
            rows = jnp.concatenate([heads, index, jnp.zeros((7, 256), jnp.float32)], axis=0)
            here[v] = rows
            sent[v] = swapped(rows)


def pair_kernel(ours, theirs, here, up, down):
    index = slice(HEADS, HEADS + 1)
    heads = slice(0, HEADS)
    tops, totals = merge(ours[0, heads, :], ours[1, heads, :], theirs[0, heads, :], theirs[1, heads, :], SCORE2)
    top, total = merge(ours[0, index, :], ours[1, index, :], theirs[0, index, :], theirs[1, index, :], LOG2E)
    for v, (main, extra) in enumerate(((tops, top), (totals, total))):
        pad = jnp.zeros((7, 256), jnp.float32)
        here[v] = jnp.concatenate([main, extra, pad], axis=0)
        up[v] = jnp.concatenate([main[0:4], main[12:16]], axis=0)
        down[v] = jnp.concatenate([main[4:12], extra, pad], axis=0)


def pair_call(ours, theirs):
    return pl.pallas_call(
        pair_kernel,
        in_specs=[HERE] * 2,
        out_specs=[HERE] * 3,
        out_shape=[pltpu.VMEM((2, rows, 256), jnp.float32) for rows in (24, 8, 16)],
        compiler_params=pltpu.CompilerParams(vmem_limit_bytes=1 << 20),
        name="pair_statistics",
    )(*in_vmem(ours, theirs))


def forward_call(meta, keys, stats, ia, ib, pa, pb, wa, wb):
    return pl.pallas_call(
        forward_kernel,
        grid_spec=pltpu.PrefetchScalarGridSpec(
            num_scalar_prefetch=1,
            grid=(NI // JSTEP,),
            in_specs=[HERE] * 11,
            out_specs=[HERE] * 3,
        ),
        out_shape=[
            pltpu.VMEM((ROWS, 256), jnp.float32),
            pltpu.VMEM((2, 24, 256), jnp.float32),
            pltpu.VMEM((2, 24, 256), jnp.float32),
        ],
        cost_estimate=pl.CostEstimate(
            flops=2 * NI * ROWS * 256 * DI, bytes_accessed=5 << 20, transcendentals=0
        ),
        compiler_params=pltpu.CompilerParams(vmem_limit_bytes=VMEM),
        name="index_forward",
    )(meta, *in_vmem(keys, *stats, ia, ib, pa, pb, wa, wb))


def backward_kernel(meta, keys, logits, t0, t1, t2, t3, ia, ib, wja, wjb, rows_a, rows_b, kg, grad, acc):
    step = pl.program_id(0)

    @pl.when(step == 0)
    def _():
        parts = (t0, t1, t2, t3)

        def value(part, row):
            terms = part[ROWS:, :].astype(jnp.float32)
            return terms[row : row + 1] + terms[row + 1 : row + 2] + terms[row + 2 : row + 3]

        tops = [value(part, 0) for part in parts]
        top = tops[0]
        for other in tops[1:]:
            top = jnp.maximum(top, other)
        total = jnp.zeros((1, 256), jnp.float32)
        for part, other in zip(parts, tops):
            total = total + value(part, 3) * jnp.exp(other - top)
        norm = top + jnp.log(total)
        goal = jnp.zeros((ROWS, 256), jnp.float32)
        for part in parts:
            goal = goal + part[0:ROWS, :].astype(jnp.float32)
        goal = goal * (1.0 / 64.0)
        held = logits[...]
        seen = held != NEG
        logp = held - norm
        live = seen & (goal > 0)
        safe = jnp.where(goal > 0, goal, 1.0)
        part = jnp.where(live, goal * (jnp.log(safe) - logp), 0.0)
        part = jnp.sum(part, axis=0, keepdims=True)
        part = jnp.concatenate([part, jnp.zeros((15, 256), jnp.float32)], axis=0)
        rows_a[NI:, :] = part[:, :128]
        rows_b[NI:, :] = part[:, 128:]
        grad[...] = jnp.where(seen, jnp.exp(logp) - goal, 0.0) * INDEX_SCALE
        acc[...] = jnp.zeros_like(acc)

    total = acc[...]
    slope = grad[...]
    for j in range(JSTEP):
        at = step * JSTEP + j
        inner, queries = inner_of(keys, ia, ib, at)
        weight = jnp.concatenate([wja[pl.ds(at, 1), :], wjb[pl.ds(at, 1), :]], axis=1)
        share = jnp.sum(slope * jnp.maximum(inner, 0.0), axis=0, keepdims=True)
        rows_a[pl.ds(at, 1), :] = share[:, :128]
        rows_b[pl.ds(at, 1), :] = share[:, 128:]
        coeff = jnp.where(inner > 0, slope * weight, 0.0).astype(jnp.bfloat16)
        total = total + jnp.dot(coeff, queries, preferred_element_type=jnp.float32)
    acc[...] = total

    @pl.when(step == NI // JSTEP - 1)
    def _():
        quarter = meta[4]
        for b in range(BLOCKS):
            kg[b, 0:UNIT, :] = acc[b * UNIT : (b + 1) * UNIT, :].astype(jnp.bfloat16)
            at = 256 + (b // 4) * UNIT
            extra = jnp.where(quarter == b % 4, acc[at : at + UNIT, :], 0.0)
            kg[b, UNIT:, :] = extra.astype(jnp.bfloat16)


def backward_call(meta, keys, logits, target, ia, ib, wa, wb):
    return pl.pallas_call(
        backward_kernel,
        grid_spec=pltpu.PrefetchScalarGridSpec(
            num_scalar_prefetch=1,
            grid=(NI // JSTEP,),
            in_specs=[HERE] * 10,
            out_specs=[HERE] * 3,
            scratch_shapes=[
                pltpu.VMEM((ROWS, 256), jnp.float32),
                pltpu.VMEM((ROWS, DI), jnp.float32),
            ],
        ),
        out_shape=[
            pltpu.VMEM((NI + 16, 128), jnp.float32),
            pltpu.VMEM((NI + 16, 128), jnp.float32),
            pltpu.VMEM((BLOCKS, 2 * UNIT, DI), jnp.bfloat16),
        ],
        cost_estimate=pl.CostEstimate(
            flops=4 * NI * ROWS * 256 * DI, bytes_accessed=6 << 20, transcendentals=0
        ),
        compiler_params=pltpu.CompilerParams(vmem_limit_bytes=VMEM),
        name="index_backward",
    )(meta, *in_vmem(keys, logits, *target, ia, ib, wa, wb))


def gather_head(value):
    wide = jnp.broadcast_to(value[None], (8,) + value.shape)
    return lax.all_to_all(wide, ("yhi", "xh", "xp"), 0, 0, tiled=True)


def after(value, *others):
    return lax.optimization_barrier((value,) + others)[0]


def body(main_queries, latent_keys, index_queries, index_weights, index_keys, tile_order, offset):
    z, ylo, core = lax.axis_index("z"), lax.axis_index("ylo"), lax.axis_index("core")
    half = lax.axis_index("xp")
    quarter = lax.axis_index("yhi") * 2 + lax.axis_index("xh")

    rows = jnp.arange(TILE, dtype=jnp.int32)
    place = (offset + (tile_order[:, None] * TILE + rows[None, :])).reshape(1, 128)
    pa, wa = place.astype(jnp.float32), index_weights.T
    own = jnp.concatenate([index_keys, latent_keys], axis=1)
    own = lax.dynamic_slice_in_dim(own, half * HALF, HALF, 0)
    meta = jnp.stack([z, ylo, core, half, quarter]).astype(jnp.int32)
    own, meta = lax.optimization_barrier((own, meta))

    queries = main_queries.transpose(0, 2, 1)
    f1, b1 = shift(own, dz=1), shift(own, dz=7)
    queries_far = swap_core(queries)
    halves = after(queries, own)
    left, right = shift(halves[:4], dx=1), shift(halves[4:], dx=3)
    f1, b1 = lax.optimization_barrier((f1, b1))
    f2, b2 = shift(f1, dz=1), shift(b1, dz=7)
    f2, b2 = lax.optimization_barrier((f2, b2))
    f3, b3 = shift(f2, dz=1), shift(b2, dz=7)
    pb = swap_core(pa)
    ia = index_queries.transpose(1, 0, 2)
    f3, b3, left, right, ia, pb = lax.optimization_barrier((f3, b3, left, right, ia, pb))
    f4 = shift(f3, dz=1)
    left_far, right_far = swap_core(left), swap_core(right)
    y0, y1 = jnp.concatenate([own, f1, b1, f2]), jnp.concatenate([b2, f3, b3, f4])
    y0, y1 = shift(y0, dy=1), shift(y1, dy=3)
    ia, wa = lax.optimization_barrier((ia, wa, f4, left_far, right_far))[:2]
    ib, wb = swap_core(ia), swap_core(wa)

    sides = (queries, queries_far, left, left_far, right, right_far, pa, pb)
    exps, m0, l0, keys = score_call(meta, 0, [own, f1, b1, f2, b2, f3, b3, f4], [], *sides)
    exps, m1, l1, keys = score_call(meta, 1, [y0, y1], in_vmem(exps, keys), *sides)

    logits, ours, sent = forward_call(meta, keys, (m0, l0, m1, l1), ia, ib, pa, pb, wa, wb)
    here, up, down = pair_call(ours, swap_core(sent))
    up, down = shift(up, dx=1), shift(down, dx=3)
    sums = head_sum_call(meta, exps, m0, m1, here, up, down)
    group = (dict(dx=2), dict(dy=2), dict(dx=2, dy=2))
    target = [sums[0]] + [shift(part, **move) for part, move in zip(sums[1:], group)]

    mine, other, kg = backward_call(meta, keys, logits, target, ia, ib, wa, wb)
    rows_out = mine + swap_core(other)
    rows_high = lax.reduce_precision(rows_out, 8, 7)
    low = jnp.concatenate([jnp.zeros((NI + 8, 128), jnp.float32), (rows_out - rows_high)[NI : NI + 8]])
    tail = rows_high + low
    kg = lax.all_to_all(kg, ("z", "ylo"), 0, 0, tiled=True)
    kg = jnp.sum(kg.astype(jnp.float32), axis=0)
    last = gather_head(jnp.concatenate([kg, tail]).astype(jnp.bfloat16)).astype(jnp.float32)
    rows_sum = jnp.sum(last[:, 2 * UNIT :], axis=0)
    pieces = last[:, : 2 * UNIT].reshape(4, 2, 2 * UNIT, DI)
    main = pieces[:, :, :UNIT].transpose(1, 0, 2, 3).reshape(2, 4 * UNIT, DI)
    extra = jnp.sum(pieces[:, :, UNIT:], axis=0)
    key_grad = jnp.concatenate([main, extra], axis=1).reshape(160, DI)
    return rows_sum[NI] + rows_sum[NI + 8], rows_sum[:NI].T, key_grad


def solution(mesh):
    fine = Mesh(np.asarray(mesh.devices).reshape(2, 2, 2, 8, 2, 2), ALL)
    head, ctx = ("yhi", "xh", "xp"), ("z", "ylo", "core")
    in_specs = (
        P(head, ctx, None),
        P(ctx, None),
        P(ctx, None, None),
        P(ctx, None),
        P(ctx, None),
        P(ctx),
        P(),
    )
    out_specs = (P(ctx), P(ctx, None), P(ctx, None))
    return jax.shard_map(body, mesh=fine, in_specs=in_specs, out_specs=out_specs, check_vma=False)
```

```python
import math

import jax
import jax.numpy as jnp
import numpy as np
from jax import lax
from jax.experimental import pallas as pl
from jax.experimental.pallas import tpu as pltpu
from jax.sharding import Mesh
from jax.sharding import PartitionSpec as P

TILE = 32
DQ = 576
DI = 128
NI = 64
HALF = 80
UNIT = 16
BLOCKS = 16
ROWS = 320
SCORE2 = 192.0 ** (-0.5) * math.log2(math.e)
INDEX_SCALE = DI ** (-0.5)
ALL = ("yhi", "xh", "xp", "z", "ylo", "core")
NEG = -jnp.inf
VMEM = 12 << 20
HERE = pl.BlockSpec(memory_space=pltpu.VMEM)


def flat(x, y, z, c):
    return ((y // 2) * 4 + x) * 32 + (z * 2 + (y % 2)) * 2 + c


def shift(value, dx=0, dy=0, dz=0, flip=0):
    pairs = [
        (flat(x, y, z, c), flat((x + dx) % 4, (y + dy) % 4, (z + dz) % 8, c ^ flip))
        for x in range(4)
        for y in range(4)
        for z in range(8)
        for c in range(2)
    ]
    return lax.ppermute(value, ALL, pairs)


def swap_core(value):
    return shift(value, flip=1)


LOG2E = math.log2(math.e)


def in_vmem(*values):
    return [pltpu.with_memory_space_constraint(value, pltpu.VMEM) for value in values]


def slot_of(meta, i):
    k = i & 7
    reach = (k + 1) >> 1
    step = reach * (1 - 2 * (k & 1))
    return ((meta[0] + 8 + step) & 7) * 2 + (meta[1] ^ (i >> 3))


def place_of(pa, pb):
    return jnp.concatenate([pa[...], pb[...]], axis=1)


def merge(m0, l0, m1, l1, rate):
    top = jnp.maximum(m0, m1)
    return top, l0 * jnp.exp2((m0 - top) * rate) + l1 * jnp.exp2((m1 - top) * rate)


def swapped(value):
    return jnp.concatenate([value[:, 128:], value[:, :128]], axis=1)


HEADS = 16
CHUNK = 8 * HALF


def score_kernel(chunk, spans, meta, *refs):
    n = len(spans)
    blocks, refs = refs[:n], refs[n:]
    if chunk:
        _, ik_before, refs = refs[0], refs[1], refs[2:]
    qa, qb, na, nb, ma, mb, pa, pb = refs[:8]
    e_ref, m_ref, l_ref, ik_ref, keys, bias, raw, tops, sems = refs[8:]
    step = pl.program_id(0)
    cut = 320

    @pl.when(step == 0)
    def _():
        copies = []
        at = 0
        for i, (block, span) in enumerate(zip(blocks, spans)):
            copies.append(pltpu.make_async_copy(block, keys.at[at : at + span, :], sems.at[i]))
            copies[-1].start()
            at += span
        place = place_of(pa, pb)
        offsets = lax.broadcasted_iota(jnp.int32, (HALF, 256), 0).astype(jnp.float32)
        slots = [slot_of(meta, 8 * chunk + i) for i in range(8)]
        for i in range(8):
            base = ((slots[i] * 2 + meta[2]) * 160 + meta[3] * HALF).astype(jnp.float32)
            bias[i * HALF : (i + 1) * HALF, :] = jnp.where(offsets + base <= place, 0.0, NEG)
        tops[...] = jnp.zeros_like(tops)
        ik_ref[...] = ik_before[...] if chunk else jnp.zeros_like(ik_ref)
        for copy in copies:
            copy.wait()
        quarter = meta[4]
        for i in range(8):
            slot = slots[i]
            mine = pl.ds(pl.multiple_of(i * HALF + quarter * UNIT, UNIT), UNIT)
            ik_ref[pl.ds(pl.multiple_of(slot * UNIT, UNIT), UNIT), :] = keys[mine, 0:DI]

            @pl.when((slot & 3) == quarter)
            def _():
                extra = pl.multiple_of(256 + (slot >> 2) * UNIT, UNIT)
                ik_ref[pl.ds(extra, UNIT), :] = keys[i * HALF + 4 * UNIT : (i + 1) * HALF, 0:DI]

    def work(now, last):
        for k in range(2):
            own, left, right = (
                jnp.concatenate([a[at], b[at]], axis=1)
                for a, b, at in (
                    (qa, qb, 2 * jnp.minimum(step, 3) + k),
                    (na, nb, 2 * jnp.clip(step - 4, 0, 1) + k),
                    (ma, mb, 2 * jnp.clip(step - 6, 0, 1) + k),
                )
            )
            queries = jnp.where(step < 4, own, jnp.where(step < 6, left, right))
            top = jnp.max(tops[last, k], axis=0, keepdims=True)
            safe = jnp.where(top == NEG, 0.0, top)
            head = 2 * jnp.maximum(step - 1, 0) + k
            new = jnp.full((8, 256), NEG, jnp.float32)
            total = jnp.zeros((8, 256), jnp.float32)
            for t in range(0, CHUNK, cut):
                piece, rows = slice(t, t + cut), slice(chunk * CHUNK + t, chunk * CHUNK + t + cut)
                scores = jnp.dot(keys[piece, DI:], queries, preferred_element_type=jnp.float32)
                scores = scores + bias[piece, :]
                raw[now, k, piece, :] = scores
                new = jnp.maximum(new, jnp.max(scores.reshape(cut // 8, 8, 256), axis=0))
                exps = jnp.exp2((raw[last, k, piece, :] - safe) * SCORE2)
                e_ref[head, rows, :] = exps.astype(jnp.bfloat16)
                total = total + jnp.sum(exps.reshape(cut // 8, 8, 256), axis=0)
            tops[now, k] = new
            m_ref[pl.ds(head, 1), :] = top
            l_ref[pl.ds(head, 1), :] = jnp.sum(total, axis=0, keepdims=True)

    @pl.when(step % 2 == 0)
    def _():
        work(0, 1)

    @pl.when(step % 2 == 1)
    def _():
        work(1, 0)


def score_call(meta, chunk, blocks, before, qa, qb, na, nb, ma, mb, pa, pb):
    spans = [b.shape[0] for b in blocks]
    anywhere = pl.BlockSpec(memory_space=pl.ANY)
    return pl.pallas_call(
        lambda *refs: score_kernel(chunk, spans, *refs),
        grid_spec=pltpu.PrefetchScalarGridSpec(
            num_scalar_prefetch=1,
            grid=(HEADS // 2 + 1,),
            in_specs=[anywhere] * len(blocks)
            + [HERE] * (len(before) + 8),
            out_specs=[HERE] * 4,
            scratch_shapes=[
                pltpu.VMEM((CHUNK, DI + DQ), jnp.bfloat16),
                pltpu.VMEM((CHUNK, 256), jnp.float32),
                pltpu.VMEM((2, 2, CHUNK, 256), jnp.float32),
                pltpu.VMEM((2, 2, 8, 256), jnp.float32),
                pltpu.SemaphoreType.DMA((len(blocks),)),
            ],
        ),
        out_shape=[
            pltpu.VMEM((HEADS, 2 * CHUNK, 256), jnp.bfloat16),
            pltpu.VMEM((HEADS, 256), jnp.float32),
            pltpu.VMEM((HEADS, 256), jnp.float32),
            pltpu.VMEM((ROWS, DI), jnp.bfloat16),
        ],
        input_output_aliases={1 + len(blocks): 0} if chunk else {},
        cost_estimate=pl.CostEstimate(
            flops=4 * HEADS * CHUNK * 256 * DQ,
            bytes_accessed=HEADS * CHUNK * 512,
            transcendentals=HEADS * CHUNK * 256,
        ),
        compiler_params=pltpu.CompilerParams(vmem_limit_bytes=VMEM),
        name="scores",
    )(meta, *in_vmem(*blocks), *before, *in_vmem(qa, qb, na, nb, ma, mb, pa, pb))


def head_sum_kernel(meta, e_ref, m0, m1, here, up, down, o0, o1, o2, o3, total_ref, ratio):
    i = pl.program_id(0)

    @pl.when(i == 0)
    def _():
        def side(v):
            heads = [down[v, 4:8, :], up[v, 4:8, :], up[v, 0:4, :], down[v, 0:4, :]]
            return jnp.concatenate(heads, axis=0)

        top, total = merge(here[0, 0:16, :], here[1, 0:16, :], side(0), side(1), SCORE2)
        for c, m in enumerate((m0, m1)):
            ratio[c] = jnp.exp2((m[...] - top) * SCORE2) / total
        index = slice(HEADS, HEADS + 1)
        terms = []
        for left in merge(here[0, index, :], here[1, index, :], down[0, 8:9, :], down[1, 8:9, :], LOG2E):
            for _ in range(3):
                term = left.astype(jnp.bfloat16).astype(jnp.float32)
                terms.append(term)
                left = left - term
        packed = jnp.concatenate(terms + [jnp.zeros((10, 256), jnp.float32)], axis=0)
        for out in (o0, o1, o2, o3):
            out[ROWS:, :] = packed.astype(jnp.bfloat16)

    chunk = i // 8
    total = jnp.zeros((HALF, 256), jnp.float32)
    for h in range(HEADS):
        part = e_ref[h, pl.ds(pl.multiple_of(i * HALF, HALF), HALF), :]
        total = total + part.astype(jnp.float32) * ratio[chunk, h : h + 1, :]
    total_ref[...] = total
    slot = slot_of(meta, i)
    quarter = meta[4]
    at = pl.ds(pl.multiple_of(slot * UNIT, UNIT), UNIT)
    extra = pl.ds(pl.multiple_of(256 + (slot >> 2) * UNIT, UNIT), UNIT)
    for k, out in enumerate((o0, o1, o2, o3)):
        unit = pl.multiple_of((quarter ^ k) * UNIT, UNIT)
        out[at, :] = total_ref[pl.ds(unit, UNIT), :].astype(jnp.bfloat16)

        @pl.when((slot & 3) == (quarter ^ k))
        def _():
            out[extra, :] = total_ref[4 * UNIT :, :].astype(jnp.bfloat16)


def head_sum_call(meta, exps, *stats):
    return pl.pallas_call(
        head_sum_kernel,
        grid_spec=pltpu.PrefetchScalarGridSpec(
            num_scalar_prefetch=1,
            grid=(BLOCKS,),
            in_specs=[HERE] * (1 + len(stats)),
            out_specs=[HERE] * 4,
            scratch_shapes=[
                pltpu.VMEM((HALF, 256), jnp.float32),
                pltpu.VMEM((2, HEADS, 256), jnp.float32),
            ],
        ),
        out_shape=[pltpu.VMEM((ROWS + UNIT, 256), jnp.bfloat16)] * 4,
        cost_estimate=pl.CostEstimate(flops=0, bytes_accessed=11 << 20, transcendentals=0),
        compiler_params=pltpu.CompilerParams(vmem_limit_bytes=VMEM),
        name="head_sum",
    )(meta, *in_vmem(exps, *stats))


def key_places(meta):
    core, half, quarter = meta[2], meta[3], meta[4]
    rows = lax.broadcasted_iota(jnp.int32, (UNIT, 256), 0)
    out = []
    for u in range(16):
        out.append(rows + ((u // 2 * 4 + (u % 2) * 2 + core) * 160 + half * HALF + quarter * UNIT))
    for e in range(4):
        z, ylo = 2 * e + (quarter >> 1), quarter & 1
        out.append(rows + ((z * 4 + ylo * 2 + core) * 160 + half * HALF + 4 * UNIT))
    return out


def inner_of(keys, ia, ib, j):
    queries = jnp.concatenate([ia[j], ib[j]], axis=0)
    return lax.dot_general(
        keys[...], queries, (((1,), (1,)), ((), ())), preferred_element_type=jnp.float32
    ), queries


JSTEP = 32


def forward_kernel(meta, keys, m0, l0, m1, l1, ia, ib, pa, pb, wja, wjb, logits, here, sent):
    step = pl.program_id(0)

    @pl.when(step == 0)
    def _():
        logits[...] = jnp.zeros_like(logits)

    total = logits[...]
    for j in range(JSTEP):
        at = step * JSTEP + j
        inner, _ = inner_of(keys, ia, ib, at)
        weight = jnp.concatenate([wja[pl.ds(at, 1), :], wjb[pl.ds(at, 1), :]], axis=1)
        total = total + weight * jnp.maximum(inner, 0.0)
    logits[...] = total

    @pl.when(step == NI // JSTEP - 1)
    def _():
        place = place_of(pa, pb)
        places = key_places(meta)
        top = jnp.full((1, 256), NEG, jnp.float32)
        for u in range(20):
            cut = slice(u * UNIT, (u + 1) * UNIT)
            value = logits[cut, :] * INDEX_SCALE
            value = jnp.where(places[u].astype(jnp.float32) <= place, value, NEG)
            logits[cut, :] = value
            top = jnp.maximum(top, jnp.max(value, axis=0, keepdims=True))
        safe = jnp.where(top == NEG, 0.0, top)
        total = jnp.sum(jnp.exp(logits[...] - safe), axis=0, keepdims=True)
        tops, totals = merge(m0[...], l0[...], m1[...], l1[...], SCORE2)
        for v, (heads, index) in enumerate(((tops, top), (totals, total))):
            rows = jnp.concatenate([heads, index, jnp.zeros((7, 256), jnp.float32)], axis=0)
            here[v] = rows
            sent[v] = swapped(rows)


def pair_kernel(ours, theirs, here, up, down):
    index = slice(HEADS, HEADS + 1)
    heads = slice(0, HEADS)
    tops, totals = merge(ours[0, heads, :], ours[1, heads, :], theirs[0, heads, :], theirs[1, heads, :], SCORE2)
    top, total = merge(ours[0, index, :], ours[1, index, :], theirs[0, index, :], theirs[1, index, :], LOG2E)
    for v, (main, extra) in enumerate(((tops, top), (totals, total))):
        pad = jnp.zeros((7, 256), jnp.float32)
        here[v] = jnp.concatenate([main, extra, pad], axis=0)
        up[v] = jnp.concatenate([main[0:4], main[12:16]], axis=0)
        down[v] = jnp.concatenate([main[4:12], extra, pad], axis=0)


def pair_call(ours, theirs):
    return pl.pallas_call(
        pair_kernel,
        in_specs=[HERE] * 2,
        out_specs=[HERE] * 3,
        out_shape=[pltpu.VMEM((2, rows, 256), jnp.float32) for rows in (24, 8, 16)],
        compiler_params=pltpu.CompilerParams(vmem_limit_bytes=1 << 20),
        name="pair_statistics",
    )(*in_vmem(ours, theirs))


def forward_call(meta, keys, stats, ia, ib, pa, pb, wa, wb):
    return pl.pallas_call(
        forward_kernel,
        grid_spec=pltpu.PrefetchScalarGridSpec(
            num_scalar_prefetch=1,
            grid=(NI // JSTEP,),
            in_specs=[HERE] * 11,
            out_specs=[HERE] * 3,
        ),
        out_shape=[
            pltpu.VMEM((ROWS, 256), jnp.float32),
            pltpu.VMEM((2, 24, 256), jnp.float32),
            pltpu.VMEM((2, 24, 256), jnp.float32),
        ],
        cost_estimate=pl.CostEstimate(
            flops=2 * NI * ROWS * 256 * DI, bytes_accessed=5 << 20, transcendentals=0
        ),
        compiler_params=pltpu.CompilerParams(vmem_limit_bytes=VMEM),
        name="index_forward",
    )(meta, *in_vmem(keys, *stats, ia, ib, pa, pb, wa, wb))


def backward_kernel(meta, keys, logits, t0, t1, t2, t3, ia, ib, wja, wjb, rows_a, rows_b, kg, grad, acc):
    step = pl.program_id(0)

    @pl.when(step == 0)
    def _():
        parts = (t0, t1, t2, t3)

        def value(part, row):
            terms = part[ROWS:, :].astype(jnp.float32)
            return terms[row : row + 1] + terms[row + 1 : row + 2] + terms[row + 2 : row + 3]

        tops = [value(part, 0) for part in parts]
        top = tops[0]
        for other in tops[1:]:
            top = jnp.maximum(top, other)
        total = jnp.zeros((1, 256), jnp.float32)
        for part, other in zip(parts, tops):
            total = total + value(part, 3) * jnp.exp(other - top)
        norm = top + jnp.log(total)
        goal = jnp.zeros((ROWS, 256), jnp.float32)
        for part in parts:
            goal = goal + part[0:ROWS, :].astype(jnp.float32)
        goal = goal * (1.0 / 64.0)
        held = logits[...]
        seen = held != NEG
        logp = held - norm
        live = seen & (goal > 0)
        safe = jnp.where(goal > 0, goal, 1.0)
        part = jnp.where(live, goal * (jnp.log(safe) - logp), 0.0)
        part = jnp.sum(part, axis=0, keepdims=True)
        part = jnp.concatenate([part, jnp.zeros((15, 256), jnp.float32)], axis=0)
        rows_a[NI:, :] = part[:, :128]
        rows_b[NI:, :] = part[:, 128:]
        grad[...] = jnp.where(seen, jnp.exp(logp) - goal, 0.0) * INDEX_SCALE
        acc[...] = jnp.zeros_like(acc)

    total = acc[...]
    slope = grad[...]
    for j in range(JSTEP):
        at = step * JSTEP + j
        inner, queries = inner_of(keys, ia, ib, at)
        weight = jnp.concatenate([wja[pl.ds(at, 1), :], wjb[pl.ds(at, 1), :]], axis=1)
        open_slope = jnp.where(inner > 0, slope, 0.0)
        share = jnp.sum(open_slope * inner, axis=0, keepdims=True)
        rows_a[pl.ds(at, 1), :] = share[:, :128]
        rows_b[pl.ds(at, 1), :] = share[:, 128:]
        coeff = (open_slope * weight).astype(jnp.bfloat16)
        total = total + jnp.dot(coeff, queries, preferred_element_type=jnp.float32)
    acc[...] = total

    @pl.when(step == NI // JSTEP - 1)
    def _():
        quarter = meta[4]
        for b in range(BLOCKS):
            kg[b, 0:UNIT, :] = acc[b * UNIT : (b + 1) * UNIT, :].astype(jnp.bfloat16)
            at = 256 + (b // 4) * UNIT
            extra = jnp.where(quarter == b % 4, acc[at : at + UNIT, :], 0.0)
            kg[b, UNIT:, :] = extra.astype(jnp.bfloat16)


def backward_call(meta, keys, logits, target, ia, ib, wa, wb):
    return pl.pallas_call(
        backward_kernel,
        grid_spec=pltpu.PrefetchScalarGridSpec(
            num_scalar_prefetch=1,
            grid=(NI // JSTEP,),
            in_specs=[HERE] * 10,
            out_specs=[HERE] * 3,
            scratch_shapes=[
                pltpu.VMEM((ROWS, 256), jnp.float32),
                pltpu.VMEM((ROWS, DI), jnp.float32),
            ],
        ),
        out_shape=[
            pltpu.VMEM((NI + 16, 128), jnp.float32),
            pltpu.VMEM((NI + 16, 128), jnp.float32),
            pltpu.VMEM((BLOCKS, 2 * UNIT, DI), jnp.bfloat16),
        ],
        cost_estimate=pl.CostEstimate(
            flops=4 * NI * ROWS * 256 * DI, bytes_accessed=6 << 20, transcendentals=0
        ),
        compiler_params=pltpu.CompilerParams(vmem_limit_bytes=VMEM),
        name="index_backward",
    )(meta, *in_vmem(keys, logits, *target, ia, ib, wa, wb))


PART = 7 * UNIT


def finish_kernel(meta, p0, p1, p2, p3, div, weight, key, held):
    quarter = meta[4]
    for r, pair in enumerate((p0, p1, p2, p3)):
        held[r] = pair[...]
    x, yhi = (quarter & 1) * 2 + meta[3], quarter >> 1
    rows = jnp.zeros((PART - 2 * UNIT, 128), jnp.float32)
    rest = [jnp.zeros((UNIT, DI), jnp.float32)] * 2
    for y in range(2):
        for k in range(4):
            at = pl.ds(pl.multiple_of((yhi ^ y) * PART, UNIT), PART)
            part = held[(x - k) & 3, at, :].astype(jnp.float32)
            rows = rows + part[2 * UNIT :]
            half = k & 1
            first = half * HALF + (y * 2 + (k >> 1)) * UNIT
            key[first : first + UNIT, :] = part[0:UNIT]
            rest[half] = rest[half] + part[UNIT : 2 * UNIT]
    for half in range(2):
        key[half * HALF + 4 * UNIT : (half + 1) * HALF, :] = rest[half]
    weight[...] = rows[0:NI]
    div[...] = rows[NI : NI + 1] + rows[NI + 8 : NI + 9]


def finish_call(meta, *pairs):
    return pl.pallas_call(
        finish_kernel,
        grid_spec=pltpu.PrefetchScalarGridSpec(
            num_scalar_prefetch=1,
            grid=(1,),
            in_specs=[HERE] * 4,
            out_specs=[HERE] * 3,
            scratch_shapes=[pltpu.VMEM((4, 2 * PART, 128), jnp.bfloat16)],
        ),
        out_shape=[jax.ShapeDtypeStruct((rows, 128), jnp.float32) for rows in (1, NI, 2 * HALF)],
        compiler_params=pltpu.CompilerParams(vmem_limit_bytes=2 << 20),
        name="finish",
    )(meta, *in_vmem(*pairs))


def after(value, *others):
    return lax.optimization_barrier((value,) + others)[0]


def body(main_queries, latent_keys, index_queries, index_weights, index_keys, tile_order, offset):
    z, ylo, core = lax.axis_index("z"), lax.axis_index("ylo"), lax.axis_index("core")
    half = lax.axis_index("xp")
    quarter = lax.axis_index("yhi") * 2 + lax.axis_index("xh")

    rows = jnp.arange(TILE, dtype=jnp.int32)
    place = (offset + (tile_order[:, None] * TILE + rows[None, :])).reshape(1, 128)
    pa, wa = place.astype(jnp.float32), index_weights.T
    own = jnp.concatenate([index_keys, latent_keys], axis=1)
    own = lax.dynamic_slice_in_dim(own, half * HALF, HALF, 0)
    meta = jnp.stack([z, ylo, core, half, quarter]).astype(jnp.int32)
    own, meta = lax.optimization_barrier((own, meta))

    queries = main_queries.transpose(0, 2, 1)
    f1, b1 = shift(own, dz=1), shift(own, dz=7)
    queries_far = swap_core(queries)
    halves = after(queries, own)
    left, right = shift(halves[:4], dx=1), shift(halves[4:], dx=3)
    f1, b1 = lax.optimization_barrier((f1, b1))
    f2, b2 = shift(f1, dz=1), shift(b1, dz=7)
    f2, b2 = lax.optimization_barrier((f2, b2))
    f3, b3 = shift(f2, dz=1), shift(b2, dz=7)
    pb = swap_core(pa)
    ia = index_queries.transpose(1, 0, 2)
    f3, b3, left, right, ia, pb = lax.optimization_barrier((f3, b3, left, right, ia, pb))
    f4 = shift(f3, dz=1)
    left_far, right_far = swap_core(left), swap_core(right)
    y0, y1 = jnp.concatenate([own, f1, b1, f2]), jnp.concatenate([b2, f3, b3, f4])
    y0, y1 = shift(y0, dy=1), shift(y1, dy=3)
    ia, wa = lax.optimization_barrier((ia, wa, f4, left_far, right_far))[:2]
    ib, wb = swap_core(ia), swap_core(wa)

    sides = (queries, queries_far, left, left_far, right, right_far, pa, pb)
    exps, m0, l0, keys = score_call(meta, 0, [own, f1, b1, f2, b2, f3, b3, f4], [], *sides)
    exps, m1, l1, keys = score_call(meta, 1, [y0, y1], in_vmem(exps, keys), *sides)

    logits, ours, sent = forward_call(meta, keys, (m0, l0, m1, l1), ia, ib, pa, pb, wa, wb)
    here, up, down = pair_call(ours, swap_core(sent))
    up, down = shift(up, dx=1), shift(down, dx=3)
    sums = head_sum_call(meta, exps, m0, m1, here, up, down)
    group = (dict(dx=2), dict(dy=2), dict(dx=2, dy=2))
    target = [sums[0]] + [shift(part, **move) for part, move in zip(sums[1:], group)]

    mine, other, kg = backward_call(meta, keys, logits, target, ia, ib, wa, wb)
    rows_out = mine + swap_core(other)
    rows_high = lax.reduce_precision(rows_out, 8, 7)
    low = jnp.concatenate([jnp.zeros((NI + 8, 128), jnp.float32), (rows_out - rows_high)[NI : NI + 8]])
    tail = rows_high + low
    kg = lax.all_to_all(kg, ("z", "ylo"), 0, 0, tiled=True)
    kg = jnp.sum(kg.astype(jnp.float32), axis=0)
    part = jnp.concatenate([kg, tail]).astype(jnp.bfloat16)
    pair = jnp.concatenate([part, shift(part, dy=2)])
    div, weight, key_grad = finish_call(meta, pair, *(shift(pair, dx=dx) for dx in (1, 2, 3)))
    return div.reshape(128), weight.T, key_grad


def solution(mesh):
    fine = Mesh(np.asarray(mesh.devices).reshape(2, 2, 2, 8, 2, 2), ALL)
    head, ctx = ("yhi", "xh", "xp"), ("z", "ylo", "core")
    in_specs = (
        P(head, ctx, None),
        P(ctx, None),
        P(ctx, None, None),
        P(ctx, None),
        P(ctx, None),
        P(ctx),
        P(),
    )
    out_specs = (P(ctx), P(ctx, None), P(ctx, None))
    return jax.shard_map(body, mesh=fine, in_specs=in_specs, out_specs=out_specs, check_vma=False)
```

```python
import math

import jax
import jax.numpy as jnp
import numpy as np
from jax import lax
from jax.experimental import pallas as pl
from jax.experimental.pallas import tpu as pltpu
from jax.sharding import Mesh
from jax.sharding import PartitionSpec as P

TILE = 32
DQ = 576
DI = 128
NI = 64
HALF = 80
UNIT = 16
BLOCKS = 16
ROWS = 320
SCORE2 = 192.0 ** (-0.5) * math.log2(math.e)
INDEX_SCALE = DI ** (-0.5)
ALL = ("yhi", "xh", "xp", "z", "ylo", "core")
NEG = -jnp.inf
VMEM = 12 << 20
HERE = pl.BlockSpec(memory_space=pltpu.VMEM)


def flat(x, y, z, c):
    return ((y // 2) * 4 + x) * 32 + (z * 2 + (y % 2)) * 2 + c


def shift(value, dx=0, dy=0, dz=0, flip=0):
    pairs = [
        (flat(x, y, z, c), flat((x + dx) % 4, (y + dy) % 4, (z + dz) % 8, c ^ flip))
        for x in range(4)
        for y in range(4)
        for z in range(8)
        for c in range(2)
    ]
    return lax.ppermute(value, ALL, pairs)


def swap_core(value):
    return shift(value, flip=1)


LOG2E = math.log2(math.e)


def in_vmem(*values):
    return [pltpu.with_memory_space_constraint(value, pltpu.VMEM) for value in values]


def slot_of(meta, i):
    k = i & 7
    reach = (k + 1) >> 1
    step = reach * (1 - 2 * (k & 1))
    return ((meta[0] + 8 + step) & 7) * 2 + (meta[1] ^ (i >> 3))


def place_of(pa, pb):
    return jnp.concatenate([pa[...], pb[...]], axis=1)


def merge(m0, l0, m1, l1, rate):
    top = jnp.maximum(m0, m1)
    return top, l0 * jnp.exp2((m0 - top) * rate) + l1 * jnp.exp2((m1 - top) * rate)


def swapped(value):
    return jnp.concatenate([value[:, 128:], value[:, :128]], axis=1)


HEADS = 16
CHUNK = 8 * HALF


def score_kernel(chunk, spans, meta, *refs):
    n = len(spans)
    blocks, refs = refs[:n], refs[n:]
    if chunk:
        _, ik_before, refs = refs[0], refs[1], refs[2:]
    qa, qb, na, nb, ma, mb, pa, pb = refs[:8]
    e_ref, m_ref, l_ref, ik_ref, keys, bias, raw, tops, sems = refs[8:]
    step = pl.program_id(0)
    cut = 320

    @pl.when(step == 0)
    def _():
        copies = []
        at = 0
        for i, (block, span) in enumerate(zip(blocks, spans)):
            copies.append(pltpu.make_async_copy(block, keys.at[at : at + span, :], sems.at[i]))
            copies[-1].start()
            at += span
        place = place_of(pa, pb)
        offsets = lax.broadcasted_iota(jnp.int32, (HALF, 256), 0).astype(jnp.float32)
        slots = [slot_of(meta, 8 * chunk + i) for i in range(8)]
        for i in range(8):
            base = ((slots[i] * 2 + meta[2]) * 160 + meta[3] * HALF).astype(jnp.float32)
            bias[i * HALF : (i + 1) * HALF, :] = jnp.where(offsets + base <= place, 0.0, NEG)
        tops[...] = jnp.zeros_like(tops)
        ik_ref[...] = ik_before[...] if chunk else jnp.zeros_like(ik_ref)
        for copy in copies:
            copy.wait()
        quarter = meta[4]
        for i in range(8):
            slot = slots[i]
            mine = pl.ds(pl.multiple_of(i * HALF + quarter * UNIT, UNIT), UNIT)
            ik_ref[pl.ds(pl.multiple_of(slot * UNIT, UNIT), UNIT), :] = keys[mine, 0:DI]

            @pl.when((slot & 3) == quarter)
            def _():
                extra = pl.multiple_of(256 + (slot >> 2) * UNIT, UNIT)
                ik_ref[pl.ds(extra, UNIT), :] = keys[i * HALF + 4 * UNIT : (i + 1) * HALF, 0:DI]

    def work(now, last):
        for k in range(2):
            own, left, right = (
                jnp.concatenate([a[at], b[at]], axis=1)
                for a, b, at in (
                    (qa, qb, 2 * jnp.minimum(step, 3) + k),
                    (na, nb, 2 * jnp.clip(step - 4, 0, 1) + k),
                    (ma, mb, 2 * jnp.clip(step - 6, 0, 1) + k),
                )
            )
            queries = jnp.where(step < 4, own, jnp.where(step < 6, left, right))
            top = jnp.max(tops[last, k], axis=0, keepdims=True)
            safe = jnp.where(top == NEG, 0.0, top)
            head = 2 * jnp.maximum(step - 1, 0) + k
            new = jnp.full((8, 256), NEG, jnp.float32)
            total = jnp.zeros((8, 256), jnp.float32)
            for t in range(0, CHUNK, cut):
                piece, rows = slice(t, t + cut), slice(chunk * CHUNK + t, chunk * CHUNK + t + cut)
                scores = jnp.dot(keys[piece, DI:], queries, preferred_element_type=jnp.float32)
                scores = scores + bias[piece, :]
                raw[now, k, piece, :] = scores
                new = jnp.maximum(new, jnp.max(scores.reshape(cut // 8, 8, 256), axis=0))
                exps = jnp.exp2((raw[last, k, piece, :] - safe) * SCORE2)
                e_ref[head, rows, :] = exps.astype(jnp.bfloat16)
                total = total + jnp.sum(exps.reshape(cut // 8, 8, 256), axis=0)
            tops[now, k] = new
            m_ref[pl.ds(head, 1), :] = top
            l_ref[pl.ds(head, 1), :] = jnp.sum(total, axis=0, keepdims=True)

    @pl.when(step % 2 == 0)
    def _():
        work(0, 1)

    @pl.when(step % 2 == 1)
    def _():
        work(1, 0)


def score_call(meta, chunk, blocks, before, qa, qb, na, nb, ma, mb, pa, pb):
    spans = [b.shape[0] for b in blocks]
    anywhere = pl.BlockSpec(memory_space=pl.ANY)
    return pl.pallas_call(
        lambda *refs: score_kernel(chunk, spans, *refs),
        grid_spec=pltpu.PrefetchScalarGridSpec(
            num_scalar_prefetch=1,
            grid=(HEADS // 2 + 1,),
            in_specs=[anywhere] * len(blocks)
            + [HERE] * (len(before) + 8),
            out_specs=[HERE] * 4,
            scratch_shapes=[
                pltpu.VMEM((CHUNK, DI + DQ), jnp.bfloat16),
                pltpu.VMEM((CHUNK, 256), jnp.float32),
                pltpu.VMEM((2, 2, CHUNK, 256), jnp.float32),
                pltpu.VMEM((2, 2, 8, 256), jnp.float32),
                pltpu.SemaphoreType.DMA((len(blocks),)),
            ],
        ),
        out_shape=[
            pltpu.VMEM((HEADS, 2 * CHUNK, 256), jnp.bfloat16),
            pltpu.VMEM((HEADS, 256), jnp.float32),
            pltpu.VMEM((HEADS, 256), jnp.float32),
            pltpu.VMEM((ROWS, DI), jnp.bfloat16),
        ],
        input_output_aliases={1 + len(blocks): 0} if chunk else {},
        cost_estimate=pl.CostEstimate(
            flops=4 * HEADS * CHUNK * 256 * DQ,
            bytes_accessed=HEADS * CHUNK * 512,
            transcendentals=HEADS * CHUNK * 256,
        ),
        compiler_params=pltpu.CompilerParams(vmem_limit_bytes=VMEM),
        name="scores",
    )(meta, *in_vmem(*blocks), *before, *in_vmem(qa, qb, na, nb, ma, mb, pa, pb))


def head_sum_kernel(meta, e_ref, m0, m1, here, up, down, o0, o1, o2, o3, total_ref, ratio):
    i = pl.program_id(0)

    @pl.when(i == 0)
    def _():
        def side(v):
            heads = [down[v, 4:8, :], up[v, 4:8, :], up[v, 0:4, :], down[v, 0:4, :]]
            return jnp.concatenate(heads, axis=0)

        top, total = merge(here[0, 0:16, :], here[1, 0:16, :], side(0), side(1), SCORE2)
        for c, m in enumerate((m0, m1)):
            ratio[c] = jnp.exp2((m[...] - top) * SCORE2) / total
        index = slice(HEADS, HEADS + 1)
        terms = []
        for left in merge(here[0, index, :], here[1, index, :], down[0, 8:9, :], down[1, 8:9, :], LOG2E):
            for _ in range(3):
                term = left.astype(jnp.bfloat16).astype(jnp.float32)
                terms.append(term)
                left = left - term
        packed = jnp.concatenate(terms + [jnp.zeros((10, 256), jnp.float32)], axis=0)
        for out in (o0, o1, o2, o3):
            out[ROWS:, :] = packed.astype(jnp.bfloat16)

    chunk = i // 8
    total = jnp.zeros((HALF, 256), jnp.float32)
    for h in range(HEADS):
        part = e_ref[h, pl.ds(pl.multiple_of(i * HALF, HALF), HALF), :]
        total = total + part.astype(jnp.float32) * ratio[chunk, h : h + 1, :]
    total_ref[...] = total
    slot = slot_of(meta, i)
    quarter = meta[4]
    at = pl.ds(pl.multiple_of(slot * UNIT, UNIT), UNIT)
    extra = pl.ds(pl.multiple_of(256 + (slot >> 2) * UNIT, UNIT), UNIT)
    for k, out in enumerate((o0, o1, o2, o3)):
        unit = pl.multiple_of((quarter ^ k) * UNIT, UNIT)
        out[at, :] = total_ref[pl.ds(unit, UNIT), :].astype(jnp.bfloat16)

        @pl.when((slot & 3) == (quarter ^ k))
        def _():
            out[extra, :] = total_ref[4 * UNIT :, :].astype(jnp.bfloat16)


def head_sum_call(meta, exps, *stats):
    return pl.pallas_call(
        head_sum_kernel,
        grid_spec=pltpu.PrefetchScalarGridSpec(
            num_scalar_prefetch=1,
            grid=(BLOCKS,),
            in_specs=[HERE] * (1 + len(stats)),
            out_specs=[HERE] * 4,
            scratch_shapes=[
                pltpu.VMEM((HALF, 256), jnp.float32),
                pltpu.VMEM((2, HEADS, 256), jnp.float32),
            ],
        ),
        out_shape=[pltpu.VMEM((ROWS + UNIT, 256), jnp.bfloat16)] * 4,
        cost_estimate=pl.CostEstimate(flops=0, bytes_accessed=11 << 20, transcendentals=0),
        compiler_params=pltpu.CompilerParams(vmem_limit_bytes=VMEM),
        name="head_sum",
    )(meta, *in_vmem(exps, *stats))


def key_places(meta):
    core, half, quarter = meta[2], meta[3], meta[4]
    rows = lax.broadcasted_iota(jnp.int32, (UNIT, 256), 0)
    out = []
    for u in range(16):
        out.append(rows + ((u // 2 * 4 + (u % 2) * 2 + core) * 160 + half * HALF + quarter * UNIT))
    for e in range(4):
        z, ylo = 2 * e + (quarter >> 1), quarter & 1
        out.append(rows + ((z * 4 + ylo * 2 + core) * 160 + half * HALF + 4 * UNIT))
    return out


def inner_of(keys, ia, ib, j):
    queries = jnp.concatenate([ia[j], ib[j]], axis=0)
    return lax.dot_general(
        keys[...], queries, (((1,), (1,)), ((), ())), preferred_element_type=jnp.float32
    ), queries


JSTEP = 32


def forward_kernel(meta, keys, m0, l0, m1, l1, ia, ib, pa, pb, wja, wjb, logits, here, sent):
    step = pl.program_id(0)

    @pl.when(step == 0)
    def _():
        logits[...] = jnp.zeros_like(logits)

    total = logits[...]
    for j in range(JSTEP):
        at = step * JSTEP + j
        inner, _ = inner_of(keys, ia, ib, at)
        weight = jnp.concatenate([wja[pl.ds(at, 1), :], wjb[pl.ds(at, 1), :]], axis=1)
        total = total + weight * jnp.maximum(inner, 0.0)
    logits[...] = total

    @pl.when(step == NI // JSTEP - 1)
    def _():
        place = place_of(pa, pb)
        places = key_places(meta)
        top = jnp.full((1, 256), NEG, jnp.float32)
        for u in range(20):
            cut = slice(u * UNIT, (u + 1) * UNIT)
            value = logits[cut, :] * INDEX_SCALE
            value = jnp.where(places[u].astype(jnp.float32) <= place, value, NEG)
            logits[cut, :] = value
            top = jnp.maximum(top, jnp.max(value, axis=0, keepdims=True))
        safe = jnp.where(top == NEG, 0.0, top)
        total = jnp.sum(jnp.exp(logits[...] - safe), axis=0, keepdims=True)
        tops, totals = merge(m0[...], l0[...], m1[...], l1[...], SCORE2)
        for v, (heads, index) in enumerate(((tops, top), (totals, total))):
            rows = jnp.concatenate([heads, index, jnp.zeros((7, 256), jnp.float32)], axis=0)
            here[v] = rows
            sent[v] = swapped(rows)


def pair_kernel(ours, theirs, here, up, down):
    index = slice(HEADS, HEADS + 1)
    heads = slice(0, HEADS)
    tops, totals = merge(ours[0, heads, :], ours[1, heads, :], theirs[0, heads, :], theirs[1, heads, :], SCORE2)
    top, total = merge(ours[0, index, :], ours[1, index, :], theirs[0, index, :], theirs[1, index, :], LOG2E)
    for v, (main, extra) in enumerate(((tops, top), (totals, total))):
        pad = jnp.zeros((7, 256), jnp.float32)
        here[v] = jnp.concatenate([main, extra, pad], axis=0)
        up[v] = jnp.concatenate([main[0:4], main[12:16]], axis=0)
        down[v] = jnp.concatenate([main[4:12], extra, pad], axis=0)


def pair_call(ours, theirs):
    return pl.pallas_call(
        pair_kernel,
        in_specs=[HERE] * 2,
        out_specs=[HERE] * 3,
        out_shape=[pltpu.VMEM((2, rows, 256), jnp.float32) for rows in (24, 8, 16)],
        compiler_params=pltpu.CompilerParams(vmem_limit_bytes=1 << 20),
        name="pair_statistics",
    )(*in_vmem(ours, theirs))


def forward_call(meta, keys, stats, ia, ib, pa, pb, wa, wb):
    return pl.pallas_call(
        forward_kernel,
        grid_spec=pltpu.PrefetchScalarGridSpec(
            num_scalar_prefetch=1,
            grid=(NI // JSTEP,),
            in_specs=[HERE] * 11,
            out_specs=[HERE] * 3,
        ),
        out_shape=[
            pltpu.VMEM((ROWS, 256), jnp.float32),
            pltpu.VMEM((2, 24, 256), jnp.float32),
            pltpu.VMEM((2, 24, 256), jnp.float32),
        ],
        cost_estimate=pl.CostEstimate(
            flops=2 * NI * ROWS * 256 * DI, bytes_accessed=5 << 20, transcendentals=0
        ),
        compiler_params=pltpu.CompilerParams(vmem_limit_bytes=VMEM),
        name="index_forward",
    )(meta, *in_vmem(keys, *stats, ia, ib, pa, pb, wa, wb))


def backward_kernel(meta, keys, logits, t0, t1, t2, t3, ia, ib, wja, wjb, rows_a, rows_b, kg, grad, acc):
    step = pl.program_id(0)

    @pl.when(step == 0)
    def _():
        parts = (t0, t1, t2, t3)

        def value(part, row):
            terms = part[ROWS:, :].astype(jnp.float32)
            return terms[row : row + 1] + terms[row + 1 : row + 2] + terms[row + 2 : row + 3]

        tops = [value(part, 0) for part in parts]
        top = tops[0]
        for other in tops[1:]:
            top = jnp.maximum(top, other)
        total = jnp.zeros((1, 256), jnp.float32)
        for part, other in zip(parts, tops):
            total = total + value(part, 3) * jnp.exp(other - top)
        norm = top + jnp.log(total)
        goal = jnp.zeros((ROWS, 256), jnp.float32)
        for part in parts:
            goal = goal + part[0:ROWS, :].astype(jnp.float32)
        goal = goal * (1.0 / 64.0)
        held = logits[...]
        seen = held != NEG
        logp = held - norm
        live = seen & (goal > 0)
        safe = jnp.where(goal > 0, goal, 1.0)
        part = jnp.where(live, goal * (jnp.log(safe) - logp), 0.0)
        part = jnp.sum(part, axis=0, keepdims=True)
        part = jnp.concatenate([part, jnp.zeros((15, 256), jnp.float32)], axis=0)
        rows_a[NI:, :] = part[:, :128]
        rows_b[NI:, :] = part[:, 128:]
        grad[...] = jnp.where(seen, jnp.exp(logp) - goal, 0.0) * INDEX_SCALE
        acc[...] = jnp.zeros_like(acc)

    total = acc[...]
    slope = grad[...]
    for j in range(JSTEP):
        at = step * JSTEP + j
        inner, queries = inner_of(keys, ia, ib, at)
        weight = jnp.concatenate([wja[pl.ds(at, 1), :], wjb[pl.ds(at, 1), :]], axis=1)
        open_slope = jnp.where(inner > 0, slope, 0.0)
        share = jnp.sum(open_slope * inner, axis=0, keepdims=True)
        rows_a[pl.ds(at, 1), :] = share[:, :128]
        rows_b[pl.ds(at, 1), :] = share[:, 128:]
        coeff = (open_slope * weight).astype(jnp.bfloat16)
        total = total + jnp.dot(coeff, queries, preferred_element_type=jnp.float32)
    acc[...] = total

    @pl.when(step == NI // JSTEP - 1)
    def _():
        quarter = meta[4]
        for b in range(BLOCKS):
            kg[b, 0:UNIT, :] = acc[b * UNIT : (b + 1) * UNIT, :].astype(jnp.bfloat16)
            at = 256 + (b // 4) * UNIT
            extra = jnp.where(quarter == b % 4, acc[at : at + UNIT, :], 0.0)
            kg[b, UNIT:, :] = extra.astype(jnp.bfloat16)


def backward_call(meta, keys, logits, target, ia, ib, wa, wb):
    return pl.pallas_call(
        backward_kernel,
        grid_spec=pltpu.PrefetchScalarGridSpec(
            num_scalar_prefetch=1,
            grid=(NI // JSTEP,),
            in_specs=[HERE] * 10,
            out_specs=[HERE] * 3,
            scratch_shapes=[
                pltpu.VMEM((ROWS, 256), jnp.float32),
                pltpu.VMEM((ROWS, DI), jnp.float32),
            ],
        ),
        out_shape=[
            pltpu.VMEM((NI + 16, 128), jnp.float32),
            pltpu.VMEM((NI + 16, 128), jnp.float32),
            pltpu.VMEM((BLOCKS, 2 * UNIT, DI), jnp.bfloat16),
        ],
        cost_estimate=pl.CostEstimate(
            flops=4 * NI * ROWS * 256 * DI, bytes_accessed=6 << 20, transcendentals=0
        ),
        compiler_params=pltpu.CompilerParams(vmem_limit_bytes=VMEM),
        name="index_backward",
    )(meta, *in_vmem(keys, logits, *target, ia, ib, wa, wb))


PART = 7 * UNIT


def finish_kernel(meta, p0, p1, p2, p3, div, weight, key, held):
    quarter = meta[4]
    for r, pair in enumerate((p0, p1, p2, p3)):
        held[r] = pair[...]
    x, yhi = (quarter & 1) * 2 + meta[3], quarter >> 1
    rows = jnp.zeros((PART - 2 * UNIT, 128), jnp.float32)
    rest = [jnp.zeros((UNIT, DI), jnp.float32)] * 2
    for y in range(2):
        for k in range(4):
            at = pl.ds(pl.multiple_of((yhi ^ y) * PART, UNIT), PART)
            part = held[(x - k) & 3, at, :].astype(jnp.float32)
            rows = rows + part[2 * UNIT :]
            half = k & 1
            first = half * HALF + (y * 2 + (k >> 1)) * UNIT
            key[first : first + UNIT, :] = part[0:UNIT]
            rest[half] = rest[half] + part[UNIT : 2 * UNIT]
    for half in range(2):
        key[half * HALF + 4 * UNIT : (half + 1) * HALF, :] = rest[half]
    weight[...] = rows[0:NI]
    div[...] = rows[NI : NI + 1] + rows[NI + 8 : NI + 9]


def finish_call(meta, *pairs):
    return pl.pallas_call(
        finish_kernel,
        grid_spec=pltpu.PrefetchScalarGridSpec(
            num_scalar_prefetch=1,
            grid=(1,),
            in_specs=[HERE] * 4,
            out_specs=[HERE] * 3,
            scratch_shapes=[pltpu.VMEM((4, 2 * PART, 128), jnp.bfloat16)],
        ),
        out_shape=[jax.ShapeDtypeStruct((rows, 128), jnp.float32) for rows in (1, NI, 2 * HALF)],
        compiler_params=pltpu.CompilerParams(vmem_limit_bytes=2 << 20),
        name="finish",
    )(meta, *in_vmem(*pairs))


def after(value, *others):
    return lax.optimization_barrier((value,) + others)[0]


def body(main_queries, latent_keys, index_queries, index_weights, index_keys, tile_order, offset):
    z, ylo, core = lax.axis_index("z"), lax.axis_index("ylo"), lax.axis_index("core")
    half = lax.axis_index("xp")
    quarter = lax.axis_index("yhi") * 2 + lax.axis_index("xh")

    rows = jnp.arange(TILE, dtype=jnp.int32)
    place = (offset + (tile_order[:, None] * TILE + rows[None, :])).reshape(1, 128)
    pa, wa = place.astype(jnp.float32), index_weights.T
    own = jnp.concatenate([index_keys, latent_keys], axis=1)
    own = lax.dynamic_slice_in_dim(own, half * HALF, HALF, 0)
    meta = jnp.stack([z, ylo, core, half, quarter]).astype(jnp.int32)
    own, meta = lax.optimization_barrier((own, meta))

    queries = main_queries.transpose(0, 2, 1)
    f1, b1 = shift(own, dz=1), shift(own, dz=7)
    queries_far = swap_core(queries)
    f1, b1, left, right = lax.optimization_barrier((f1, b1, queries[:4], queries[4:]))
    left, right = shift(left, dx=1), shift(right, dx=3)
    f2, b2 = shift(f1, dz=1), shift(b1, dz=7)
    f2, b2 = lax.optimization_barrier((f2, b2))
    f3, b3 = shift(f2, dz=1), shift(b2, dz=7)
    pb = swap_core(pa)
    ia = index_queries.transpose(1, 0, 2)
    f3, b3, left, right, ia, pb = lax.optimization_barrier((f3, b3, left, right, ia, pb))
    f4 = shift(f3, dz=1)
    left_far, right_far = swap_core(left), swap_core(right)
    y0, y1 = jnp.concatenate([own, f1, b1, f2]), jnp.concatenate([b2, f3, b3, f4])
    y0, y1 = shift(y0, dy=1), shift(y1, dy=3)
    ia, wa = lax.optimization_barrier((ia, wa, f4, left_far, right_far))[:2]
    ib, wb = swap_core(ia), swap_core(wa)

    sides = (queries, queries_far, left, left_far, right, right_far, pa, pb)
    exps, m0, l0, keys = score_call(meta, 0, [own, f1, b1, f2, b2, f3, b3, f4], [], *sides)
    exps, m1, l1, keys = score_call(meta, 1, [y0, y1], in_vmem(exps, keys), *sides)

    logits, ours, sent = forward_call(meta, keys, (m0, l0, m1, l1), ia, ib, pa, pb, wa, wb)
    here, up, down = pair_call(ours, swap_core(sent))
    up, down = shift(up, dx=1), shift(down, dx=3)
    sums = head_sum_call(meta, exps, m0, m1, here, up, down)
    group = (dict(dx=2), dict(dy=2), dict(dx=2, dy=2))
    target = [sums[0]] + [shift(part, **move) for part, move in zip(sums[1:], group)]

    mine, other, kg = backward_call(meta, keys, logits, target, ia, ib, wa, wb)
    rows_out = mine + swap_core(other)
    rows_high = lax.reduce_precision(rows_out, 8, 7)
    low = jnp.concatenate([jnp.zeros((NI + 8, 128), jnp.float32), (rows_out - rows_high)[NI : NI + 8]])
    tail = rows_high + low
    kg = lax.all_to_all(kg, ("z", "ylo"), 0, 0, tiled=True)
    kg = jnp.sum(kg.astype(jnp.float32), axis=0)
    part = jnp.concatenate([kg, tail]).astype(jnp.bfloat16)
    pair = jnp.concatenate([part, shift(part, dy=2)])
    div, weight, key_grad = finish_call(meta, pair, *(shift(pair, dx=dx) for dx in (1, 2, 3)))
    return div.reshape(128), weight.T, key_grad


def solution(mesh):
    fine = Mesh(np.asarray(mesh.devices).reshape(2, 2, 2, 8, 2, 2), ALL)
    head, ctx = ("yhi", "xh", "xp"), ("z", "ylo", "core")
    in_specs = (
        P(head, ctx, None),
        P(ctx, None),
        P(ctx, None, None),
        P(ctx, None),
        P(ctx, None),
        P(ctx),
        P(),
    )
    out_specs = (P(ctx), P(ctx, None), P(ctx, None))
    return jax.shard_map(body, mesh=fine, in_specs=in_specs, out_specs=out_specs, check_vma=False)
```

```python
import math

import jax
import jax.numpy as jnp
import numpy as np
from jax import lax
from jax.experimental import pallas as pl
from jax.experimental.pallas import tpu as pltpu
from jax.sharding import Mesh
from jax.sharding import PartitionSpec as P

TILE = 32
DQ = 576
DI = 128
NI = 64
HALF = 80
UNIT = 16
BLOCKS = 16
ROWS = 320
SCORE2 = 192.0 ** (-0.5) * math.log2(math.e)
INDEX_SCALE = DI ** (-0.5)
ALL = ("yhi", "xh", "xp", "z", "ylo", "core")
NEG = -jnp.inf
VMEM = 12 << 20
HERE = pl.BlockSpec(memory_space=pltpu.VMEM)


def flat(x, y, z, c):
    return ((y // 2) * 4 + x) * 32 + (z * 2 + (y % 2)) * 2 + c


def shift(value, dx=0, dy=0, dz=0, flip=0):
    pairs = [
        (flat(x, y, z, c), flat((x + dx) % 4, (y + dy) % 4, (z + dz) % 8, c ^ flip))
        for x in range(4)
        for y in range(4)
        for z in range(8)
        for c in range(2)
    ]
    return lax.ppermute(value, ALL, pairs)


def swap_core(value):
    return shift(value, flip=1)


LOG2E = math.log2(math.e)


def in_vmem(*values):
    return [pltpu.with_memory_space_constraint(value, pltpu.VMEM) for value in values]


def slot_of(meta, i):
    k = i & 7
    reach = (k + 1) >> 1
    step = reach * (1 - 2 * (k & 1))
    return ((meta[0] + 8 + step) & 7) * 2 + (meta[1] ^ (i >> 3))


def place_of(pa, pb):
    return jnp.concatenate([pa[...], pb[...]], axis=1)


def merge(m0, l0, m1, l1, rate):
    top = jnp.maximum(m0, m1)
    return top, l0 * jnp.exp2((m0 - top) * rate) + l1 * jnp.exp2((m1 - top) * rate)


def swapped(value):
    return jnp.concatenate([value[:, 128:], value[:, :128]], axis=1)


HEADS = 16
CHUNK = 8 * HALF


def score_kernel(chunk, spans, meta, *refs):
    n = len(spans)
    blocks, refs = refs[:n], refs[n:]
    if chunk:
        _, ik_before, refs = refs[0], refs[1], refs[2:]
    qa, qb, na, nb, ma, mb, pa, pb = refs[:8]
    e_ref, m_ref, l_ref, ik_ref, keys, bias, raw, tops, sems = refs[8:]
    step = pl.program_id(0)
    cut = 320

    @pl.when(step == 0)
    def _():
        copies = []
        at = 0
        for i, (block, span) in enumerate(zip(blocks, spans)):
            copies.append(pltpu.make_async_copy(block, keys.at[at : at + span, :], sems.at[i]))
            copies[-1].start()
            at += span
        place = place_of(pa, pb)
        offsets = lax.broadcasted_iota(jnp.int32, (HALF, 256), 0).astype(jnp.float32)
        slots = [slot_of(meta, 8 * chunk + i) for i in range(8)]
        for i in range(8):
            base = ((slots[i] * 2 + meta[2]) * 160 + meta[3] * HALF).astype(jnp.float32)
            bias[i * HALF : (i + 1) * HALF, :] = jnp.where(offsets + base <= place, 0.0, NEG)
        tops[...] = jnp.zeros_like(tops)
        ik_ref[...] = ik_before[...] if chunk else jnp.zeros_like(ik_ref)
        for copy in copies:
            copy.wait()
        quarter = meta[4]
        for i in range(8):
            slot = slots[i]
            mine = pl.ds(pl.multiple_of(i * HALF + quarter * UNIT, UNIT), UNIT)
            ik_ref[pl.ds(pl.multiple_of(slot * UNIT, UNIT), UNIT), :] = keys[mine, 0:DI]

            @pl.when((slot & 3) == quarter)
            def _():
                extra = pl.multiple_of(256 + (slot >> 2) * UNIT, UNIT)
                ik_ref[pl.ds(extra, UNIT), :] = keys[i * HALF + 4 * UNIT : (i + 1) * HALF, 0:DI]

    def work(now, last):
        for k in range(2):
            own, left, right = (
                jnp.concatenate([a[at], b[at]], axis=1)
                for a, b, at in (
                    (qa, qb, 2 * jnp.minimum(step, 3) + k),
                    (na, nb, 2 * jnp.clip(step - 4, 0, 1) + k),
                    (ma, mb, 2 * jnp.clip(step - 6, 0, 1) + k),
                )
            )
            queries = jnp.where(step < 4, own, jnp.where(step < 6, left, right))
            top = jnp.max(tops[last, k], axis=0, keepdims=True)
            safe = jnp.where(top == NEG, 0.0, top)
            head = 2 * jnp.maximum(step - 1, 0) + k
            new = jnp.full((8, 256), NEG, jnp.float32)
            total = jnp.zeros((8, 256), jnp.float32)
            for t in range(0, CHUNK, cut):
                piece, rows = slice(t, t + cut), slice(chunk * CHUNK + t, chunk * CHUNK + t + cut)
                scores = jnp.dot(keys[piece, DI:], queries, preferred_element_type=jnp.float32)
                scores = scores + bias[piece, :]
                raw[now, k, piece, :] = scores
                new = jnp.maximum(new, jnp.max(scores.reshape(cut // 8, 8, 256), axis=0))
                exps = jnp.exp2((raw[last, k, piece, :] - safe) * SCORE2)
                e_ref[head, rows, :] = exps.astype(jnp.bfloat16)
                total = total + jnp.sum(exps.reshape(cut // 8, 8, 256), axis=0)
            tops[now, k] = new
            m_ref[pl.ds(head, 1), :] = top
            l_ref[pl.ds(head, 1), :] = jnp.sum(total, axis=0, keepdims=True)

    @pl.when(step % 2 == 0)
    def _():
        work(0, 1)

    @pl.when(step % 2 == 1)
    def _():
        work(1, 0)


def score_call(meta, chunk, blocks, before, qa, qb, na, nb, ma, mb, pa, pb):
    spans = [b.shape[0] for b in blocks]
    anywhere = pl.BlockSpec(memory_space=pl.ANY)
    return pl.pallas_call(
        lambda *refs: score_kernel(chunk, spans, *refs),
        grid_spec=pltpu.PrefetchScalarGridSpec(
            num_scalar_prefetch=1,
            grid=(HEADS // 2 + 1,),
            in_specs=[anywhere] * len(blocks)
            + [HERE] * (len(before) + 8),
            out_specs=[HERE] * 4,
            scratch_shapes=[
                pltpu.VMEM((CHUNK, DI + DQ), jnp.bfloat16),
                pltpu.VMEM((CHUNK, 256), jnp.float32),
                pltpu.VMEM((2, 2, CHUNK, 256), jnp.float32),
                pltpu.VMEM((2, 2, 8, 256), jnp.float32),
                pltpu.SemaphoreType.DMA((len(blocks),)),
            ],
        ),
        out_shape=[
            pltpu.VMEM((HEADS, 2 * CHUNK, 256), jnp.bfloat16),
            pltpu.VMEM((HEADS, 256), jnp.float32),
            pltpu.VMEM((HEADS, 256), jnp.float32),
            pltpu.VMEM((ROWS, DI), jnp.bfloat16),
        ],
        input_output_aliases={1 + len(blocks): 0} if chunk else {},
        cost_estimate=pl.CostEstimate(
            flops=4 * HEADS * CHUNK * 256 * DQ,
            bytes_accessed=HEADS * CHUNK * 512,
            transcendentals=HEADS * CHUNK * 256,
        ),
        compiler_params=pltpu.CompilerParams(vmem_limit_bytes=VMEM),
        name="scores",
    )(meta, *in_vmem(*blocks), *before, *in_vmem(qa, qb, na, nb, ma, mb, pa, pb))


def head_sum_kernel(meta, e_ref, m0, m1, here, up, down, o0, o1, o2, o3, total_ref, ratio):
    i = pl.program_id(0)

    @pl.when(i == 0)
    def _():
        def side(v):
            heads = [down[v, 4:8, :], up[v, 4:8, :], up[v, 0:4, :], down[v, 0:4, :]]
            return jnp.concatenate(heads, axis=0)

        top, total = merge(here[0, 0:16, :], here[1, 0:16, :], side(0), side(1), SCORE2)
        for c, m in enumerate((m0, m1)):
            ratio[c] = jnp.exp2((m[...] - top) * SCORE2) / total
        index = slice(HEADS, HEADS + 1)
        terms = []
        for left in merge(here[0, index, :], here[1, index, :], down[0, 8:9, :], down[1, 8:9, :], LOG2E):
            for _ in range(3):
                term = left.astype(jnp.bfloat16).astype(jnp.float32)
                terms.append(term)
                left = left - term
        packed = jnp.concatenate(terms + [jnp.zeros((10, 256), jnp.float32)], axis=0)
        for out in (o0, o1, o2, o3):
            out[ROWS:, :] = packed.astype(jnp.bfloat16)

    chunk = i // 8
    total = jnp.zeros((HALF, 256), jnp.float32)
    for h in range(HEADS):
        part = e_ref[h, pl.ds(pl.multiple_of(i * HALF, HALF), HALF), :]
        total = total + part.astype(jnp.float32) * ratio[chunk, h : h + 1, :]
    total_ref[...] = total
    slot = slot_of(meta, i)
    quarter = meta[4]
    at = pl.ds(pl.multiple_of(slot * UNIT, UNIT), UNIT)
    extra = pl.ds(pl.multiple_of(256 + (slot >> 2) * UNIT, UNIT), UNIT)
    for k, out in enumerate((o0, o1, o2, o3)):
        unit = pl.multiple_of((quarter ^ k) * UNIT, UNIT)
        out[at, :] = total_ref[pl.ds(unit, UNIT), :].astype(jnp.bfloat16)

        @pl.when((slot & 3) == (quarter ^ k))
        def _():
            out[extra, :] = total_ref[4 * UNIT :, :].astype(jnp.bfloat16)


def head_sum_call(meta, exps, *stats):
    return pl.pallas_call(
        head_sum_kernel,
        grid_spec=pltpu.PrefetchScalarGridSpec(
            num_scalar_prefetch=1,
            grid=(BLOCKS,),
            in_specs=[HERE] * (1 + len(stats)),
            out_specs=[HERE] * 4,
            scratch_shapes=[
                pltpu.VMEM((HALF, 256), jnp.float32),
                pltpu.VMEM((2, HEADS, 256), jnp.float32),
            ],
        ),
        out_shape=[pltpu.VMEM((ROWS + UNIT, 256), jnp.bfloat16)] * 4,
        cost_estimate=pl.CostEstimate(flops=0, bytes_accessed=11 << 20, transcendentals=0),
        compiler_params=pltpu.CompilerParams(vmem_limit_bytes=VMEM),
        name="head_sum",
    )(meta, *in_vmem(exps, *stats))


def key_places(meta):
    core, half, quarter = meta[2], meta[3], meta[4]
    rows = lax.broadcasted_iota(jnp.int32, (UNIT, 256), 0)
    out = []
    for u in range(16):
        out.append(rows + ((u // 2 * 4 + (u % 2) * 2 + core) * 160 + half * HALF + quarter * UNIT))
    for e in range(4):
        z, ylo = 2 * e + (quarter >> 1), quarter & 1
        out.append(rows + ((z * 4 + ylo * 2 + core) * 160 + half * HALF + 4 * UNIT))
    return out


def inner_of(keys, ia, ib, j):
    queries = jnp.concatenate([ia[j], ib[j]], axis=0)
    return lax.dot_general(
        keys[...], queries, (((1,), (1,)), ((), ())), preferred_element_type=jnp.float32
    ), queries


JSTEP = 32


def forward_kernel(meta, keys, m0, l0, m1, l1, ia, ib, pa, pb, wja, wjb, logits, here, sent):
    step = pl.program_id(0)

    @pl.when(step == 0)
    def _():
        logits[...] = jnp.zeros_like(logits)

    total = logits[...]
    for j in range(JSTEP):
        at = step * JSTEP + j
        inner, _ = inner_of(keys, ia, ib, at)
        weight = jnp.concatenate([wja[pl.ds(at, 1), :], wjb[pl.ds(at, 1), :]], axis=1)
        total = total + weight * jnp.maximum(inner, 0.0)
    logits[...] = total

    @pl.when(step == NI // JSTEP - 1)
    def _():
        place = place_of(pa, pb)
        places = key_places(meta)
        top = jnp.full((1, 256), NEG, jnp.float32)
        for u in range(20):
            cut = slice(u * UNIT, (u + 1) * UNIT)
            value = logits[cut, :] * INDEX_SCALE
            value = jnp.where(places[u].astype(jnp.float32) <= place, value, NEG)
            logits[cut, :] = value
            top = jnp.maximum(top, jnp.max(value, axis=0, keepdims=True))
        safe = jnp.where(top == NEG, 0.0, top)
        total = jnp.sum(jnp.exp(logits[...] - safe), axis=0, keepdims=True)
        tops, totals = merge(m0[...], l0[...], m1[...], l1[...], SCORE2)
        for v, (heads, index) in enumerate(((tops, top), (totals, total))):
            rows = jnp.concatenate([heads, index, jnp.zeros((7, 256), jnp.float32)], axis=0)
            here[v] = rows
            sent[v] = swapped(rows)


def pair_kernel(ours, theirs, here, up, down):
    index = slice(HEADS, HEADS + 1)
    heads = slice(0, HEADS)
    tops, totals = merge(ours[0, heads, :], ours[1, heads, :], theirs[0, heads, :], theirs[1, heads, :], SCORE2)
    top, total = merge(ours[0, index, :], ours[1, index, :], theirs[0, index, :], theirs[1, index, :], LOG2E)
    for v, (main, extra) in enumerate(((tops, top), (totals, total))):
        pad = jnp.zeros((7, 256), jnp.float32)
        here[v] = jnp.concatenate([main, extra, pad], axis=0)
        up[v] = jnp.concatenate([main[0:4], main[12:16]], axis=0)
        down[v] = jnp.concatenate([main[4:12], extra, pad], axis=0)


def pair_call(ours, theirs):
    return pl.pallas_call(
        pair_kernel,
        in_specs=[HERE] * 2,
        out_specs=[HERE] * 3,
        out_shape=[pltpu.VMEM((2, rows, 256), jnp.float32) for rows in (24, 8, 16)],
        compiler_params=pltpu.CompilerParams(vmem_limit_bytes=1 << 20),
        name="pair_statistics",
    )(*in_vmem(ours, theirs))


def forward_call(meta, keys, stats, ia, ib, pa, pb, wa, wb):
    return pl.pallas_call(
        forward_kernel,
        grid_spec=pltpu.PrefetchScalarGridSpec(
            num_scalar_prefetch=1,
            grid=(NI // JSTEP,),
            in_specs=[HERE] * 11,
            out_specs=[HERE] * 3,
        ),
        out_shape=[
            pltpu.VMEM((ROWS, 256), jnp.float32),
            pltpu.VMEM((2, 24, 256), jnp.float32),
            pltpu.VMEM((2, 24, 256), jnp.float32),
        ],
        cost_estimate=pl.CostEstimate(
            flops=2 * NI * ROWS * 256 * DI, bytes_accessed=5 << 20, transcendentals=0
        ),
        compiler_params=pltpu.CompilerParams(vmem_limit_bytes=VMEM),
        name="index_forward",
    )(meta, *in_vmem(keys, *stats, ia, ib, pa, pb, wa, wb))


def backward_kernel(meta, keys, logits, t0, t1, t2, t3, ia, ib, wja, wjb, rows_a, rows_b, kg, grad, acc):
    step = pl.program_id(0)

    @pl.when(step == 0)
    def _():
        parts = (t0, t1, t2, t3)

        def value(part, row):
            terms = part[ROWS:, :].astype(jnp.float32)
            return terms[row : row + 1] + terms[row + 1 : row + 2] + terms[row + 2 : row + 3]

        tops = [value(part, 0) for part in parts]
        top = tops[0]
        for other in tops[1:]:
            top = jnp.maximum(top, other)
        total = jnp.zeros((1, 256), jnp.float32)
        for part, other in zip(parts, tops):
            total = total + value(part, 3) * jnp.exp(other - top)
        norm = top + jnp.log(total)
        goal = jnp.zeros((ROWS, 256), jnp.float32)
        for part in parts:
            goal = goal + part[0:ROWS, :].astype(jnp.float32)
        goal = goal * (1.0 / 64.0)
        held = logits[...]
        seen = held != NEG
        logp = held - norm
        live = seen & (goal > 0)
        safe = jnp.where(goal > 0, goal, 1.0)
        part = jnp.where(live, goal * (jnp.log(safe) - logp), 0.0)
        part = jnp.sum(part, axis=0, keepdims=True)
        part = jnp.concatenate([part, jnp.zeros((15, 256), jnp.float32)], axis=0)
        rows_a[NI:, :] = part[:, :128]
        rows_b[NI:, :] = part[:, 128:]
        grad[...] = jnp.where(seen, jnp.exp(logp) - goal, 0.0) * INDEX_SCALE
        acc[...] = jnp.zeros_like(acc)

    total = acc[...]
    slope = grad[...]
    for j in range(JSTEP):
        at = step * JSTEP + j
        inner, queries = inner_of(keys, ia, ib, at)
        weight = jnp.concatenate([wja[pl.ds(at, 1), :], wjb[pl.ds(at, 1), :]], axis=1)
        open_slope = jnp.where(inner > 0, slope, 0.0)
        share = jnp.sum(open_slope * inner, axis=0, keepdims=True)
        rows_a[pl.ds(at, 1), :] = share[:, :128]
        rows_b[pl.ds(at, 1), :] = share[:, 128:]
        coeff = (open_slope * weight).astype(jnp.bfloat16)
        total = total + jnp.dot(coeff, queries, preferred_element_type=jnp.float32)
    acc[...] = total

    @pl.when(step == NI // JSTEP - 1)
    def _():
        quarter = meta[4]
        for b in range(BLOCKS):
            kg[b, 0:UNIT, :] = acc[b * UNIT : (b + 1) * UNIT, :].astype(jnp.bfloat16)
            at = 256 + (b // 4) * UNIT
            extra = jnp.where(quarter == b % 4, acc[at : at + UNIT, :], 0.0)
            kg[b, UNIT:, :] = extra.astype(jnp.bfloat16)


def backward_call(meta, keys, logits, target, ia, ib, wa, wb):
    return pl.pallas_call(
        backward_kernel,
        grid_spec=pltpu.PrefetchScalarGridSpec(
            num_scalar_prefetch=1,
            grid=(NI // JSTEP,),
            in_specs=[HERE] * 10,
            out_specs=[HERE] * 3,
            scratch_shapes=[
                pltpu.VMEM((ROWS, 256), jnp.float32),
                pltpu.VMEM((ROWS, DI), jnp.float32),
            ],
        ),
        out_shape=[
            pltpu.VMEM((NI + 16, 128), jnp.float32),
            pltpu.VMEM((NI + 16, 128), jnp.float32),
            pltpu.VMEM((BLOCKS, 2 * UNIT, DI), jnp.bfloat16),
        ],
        cost_estimate=pl.CostEstimate(
            flops=4 * NI * ROWS * 256 * DI, bytes_accessed=6 << 20, transcendentals=0
        ),
        compiler_params=pltpu.CompilerParams(vmem_limit_bytes=VMEM),
        name="index_backward",
    )(meta, *in_vmem(keys, logits, *target, ia, ib, wa, wb))


PART = 7 * UNIT


def finish_kernel(meta, p0, p1, p2, p3, div, weight, key, held):
    quarter = meta[4]
    for r, pair in enumerate((p0, p1, p2, p3)):
        held[r] = pair[...]
    x, yhi = (quarter & 1) * 2 + meta[3], quarter >> 1
    rows = jnp.zeros((PART - 2 * UNIT, 128), jnp.float32)
    rest = [jnp.zeros((UNIT, DI), jnp.float32)] * 2
    for y in range(2):
        for k in range(4):
            at = pl.ds(pl.multiple_of((yhi ^ y) * PART, UNIT), PART)
            part = held[(x - k) & 3, at, :].astype(jnp.float32)
            rows = rows + part[2 * UNIT :]
            half = k & 1
            first = half * HALF + (y * 2 + (k >> 1)) * UNIT
            key[first : first + UNIT, :] = part[0:UNIT]
            rest[half] = rest[half] + part[UNIT : 2 * UNIT]
    for half in range(2):
        key[half * HALF + 4 * UNIT : (half + 1) * HALF, :] = rest[half]
    weight[...] = rows[0:NI]
    div[...] = rows[NI : NI + 1] + rows[NI + 8 : NI + 9]


def finish_call(meta, *pairs):
    return pl.pallas_call(
        finish_kernel,
        grid_spec=pltpu.PrefetchScalarGridSpec(
            num_scalar_prefetch=1,
            grid=(1,),
            in_specs=[HERE] * 4,
            out_specs=[HERE] * 3,
            scratch_shapes=[pltpu.VMEM((4, 2 * PART, 128), jnp.bfloat16)],
        ),
        out_shape=[jax.ShapeDtypeStruct((rows, 128), jnp.float32) for rows in (1, NI, 2 * HALF)],
        compiler_params=pltpu.CompilerParams(vmem_limit_bytes=2 << 20),
        name="finish",
    )(meta, *in_vmem(*pairs))


def after(value, *others):
    return lax.optimization_barrier((value,) + others)[0]


def body(main_queries, latent_keys, index_queries, index_weights, index_keys, tile_order, offset):
    z, ylo, core = lax.axis_index("z"), lax.axis_index("ylo"), lax.axis_index("core")
    half = lax.axis_index("xp")
    quarter = lax.axis_index("yhi") * 2 + lax.axis_index("xh")

    rows = jnp.arange(TILE, dtype=jnp.int32)
    place = (offset + (tile_order[:, None] * TILE + rows[None, :])).reshape(1, 128)
    pa, wa = place.astype(jnp.float32), index_weights.T
    own = jnp.concatenate([index_keys, latent_keys], axis=1)
    own = lax.dynamic_slice_in_dim(own, half * HALF, HALF, 0)
    meta = jnp.stack([z, ylo, core, half, quarter]).astype(jnp.int32)
    own, meta = lax.optimization_barrier((own, meta))

    queries = main_queries.transpose(0, 2, 1)
    f1, b1 = shift(own, dz=1), shift(own, dz=7)
    queries_far = swap_core(queries)
    f1, b1, left, right = lax.optimization_barrier((f1, b1, queries[:4], queries[4:]))
    left, right = shift(left, dx=1), shift(right, dx=3)
    f2, b2 = shift(f1, dz=1), shift(b1, dz=7)
    f2, b2 = lax.optimization_barrier((f2, b2))
    f3, b3 = shift(f2, dz=1), shift(b2, dz=7)
    pb = swap_core(pa)
    f3, b3, left, right, pb = lax.optimization_barrier((f3, b3, left, right, pb))
    f4 = shift(f3, dz=1)
    f4, ia = lax.optimization_barrier((f4, index_queries.transpose(1, 0, 2)))
    left_far, right_far = swap_core(left), swap_core(right)
    y0, y1 = jnp.concatenate([own, f1, b1, f2]), jnp.concatenate([b2, f3, b3, f4])
    y0, y1 = shift(y0, dy=1), shift(y1, dy=3)
    ia, wa = lax.optimization_barrier((ia, wa, f4, left_far, right_far))[:2]
    ib, wb = swap_core(ia), swap_core(wa)

    sides = (queries, queries_far, left, left_far, right, right_far, pa, pb)
    exps, m0, l0, keys = score_call(meta, 0, [own, f1, b1, f2, b2, f3, b3, f4], [], *sides)
    exps, m1, l1, keys = score_call(meta, 1, [y0, y1], in_vmem(exps, keys), *sides)

    logits, ours, sent = forward_call(meta, keys, (m0, l0, m1, l1), ia, ib, pa, pb, wa, wb)
    here, up, down = pair_call(ours, swap_core(sent))
    up, down = shift(up, dx=1), shift(down, dx=3)
    sums = head_sum_call(meta, exps, m0, m1, here, up, down)
    far = shift(sums[3], dx=2, dy=2)
    target = [sums[0], far, shift(sums[1], dx=2), shift(sums[2], dy=2)]

    mine, other, kg = backward_call(meta, keys, logits, target, ia, ib, wa, wb)
    rows_out = mine + swap_core(other)
    rows_high = lax.reduce_precision(rows_out, 8, 7)
    low = jnp.concatenate([jnp.zeros((NI + 8, 128), jnp.float32), (rows_out - rows_high)[NI : NI + 8]])
    tail = rows_high + low
    kg = lax.all_to_all(kg, ("z", "ylo"), 0, 0, tiled=True)
    kg = jnp.sum(kg.astype(jnp.float32), axis=0)
    part = jnp.concatenate([kg, tail]).astype(jnp.bfloat16)
    pair = jnp.concatenate([part, shift(part, dy=2)])
    div, weight, key_grad = finish_call(meta, pair, *(shift(pair, dx=dx) for dx in (1, 2, 3)))
    return div.reshape(128), weight.T, key_grad


def solution(mesh):
    fine = Mesh(np.asarray(mesh.devices).reshape(2, 2, 2, 8, 2, 2), ALL)
    head, ctx = ("yhi", "xh", "xp"), ("z", "ylo", "core")
    in_specs = (
        P(head, ctx, None),
        P(ctx, None),
        P(ctx, None, None),
        P(ctx, None),
        P(ctx, None),
        P(ctx),
        P(),
    )
    out_specs = (P(ctx), P(ctx, None), P(ctx, None))
    return jax.shard_map(body, mesh=fine, in_specs=in_specs, out_specs=out_specs, check_vma=False)
```

```python
import math

import jax
import jax.numpy as jnp
import numpy as np
from jax import lax
from jax.experimental import pallas as pl
from jax.experimental.pallas import tpu as pltpu
from jax.sharding import Mesh
from jax.sharding import PartitionSpec as P

TILE = 32
DQ = 576
DI = 128
NI = 64
HALF = 80
UNIT = 16
BLOCKS = 16
ROWS = 320
SCORE2 = 192.0 ** (-0.5) * math.log2(math.e)
INDEX_SCALE = DI ** (-0.5)
ALL = ("yhi", "xh", "xp", "z", "ylo", "core")
NEG = -jnp.inf
VMEM = 12 << 20
HERE = pl.BlockSpec(memory_space=pltpu.VMEM)


def flat(x, y, z, c):
    return ((y // 2) * 4 + x) * 32 + (z * 2 + (y % 2)) * 2 + c


def shift(value, dx=0, dy=0, dz=0, flip=0):
    pairs = [
        (flat(x, y, z, c), flat((x + dx) % 4, (y + dy) % 4, (z + dz) % 8, c ^ flip))
        for x in range(4)
        for y in range(4)
        for z in range(8)
        for c in range(2)
    ]
    return lax.ppermute(value, ALL, pairs)


def swap_core(value):
    return shift(value, flip=1)


LOG2E = math.log2(math.e)


def in_vmem(*values):
    return [pltpu.with_memory_space_constraint(value, pltpu.VMEM) for value in values]


def slot_of(meta, i):
    k = i & 7
    reach = (k + 1) >> 1
    step = reach * (1 - 2 * (k & 1))
    return ((meta[0] + 8 + step) & 7) * 2 + (meta[1] ^ (i >> 3))


def place_of(pa, pb):
    return jnp.concatenate([pa[...], pb[...]], axis=1)


def merge(m0, l0, m1, l1, rate):
    top = jnp.maximum(m0, m1)
    return top, l0 * jnp.exp2((m0 - top) * rate) + l1 * jnp.exp2((m1 - top) * rate)


def swapped(value):
    return jnp.concatenate([value[:, 128:], value[:, :128]], axis=1)


HEADS = 16
CHUNK = 8 * HALF


def score_kernel(chunk, spans, meta, *refs):
    n = len(spans)
    blocks, refs = refs[:n], refs[n:]
    if chunk:
        _, ik_before, refs = refs[0], refs[1], refs[2:]
    qa, qb, na, nb, ma, mb, pa, pb = refs[:8]
    e_ref, m_ref, l_ref, ik_ref, keys, bias, raw, tops, sems = refs[8:]
    step = pl.program_id(0)
    cut = 320

    @pl.when(step == 0)
    def _():
        copies = []
        at = 0
        for i, (block, span) in enumerate(zip(blocks, spans)):
            copies.append(pltpu.make_async_copy(block, keys.at[at : at + span, :], sems.at[i]))
            copies[-1].start()
            at += span
        place = place_of(pa, pb)
        offsets = lax.broadcasted_iota(jnp.int32, (HALF, 256), 0).astype(jnp.float32)
        slots = [slot_of(meta, 8 * chunk + i) for i in range(8)]
        for i in range(8):
            base = ((slots[i] * 2 + meta[2]) * 160 + meta[3] * HALF).astype(jnp.float32)
            bias[i * HALF : (i + 1) * HALF, :] = jnp.where(offsets + base <= place, 0.0, NEG)
        tops[...] = jnp.zeros_like(tops)
        ik_ref[...] = ik_before[...] if chunk else jnp.zeros_like(ik_ref)
        for copy in copies:
            copy.wait()
        quarter = meta[4]
        for i in range(8):
            slot = slots[i]
            mine = pl.ds(pl.multiple_of(i * HALF + quarter * UNIT, UNIT), UNIT)
            ik_ref[pl.ds(pl.multiple_of(slot * UNIT, UNIT), UNIT), :] = keys[mine, 0:DI]

            @pl.when((slot & 3) == quarter)
            def _():
                extra = pl.multiple_of(256 + (slot >> 2) * UNIT, UNIT)
                ik_ref[pl.ds(extra, UNIT), :] = keys[i * HALF + 4 * UNIT : (i + 1) * HALF, 0:DI]

    def work(now, last):
        for k in range(2):
            own, left, right = (
                jnp.concatenate([a[at], b[at]], axis=1)
                for a, b, at in (
                    (qa, qb, 2 * jnp.minimum(step, 3) + k),
                    (na, nb, 2 * jnp.clip(step - 4, 0, 1) + k),
                    (ma, mb, 2 * jnp.clip(step - 6, 0, 1) + k),
                )
            )
            queries = jnp.where(step < 4, own, jnp.where(step < 6, left, right))
            top = jnp.max(tops[last, k], axis=0, keepdims=True)
            safe = jnp.where(top == NEG, 0.0, top)
            head = 2 * jnp.maximum(step - 1, 0) + k
            new = jnp.full((8, 256), NEG, jnp.float32)
            total = jnp.zeros((8, 256), jnp.float32)
            for t in range(0, CHUNK, cut):
                piece, rows = slice(t, t + cut), slice(chunk * CHUNK + t, chunk * CHUNK + t + cut)
                scores = jnp.dot(keys[piece, DI:], queries, preferred_element_type=jnp.float32)
                scores = scores + bias[piece, :]
                raw[now, k, piece, :] = scores
                new = jnp.maximum(new, jnp.max(scores.reshape(cut // 8, 8, 256), axis=0))
                exps = jnp.exp2((raw[last, k, piece, :] - safe) * SCORE2)
                e_ref[head, rows, :] = exps.astype(jnp.bfloat16)
                total = total + jnp.sum(exps.reshape(cut // 8, 8, 256), axis=0)
            tops[now, k] = new
            m_ref[pl.ds(head, 1), :] = top
            l_ref[pl.ds(head, 1), :] = jnp.sum(total, axis=0, keepdims=True)

    @pl.when(step % 2 == 0)
    def _():
        work(0, 1)

    @pl.when(step % 2 == 1)
    def _():
        work(1, 0)


def score_call(meta, chunk, blocks, before, qa, qb, na, nb, ma, mb, pa, pb):
    spans = [b.shape[0] for b in blocks]
    anywhere = pl.BlockSpec(memory_space=pl.ANY)
    return pl.pallas_call(
        lambda *refs: score_kernel(chunk, spans, *refs),
        grid_spec=pltpu.PrefetchScalarGridSpec(
            num_scalar_prefetch=1,
            grid=(HEADS // 2 + 1,),
            in_specs=[anywhere] * len(blocks)
            + [HERE] * (len(before) + 8),
            out_specs=[HERE] * 4,
            scratch_shapes=[
                pltpu.VMEM((CHUNK, DI + DQ), jnp.bfloat16),
                pltpu.VMEM((CHUNK, 256), jnp.float32),
                pltpu.VMEM((2, 2, CHUNK, 256), jnp.float32),
                pltpu.VMEM((2, 2, 8, 256), jnp.float32),
                pltpu.SemaphoreType.DMA((len(blocks),)),
            ],
        ),
        out_shape=[
            pltpu.VMEM((HEADS, 2 * CHUNK, 256), jnp.bfloat16),
            pltpu.VMEM((HEADS, 256), jnp.float32),
            pltpu.VMEM((HEADS, 256), jnp.float32),
            pltpu.VMEM((ROWS, DI), jnp.bfloat16),
        ],
        input_output_aliases={1 + len(blocks): 0} if chunk else {},
        cost_estimate=pl.CostEstimate(
            flops=4 * HEADS * CHUNK * 256 * DQ,
            bytes_accessed=HEADS * CHUNK * 512,
            transcendentals=HEADS * CHUNK * 256,
        ),
        compiler_params=pltpu.CompilerParams(vmem_limit_bytes=VMEM),
        name="scores",
    )(meta, *in_vmem(*blocks), *before, *in_vmem(qa, qb, na, nb, ma, mb, pa, pb))


def head_sum_kernel(meta, e_ref, m0, m1, here, up, down, o0, o1, o2, o3, total_ref, ratio):
    i = pl.program_id(0)

    @pl.when(i == 0)
    def _():
        def side(v):
            heads = [down[v, 4:8, :], up[v, 4:8, :], up[v, 0:4, :], down[v, 0:4, :]]
            return jnp.concatenate(heads, axis=0)

        top, total = merge(here[0, 0:16, :], here[1, 0:16, :], side(0), side(1), SCORE2)
        for c, m in enumerate((m0, m1)):
            ratio[c] = jnp.exp2((m[...] - top) * SCORE2) / total
        index = slice(HEADS, HEADS + 1)
        terms = []
        for left in merge(here[0, index, :], here[1, index, :], down[0, 8:9, :], down[1, 8:9, :], LOG2E):
            for _ in range(3):
                term = left.astype(jnp.bfloat16).astype(jnp.float32)
                terms.append(term)
                left = left - term
        packed = jnp.concatenate(terms + [jnp.zeros((10, 256), jnp.float32)], axis=0)
        for out in (o0, o1, o2, o3):
            out[ROWS:, :] = packed.astype(jnp.bfloat16)

    chunk = i // 8
    total = jnp.zeros((HALF, 256), jnp.float32)
    for h in range(HEADS):
        part = e_ref[h, pl.ds(pl.multiple_of(i * HALF, HALF), HALF), :]
        total = total + part.astype(jnp.float32) * ratio[chunk, h : h + 1, :]
    total_ref[...] = total
    slot = slot_of(meta, i)
    quarter = meta[4]
    at = pl.ds(pl.multiple_of(slot * UNIT, UNIT), UNIT)
    extra = pl.ds(pl.multiple_of(256 + (slot >> 2) * UNIT, UNIT), UNIT)
    for k, out in enumerate((o0, o1, o2, o3)):
        unit = pl.multiple_of((quarter ^ k) * UNIT, UNIT)
        out[at, :] = total_ref[pl.ds(unit, UNIT), :].astype(jnp.bfloat16)

        @pl.when((slot & 3) == (quarter ^ k))
        def _():
            out[extra, :] = total_ref[4 * UNIT :, :].astype(jnp.bfloat16)


def head_sum_call(meta, exps, *stats):
    return pl.pallas_call(
        head_sum_kernel,
        grid_spec=pltpu.PrefetchScalarGridSpec(
            num_scalar_prefetch=1,
            grid=(BLOCKS,),
            in_specs=[HERE] * (1 + len(stats)),
            out_specs=[HERE] * 4,
            scratch_shapes=[
                pltpu.VMEM((HALF, 256), jnp.float32),
                pltpu.VMEM((2, HEADS, 256), jnp.float32),
            ],
        ),
        out_shape=[pltpu.VMEM((ROWS + UNIT, 256), jnp.bfloat16)] * 4,
        cost_estimate=pl.CostEstimate(flops=0, bytes_accessed=11 << 20, transcendentals=0),
        compiler_params=pltpu.CompilerParams(vmem_limit_bytes=VMEM),
        name="head_sum",
    )(meta, *in_vmem(exps, *stats))


def key_places(meta):
    core, half, quarter = meta[2], meta[3], meta[4]
    rows = lax.broadcasted_iota(jnp.int32, (UNIT, 256), 0)
    out = []
    for u in range(16):
        out.append(rows + ((u // 2 * 4 + (u % 2) * 2 + core) * 160 + half * HALF + quarter * UNIT))
    for e in range(4):
        z, ylo = 2 * e + (quarter >> 1), quarter & 1
        out.append(rows + ((z * 4 + ylo * 2 + core) * 160 + half * HALF + 4 * UNIT))
    return out


def inner_of(keys, ia, ib, j):
    queries = jnp.concatenate([ia[j], ib[j]], axis=0)
    return lax.dot_general(
        keys[...], queries, (((1,), (1,)), ((), ())), preferred_element_type=jnp.float32
    ), queries


JSTEP = 32


def forward_kernel(meta, keys, m0, l0, m1, l1, ia, ib, pa, pb, wja, wjb, logits, here, sent):
    step = pl.program_id(0)

    @pl.when(step == 0)
    def _():
        logits[...] = jnp.zeros_like(logits)

    total = logits[...]
    for j in range(JSTEP):
        at = step * JSTEP + j
        inner, _ = inner_of(keys, ia, ib, at)
        weight = jnp.concatenate([wja[pl.ds(at, 1), :], wjb[pl.ds(at, 1), :]], axis=1)
        total = total + weight * jnp.maximum(inner, 0.0)
    logits[...] = total

    @pl.when(step == NI // JSTEP - 1)
    def _():
        place = place_of(pa, pb)
        places = key_places(meta)
        top = jnp.full((1, 256), NEG, jnp.float32)
        for u in range(20):
            cut = slice(u * UNIT, (u + 1) * UNIT)
            value = logits[cut, :] * INDEX_SCALE
            value = jnp.where(places[u].astype(jnp.float32) <= place, value, NEG)
            logits[cut, :] = value
            top = jnp.maximum(top, jnp.max(value, axis=0, keepdims=True))
        safe = jnp.where(top == NEG, 0.0, top)
        total = jnp.sum(jnp.exp(logits[...] - safe), axis=0, keepdims=True)
        tops, totals = merge(m0[...], l0[...], m1[...], l1[...], SCORE2)
        for v, (heads, index) in enumerate(((tops, top), (totals, total))):
            rows = jnp.concatenate([heads, index, jnp.zeros((7, 256), jnp.float32)], axis=0)
            here[v] = rows
            sent[v] = swapped(rows)


def pair_kernel(ours, theirs, here, up, down):
    index = slice(HEADS, HEADS + 1)
    heads = slice(0, HEADS)
    tops, totals = merge(ours[0, heads, :], ours[1, heads, :], theirs[0, heads, :], theirs[1, heads, :], SCORE2)
    top, total = merge(ours[0, index, :], ours[1, index, :], theirs[0, index, :], theirs[1, index, :], LOG2E)
    for v, (main, extra) in enumerate(((tops, top), (totals, total))):
        pad = jnp.zeros((7, 256), jnp.float32)
        here[v] = jnp.concatenate([main, extra, pad], axis=0)
        up[v] = jnp.concatenate([main[0:4], main[12:16]], axis=0)
        down[v] = jnp.concatenate([main[4:12], extra, pad], axis=0)


def pair_call(ours, theirs):
    return pl.pallas_call(
        pair_kernel,
        in_specs=[HERE] * 2,
        out_specs=[HERE] * 3,
        out_shape=[pltpu.VMEM((2, rows, 256), jnp.float32) for rows in (24, 8, 16)],
        compiler_params=pltpu.CompilerParams(vmem_limit_bytes=1 << 20),
        name="pair_statistics",
    )(*in_vmem(ours, theirs))


def forward_call(meta, keys, stats, ia, ib, pa, pb, wa, wb):
    return pl.pallas_call(
        forward_kernel,
        grid_spec=pltpu.PrefetchScalarGridSpec(
            num_scalar_prefetch=1,
            grid=(NI // JSTEP,),
            in_specs=[HERE] * 11,
            out_specs=[HERE] * 3,
        ),
        out_shape=[
            pltpu.VMEM((ROWS, 256), jnp.float32),
            pltpu.VMEM((2, 24, 256), jnp.float32),
            pltpu.VMEM((2, 24, 256), jnp.float32),
        ],
        cost_estimate=pl.CostEstimate(
            flops=2 * NI * ROWS * 256 * DI, bytes_accessed=5 << 20, transcendentals=0
        ),
        compiler_params=pltpu.CompilerParams(vmem_limit_bytes=VMEM),
        name="index_forward",
    )(meta, *in_vmem(keys, *stats, ia, ib, pa, pb, wa, wb))


def backward_kernel(meta, keys, logits, t0, t1, t2, t3, ia, ib, wja, wjb, rows_a, rows_b, kg, grad, acc):
    step = pl.program_id(0)

    @pl.when(step == 0)
    def _():
        parts = (t0, t1, t2, t3)

        def value(part, row):
            terms = part[ROWS:, :].astype(jnp.float32)
            return terms[row : row + 1] + terms[row + 1 : row + 2] + terms[row + 2 : row + 3]

        tops = [value(part, 0) for part in parts]
        top = tops[0]
        for other in tops[1:]:
            top = jnp.maximum(top, other)
        total = jnp.zeros((1, 256), jnp.float32)
        for part, other in zip(parts, tops):
            total = total + value(part, 3) * jnp.exp(other - top)
        norm = top + jnp.log(total)
        goal = jnp.zeros((ROWS, 256), jnp.float32)
        for part in parts:
            goal = goal + part[0:ROWS, :].astype(jnp.float32)
        goal = goal * (1.0 / 64.0)
        held = logits[...]
        seen = held != NEG
        logp = held - norm
        live = seen & (goal > 0)
        safe = jnp.where(goal > 0, goal, 1.0)
        part = jnp.where(live, goal * (jnp.log(safe) - logp), 0.0)
        part = jnp.sum(part, axis=0, keepdims=True)
        part = jnp.concatenate([part, jnp.zeros((15, 256), jnp.float32)], axis=0)
        rows_a[NI:, :] = part[:, :128]
        rows_b[NI:, :] = part[:, 128:]
        grad[...] = jnp.where(seen, jnp.exp(logp) - goal, 0.0) * INDEX_SCALE
        acc[...] = jnp.zeros_like(acc)

    total = acc[...]
    slope = grad[...]
    for j in range(JSTEP):
        at = step * JSTEP + j
        inner, queries = inner_of(keys, ia, ib, at)
        weight = jnp.concatenate([wja[pl.ds(at, 1), :], wjb[pl.ds(at, 1), :]], axis=1)
        open_slope = jnp.where(inner > 0, slope, 0.0)
        share = jnp.sum(open_slope * inner, axis=0, keepdims=True)
        rows_a[pl.ds(at, 1), :] = share[:, :128]
        rows_b[pl.ds(at, 1), :] = share[:, 128:]
        coeff = (open_slope * weight).astype(jnp.bfloat16)
        total = total + jnp.dot(coeff, queries, preferred_element_type=jnp.float32)
    acc[...] = total

    @pl.when(step == NI // JSTEP - 1)
    def _():
        quarter = meta[4]
        for b in range(BLOCKS):
            kg[b, 0:UNIT, :] = acc[b * UNIT : (b + 1) * UNIT, :].astype(jnp.bfloat16)
            at = 256 + (b // 4) * UNIT
            extra = jnp.where(quarter == b % 4, acc[at : at + UNIT, :], 0.0)
            kg[b, UNIT:, :] = extra.astype(jnp.bfloat16)


def backward_call(meta, keys, logits, target, ia, ib, wa, wb):
    return pl.pallas_call(
        backward_kernel,
        grid_spec=pltpu.PrefetchScalarGridSpec(
            num_scalar_prefetch=1,
            grid=(NI // JSTEP,),
            in_specs=[HERE] * 10,
            out_specs=[HERE] * 3,
            scratch_shapes=[
                pltpu.VMEM((ROWS, 256), jnp.float32),
                pltpu.VMEM((ROWS, DI), jnp.float32),
            ],
        ),
        out_shape=[
            pltpu.VMEM((NI + 16, 128), jnp.float32),
            pltpu.VMEM((NI + 16, 128), jnp.float32),
            pltpu.VMEM((BLOCKS, 2 * UNIT, DI), jnp.bfloat16),
        ],
        cost_estimate=pl.CostEstimate(
            flops=4 * NI * ROWS * 256 * DI, bytes_accessed=6 << 20, transcendentals=0
        ),
        compiler_params=pltpu.CompilerParams(vmem_limit_bytes=VMEM),
        name="index_backward",
    )(meta, *in_vmem(keys, logits, *target, ia, ib, wa, wb))


PART = 7 * UNIT


def finish_kernel(meta, *refs):
    parts, (div, weight, key, held) = refs[:8], refs[8:]
    quarter = meta[4]
    for r, part in enumerate(parts):
        held[r] = part[...]
    x, yhi = (quarter & 1) * 2 + meta[3], quarter >> 1
    rows = jnp.zeros((PART - 2 * UNIT, 128), jnp.float32)
    rest = [jnp.zeros((UNIT, DI), jnp.float32)] * 2
    for y in range(2):
        for k in range(4):
            part = held[(yhi ^ y) * 4 + ((x - k) & 3)].astype(jnp.float32)
            rows = rows + part[2 * UNIT :]
            half = k & 1
            first = half * HALF + (y * 2 + (k >> 1)) * UNIT
            key[first : first + UNIT, :] = part[0:UNIT]
            rest[half] = rest[half] + part[UNIT : 2 * UNIT]
    for half in range(2):
        key[half * HALF + 4 * UNIT : (half + 1) * HALF, :] = rest[half]
    weight[...] = rows[0:NI]
    div[...] = rows[NI : NI + 1] + rows[NI + 8 : NI + 9]


def finish_call(meta, *parts):
    return pl.pallas_call(
        finish_kernel,
        grid_spec=pltpu.PrefetchScalarGridSpec(
            num_scalar_prefetch=1,
            grid=(1,),
            in_specs=[HERE] * 8,
            out_specs=[HERE] * 3,
            scratch_shapes=[pltpu.VMEM((8, PART, 128), jnp.bfloat16)],
        ),
        out_shape=[jax.ShapeDtypeStruct((rows, 128), jnp.float32) for rows in (1, NI, 2 * HALF)],
        compiler_params=pltpu.CompilerParams(vmem_limit_bytes=2 << 20),
        name="finish",
    )(meta, *in_vmem(*parts))


def after(value, *others):
    return lax.optimization_barrier((value,) + others)[0]


def body(main_queries, latent_keys, index_queries, index_weights, index_keys, tile_order, offset):
    z, ylo, core = lax.axis_index("z"), lax.axis_index("ylo"), lax.axis_index("core")
    half = lax.axis_index("xp")
    quarter = lax.axis_index("yhi") * 2 + lax.axis_index("xh")

    rows = jnp.arange(TILE, dtype=jnp.int32)
    place = (offset + (tile_order[:, None] * TILE + rows[None, :])).reshape(1, 128)
    pa, wa = place.astype(jnp.float32), index_weights.T
    own = jnp.concatenate([index_keys, latent_keys], axis=1)
    own = lax.dynamic_slice_in_dim(own, half * HALF, HALF, 0)
    meta = jnp.stack([z, ylo, core, half, quarter]).astype(jnp.int32)
    own, meta = lax.optimization_barrier((own, meta))

    queries = main_queries.transpose(0, 2, 1)
    f1, b1 = shift(own, dz=1), shift(own, dz=7)
    queries_far = swap_core(queries)
    f1, b1, left, right = lax.optimization_barrier((f1, b1, queries[:4], queries[4:]))
    left, right = shift(left, dx=1), shift(right, dx=3)
    f2, b2 = shift(f1, dz=1), shift(b1, dz=7)
    f2, b2 = lax.optimization_barrier((f2, b2))
    f3, b3 = shift(f2, dz=1), shift(b2, dz=7)
    pb = swap_core(pa)
    f3, b3, left, right, pb = lax.optimization_barrier((f3, b3, left, right, pb))
    f4 = shift(f3, dz=1)
    f4, ia = lax.optimization_barrier((f4, index_queries.transpose(1, 0, 2)))
    left_far, right_far = swap_core(left), swap_core(right)
    y0, y1 = jnp.concatenate([own, f1, b1, f2]), jnp.concatenate([b2, f3, b3, f4])
    y0, y1 = shift(y0, dy=1), shift(y1, dy=3)
    ia, wa = lax.optimization_barrier((ia, wa, f4, left_far, right_far))[:2]
    ib, wb = swap_core(ia), swap_core(wa)

    sides = (queries, queries_far, left, left_far, right, right_far, pa, pb)
    exps, m0, l0, keys = score_call(meta, 0, [own, f1, b1, f2, b2, f3, b3, f4], [], *sides)
    exps, m1, l1, keys = score_call(meta, 1, [y0, y1], in_vmem(exps, keys), *sides)

    logits, ours, sent = forward_call(meta, keys, (m0, l0, m1, l1), ia, ib, pa, pb, wa, wb)
    here, up, down = pair_call(ours, swap_core(sent))
    up, down = shift(up, dx=1), shift(down, dx=3)
    sums = head_sum_call(meta, exps, m0, m1, here, up, down)
    far = shift(sums[3], dx=2, dy=2)
    target = [sums[0], far, shift(sums[1], dx=2), shift(sums[2], dy=2)]

    mine, other, kg = backward_call(meta, keys, logits, target, ia, ib, wa, wb)
    rows_out = mine + swap_core(other)
    rows_high = lax.reduce_precision(rows_out, 8, 7)
    low = jnp.concatenate([jnp.zeros((NI + 8, 128), jnp.float32), (rows_out - rows_high)[NI : NI + 8]])
    tail = rows_high + low
    kg = lax.all_to_all(kg, ("z", "ylo"), 0, 0, tiled=True)
    kg = jnp.sum(kg.astype(jnp.float32), axis=0)
    part = jnp.concatenate([kg, tail]).astype(jnp.bfloat16)
    moves = [(dx, dy) for dy in (0, 2) for dx in range(4)][1:]
    div, weight, key_grad = finish_call(meta, part, *(shift(part, dx=dx, dy=dy) for dx, dy in moves))
    return div.reshape(128), weight.T, key_grad


def solution(mesh):
    fine = Mesh(np.asarray(mesh.devices).reshape(2, 2, 2, 8, 2, 2), ALL)
    head, ctx = ("yhi", "xh", "xp"), ("z", "ylo", "core")
    in_specs = (
        P(head, ctx, None),
        P(ctx, None),
        P(ctx, None, None),
        P(ctx, None),
        P(ctx, None),
        P(ctx),
        P(),
    )
    out_specs = (P(ctx), P(ctx, None), P(ctx, None))
    return jax.shard_map(body, mesh=fine, in_specs=in_specs, out_specs=out_specs, check_vma=False)
```

```python
import math

import jax
import jax.numpy as jnp
import numpy as np
from jax import lax
from jax.experimental import pallas as pl
from jax.experimental.pallas import tpu as pltpu
from jax.sharding import Mesh
from jax.sharding import PartitionSpec as P

TILE = 32
DQ = 576
DI = 128
NI = 64
HALF = 80
UNIT = 16
BLOCKS = 16
ROWS = 320
SCORE2 = 192.0 ** (-0.5) * math.log2(math.e)
INDEX_SCALE = DI ** (-0.5)
ALL = ("yhi", "xh", "xp", "z", "ylo", "core")
NEG = -jnp.inf
VMEM = 12 << 20
HERE = pl.BlockSpec(memory_space=pltpu.VMEM)


def flat(x, y, z, c):
    return ((y // 2) * 4 + x) * 32 + (z * 2 + (y % 2)) * 2 + c


def shift(value, dx=0, dy=0, dz=0, flip=0):
    pairs = [
        (flat(x, y, z, c), flat((x + dx) % 4, (y + dy) % 4, (z + dz) % 8, c ^ flip))
        for x in range(4)
        for y in range(4)
        for z in range(8)
        for c in range(2)
    ]
    return lax.ppermute(value, ALL, pairs)


def swap_core(value):
    return shift(value, flip=1)


LOG2E = math.log2(math.e)


def in_vmem(*values):
    return [pltpu.with_memory_space_constraint(value, pltpu.VMEM) for value in values]


def slot_of(meta, i):
    k = i & 7
    reach = (k + 1) >> 1
    step = reach * (1 - 2 * (k & 1))
    return ((meta[0] + 8 + step) & 7) * 2 + (meta[1] ^ (i >> 3))


def place_of(pa, pb):
    return jnp.concatenate([pa[...], pb[...]], axis=1)


def merge(m0, l0, m1, l1, rate):
    top = jnp.maximum(m0, m1)
    return top, l0 * jnp.exp2((m0 - top) * rate) + l1 * jnp.exp2((m1 - top) * rate)


def swapped(value):
    return jnp.concatenate([value[:, 128:], value[:, :128]], axis=1)


HEADS = 16
CHUNK = 8 * HALF


def score_kernel(chunk, spans, meta, *refs):
    n = len(spans)
    blocks, refs = refs[:n], refs[n:]
    if chunk:
        _, ik_before, refs = refs[0], refs[1], refs[2:]
    qa, qb, na, nb, ma, mb, pa, pb = refs[:8]
    e_ref, m_ref, l_ref, ik_ref, keys, bias, raw, tops, sems = refs[8:]
    step = pl.program_id(0)
    cut = 320

    @pl.when(step == 0)
    def _():
        copies = []
        at = 0
        for i, (block, span) in enumerate(zip(blocks, spans)):
            copies.append(pltpu.make_async_copy(block, keys.at[at : at + span, :], sems.at[i]))
            copies[-1].start()
            at += span
        place = place_of(pa, pb)
        offsets = lax.broadcasted_iota(jnp.int32, (HALF, 256), 0).astype(jnp.float32)
        slots = [slot_of(meta, 8 * chunk + i) for i in range(8)]
        for i in range(8):
            base = ((slots[i] * 2 + meta[2]) * 160 + meta[3] * HALF).astype(jnp.float32)
            bias[i * HALF : (i + 1) * HALF, :] = jnp.where(offsets + base <= place, 0.0, NEG)
        tops[...] = jnp.zeros_like(tops)
        ik_ref[...] = ik_before[...] if chunk else jnp.zeros_like(ik_ref)
        for copy in copies:
            copy.wait()
        quarter = meta[4]
        for i in range(8):
            slot = slots[i]
            mine = pl.ds(pl.multiple_of(i * HALF + quarter * UNIT, UNIT), UNIT)
            ik_ref[pl.ds(pl.multiple_of(slot * UNIT, UNIT), UNIT), :] = keys[mine, 0:DI]

            @pl.when((slot & 3) == quarter)
            def _():
                extra = pl.multiple_of(256 + (slot >> 2) * UNIT, UNIT)
                ik_ref[pl.ds(extra, UNIT), :] = keys[i * HALF + 4 * UNIT : (i + 1) * HALF, 0:DI]

    def work(now, last):
        for k in range(2):
            own, left, right = (
                jnp.concatenate([a[at], b[at]], axis=1)
                for a, b, at in (
                    (qa, qb, 2 * jnp.minimum(step, 3) + k),
                    (na, nb, 2 * jnp.clip(step - 4, 0, 1) + k),
                    (ma, mb, 2 * jnp.clip(step - 6, 0, 1) + k),
                )
            )
            queries = jnp.where(step < 4, own, jnp.where(step < 6, left, right))
            top = jnp.max(tops[last, k], axis=0, keepdims=True)
            safe = jnp.where(top == NEG, 0.0, top)
            head = 2 * jnp.maximum(step - 1, 0) + k
            new = jnp.full((8, 256), NEG, jnp.float32)
            total = jnp.zeros((8, 256), jnp.float32)
            for t in range(0, CHUNK, cut):
                piece, rows = slice(t, t + cut), slice(chunk * CHUNK + t, chunk * CHUNK + t + cut)
                scores = jnp.dot(keys[piece, DI:], queries, preferred_element_type=jnp.float32)
                scores = scores + bias[piece, :]
                raw[now, k, piece, :] = scores
                new = jnp.maximum(new, jnp.max(scores.reshape(cut // 8, 8, 256), axis=0))
                exps = jnp.exp2((raw[last, k, piece, :] - safe) * SCORE2)
                e_ref[head, rows, :] = exps.astype(jnp.bfloat16)
                total = total + jnp.sum(exps.reshape(cut // 8, 8, 256), axis=0)
            tops[now, k] = new
            m_ref[pl.ds(head, 1), :] = top
            l_ref[pl.ds(head, 1), :] = jnp.sum(total, axis=0, keepdims=True)

    @pl.when(step % 2 == 0)
    def _():
        work(0, 1)

    @pl.when(step % 2 == 1)
    def _():
        work(1, 0)


def score_call(meta, chunk, blocks, before, qa, qb, na, nb, ma, mb, pa, pb):
    spans = [b.shape[0] for b in blocks]
    anywhere = pl.BlockSpec(memory_space=pl.ANY)
    return pl.pallas_call(
        lambda *refs: score_kernel(chunk, spans, *refs),
        grid_spec=pltpu.PrefetchScalarGridSpec(
            num_scalar_prefetch=1,
            grid=(HEADS // 2 + 1,),
            in_specs=[anywhere] * len(blocks)
            + [HERE] * (len(before) + 8),
            out_specs=[HERE] * 4,
            scratch_shapes=[
                pltpu.VMEM((CHUNK, DI + DQ), jnp.bfloat16),
                pltpu.VMEM((CHUNK, 256), jnp.float32),
                pltpu.VMEM((2, 2, CHUNK, 256), jnp.float32),
                pltpu.VMEM((2, 2, 8, 256), jnp.float32),
                pltpu.SemaphoreType.DMA((len(blocks),)),
            ],
        ),
        out_shape=[
            pltpu.VMEM((HEADS, 2 * CHUNK, 256), jnp.bfloat16),
            pltpu.VMEM((HEADS, 256), jnp.float32),
            pltpu.VMEM((HEADS, 256), jnp.float32),
            pltpu.VMEM((ROWS, DI), jnp.bfloat16),
        ],
        input_output_aliases={1 + len(blocks): 0} if chunk else {},
        cost_estimate=pl.CostEstimate(
            flops=4 * HEADS * CHUNK * 256 * DQ,
            bytes_accessed=HEADS * CHUNK * 512,
            transcendentals=HEADS * CHUNK * 256,
        ),
        compiler_params=pltpu.CompilerParams(vmem_limit_bytes=VMEM),
        name="scores",
    )(meta, *in_vmem(*blocks), *before, *in_vmem(qa, qb, na, nb, ma, mb, pa, pb))


def head_sum_kernel(meta, e_ref, m0, m1, here, up, down, o0, o1, o2, o3, total_ref, ratio):
    i = pl.program_id(0)

    @pl.when(i == 0)
    def _():
        def side(v):
            heads = [down[v, 4:8, :], up[v, 4:8, :], up[v, 0:4, :], down[v, 0:4, :]]
            return jnp.concatenate(heads, axis=0)

        top, total = merge(here[0, 0:16, :], here[1, 0:16, :], side(0), side(1), SCORE2)
        for c, m in enumerate((m0, m1)):
            ratio[c] = jnp.exp2((m[...] - top) * SCORE2) / total
        index = slice(HEADS, HEADS + 1)
        terms = []
        for left in merge(here[0, index, :], here[1, index, :], down[0, 8:9, :], down[1, 8:9, :], LOG2E):
            for _ in range(3):
                term = left.astype(jnp.bfloat16).astype(jnp.float32)
                terms.append(term)
                left = left - term
        packed = jnp.concatenate(terms + [jnp.zeros((10, 256), jnp.float32)], axis=0)
        for out in (o0, o1, o2, o3):
            out[ROWS:, :] = packed.astype(jnp.bfloat16)

    chunk = i // 8
    total = jnp.zeros((HALF, 256), jnp.float32)
    for h in range(HEADS):
        part = e_ref[h, pl.ds(pl.multiple_of(i * HALF, HALF), HALF), :]
        total = total + part.astype(jnp.float32) * ratio[chunk, h : h + 1, :]
    total_ref[...] = total
    slot = slot_of(meta, i)
    quarter = meta[4]
    at = pl.ds(pl.multiple_of(slot * UNIT, UNIT), UNIT)
    extra = pl.ds(pl.multiple_of(256 + (slot >> 2) * UNIT, UNIT), UNIT)
    for k, out in enumerate((o0, o1, o2, o3)):
        unit = pl.multiple_of((quarter ^ k) * UNIT, UNIT)
        out[at, :] = total_ref[pl.ds(unit, UNIT), :].astype(jnp.bfloat16)

        @pl.when((slot & 3) == (quarter ^ k))
        def _():
            out[extra, :] = total_ref[4 * UNIT :, :].astype(jnp.bfloat16)


def head_sum_call(meta, exps, *stats):
    return pl.pallas_call(
        head_sum_kernel,
        grid_spec=pltpu.PrefetchScalarGridSpec(
            num_scalar_prefetch=1,
            grid=(BLOCKS,),
            in_specs=[HERE] * (1 + len(stats)),
            out_specs=[HERE] * 4,
            scratch_shapes=[
                pltpu.VMEM((HALF, 256), jnp.float32),
                pltpu.VMEM((2, HEADS, 256), jnp.float32),
            ],
        ),
        out_shape=[pltpu.VMEM((ROWS + UNIT, 256), jnp.bfloat16)] * 4,
        cost_estimate=pl.CostEstimate(flops=0, bytes_accessed=11 << 20, transcendentals=0),
        compiler_params=pltpu.CompilerParams(vmem_limit_bytes=VMEM),
        name="head_sum",
    )(meta, *in_vmem(exps, *stats))


def key_places(meta):
    core, half, quarter = meta[2], meta[3], meta[4]
    rows = lax.broadcasted_iota(jnp.int32, (UNIT, 256), 0)
    out = []
    for u in range(16):
        out.append(rows + ((u // 2 * 4 + (u % 2) * 2 + core) * 160 + half * HALF + quarter * UNIT))
    for e in range(4):
        z, ylo = 2 * e + (quarter >> 1), quarter & 1
        out.append(rows + ((z * 4 + ylo * 2 + core) * 160 + half * HALF + 4 * UNIT))
    return out


def inner_of(keys, ia, ib, j):
    queries = jnp.concatenate([ia[j], ib[j]], axis=0)
    return lax.dot_general(
        keys[...], queries, (((1,), (1,)), ((), ())), preferred_element_type=jnp.float32
    ), queries


JSTEP = 32


def forward_kernel(meta, keys, m0, l0, m1, l1, ia, ib, pa, pb, wja, wjb, logits, here, sent):
    step = pl.program_id(0)

    @pl.when(step == 0)
    def _():
        logits[...] = jnp.zeros_like(logits)

    total = logits[...]
    for j in range(JSTEP):
        at = step * JSTEP + j
        inner, _ = inner_of(keys, ia, ib, at)
        weight = jnp.concatenate([wja[pl.ds(at, 1), :], wjb[pl.ds(at, 1), :]], axis=1)
        total = total + weight * jnp.maximum(inner, 0.0)
    logits[...] = total

    @pl.when(step == NI // JSTEP - 1)
    def _():
        place = place_of(pa, pb)
        places = key_places(meta)
        top = jnp.full((1, 256), NEG, jnp.float32)
        for u in range(20):
            cut = slice(u * UNIT, (u + 1) * UNIT)
            value = logits[cut, :] * INDEX_SCALE
            value = jnp.where(places[u].astype(jnp.float32) <= place, value, NEG)
            logits[cut, :] = value
            top = jnp.maximum(top, jnp.max(value, axis=0, keepdims=True))
        safe = jnp.where(top == NEG, 0.0, top)
        total = jnp.sum(jnp.exp(logits[...] - safe), axis=0, keepdims=True)
        tops, totals = merge(m0[...], l0[...], m1[...], l1[...], SCORE2)
        for v, (heads, index) in enumerate(((tops, top), (totals, total))):
            rows = jnp.concatenate([heads, index, jnp.zeros((7, 256), jnp.float32)], axis=0)
            here[v] = rows
            sent[v] = swapped(rows)


def pair_kernel(ours, theirs, here, up, down):
    index = slice(HEADS, HEADS + 1)
    heads = slice(0, HEADS)
    tops, totals = merge(ours[0, heads, :], ours[1, heads, :], theirs[0, heads, :], theirs[1, heads, :], SCORE2)
    top, total = merge(ours[0, index, :], ours[1, index, :], theirs[0, index, :], theirs[1, index, :], LOG2E)
    for v, (main, extra) in enumerate(((tops, top), (totals, total))):
        pad = jnp.zeros((7, 256), jnp.float32)
        here[v] = jnp.concatenate([main, extra, pad], axis=0)
        up[v] = jnp.concatenate([main[0:4], main[12:16]], axis=0)
        down[v] = jnp.concatenate([main[4:12], extra, pad], axis=0)


def pair_call(ours, theirs):
    return pl.pallas_call(
        pair_kernel,
        in_specs=[HERE] * 2,
        out_specs=[HERE] * 3,
        out_shape=[pltpu.VMEM((2, rows, 256), jnp.float32) for rows in (24, 8, 16)],
        compiler_params=pltpu.CompilerParams(vmem_limit_bytes=1 << 20),
        name="pair_statistics",
    )(*in_vmem(ours, theirs))


def forward_call(meta, keys, stats, ia, ib, pa, pb, wa, wb):
    return pl.pallas_call(
        forward_kernel,
        grid_spec=pltpu.PrefetchScalarGridSpec(
            num_scalar_prefetch=1,
            grid=(NI // JSTEP,),
            in_specs=[HERE] * 11,
            out_specs=[HERE] * 3,
        ),
        out_shape=[
            pltpu.VMEM((ROWS, 256), jnp.float32),
            pltpu.VMEM((2, 24, 256), jnp.float32),
            pltpu.VMEM((2, 24, 256), jnp.float32),
        ],
        cost_estimate=pl.CostEstimate(
            flops=2 * NI * ROWS * 256 * DI, bytes_accessed=5 << 20, transcendentals=0
        ),
        compiler_params=pltpu.CompilerParams(vmem_limit_bytes=VMEM),
        name="index_forward",
    )(meta, *in_vmem(keys, *stats, ia, ib, pa, pb, wa, wb))


def backward_kernel(meta, keys, logits, t0, t1, t2, t3, ia, ib, wja, wjb, rows_a, rows_b, kg, grad, acc):
    step = pl.program_id(0)

    @pl.when(step == 0)
    def _():
        parts = (t0, t1, t2, t3)

        def value(part, row):
            terms = part[ROWS:, :].astype(jnp.float32)
            return terms[row : row + 1] + terms[row + 1 : row + 2] + terms[row + 2 : row + 3]

        tops = [value(part, 0) for part in parts]
        top = tops[0]
        for other in tops[1:]:
            top = jnp.maximum(top, other)
        total = jnp.zeros((1, 256), jnp.float32)
        for part, other in zip(parts, tops):
            total = total + value(part, 3) * jnp.exp(other - top)
        norm = top + jnp.log(total)
        goal = jnp.zeros((ROWS, 256), jnp.float32)
        for part in parts:
            goal = goal + part[0:ROWS, :].astype(jnp.float32)
        goal = goal * (1.0 / 64.0)
        held = logits[...]
        seen = held != NEG
        logp = held - norm
        live = seen & (goal > 0)
        safe = jnp.where(goal > 0, goal, 1.0)
        part = jnp.where(live, goal * (jnp.log(safe) - logp), 0.0)
        part = jnp.sum(part, axis=0, keepdims=True)
        part = jnp.concatenate([part, jnp.zeros((15, 256), jnp.float32)], axis=0)
        rows_a[NI:, :] = part[:, :128]
        rows_b[NI:, :] = part[:, 128:]
        grad[...] = jnp.where(seen, jnp.exp(logp) - goal, 0.0) * INDEX_SCALE
        acc[...] = jnp.zeros_like(acc)

    total = acc[...]
    slope = grad[...]
    for j in range(JSTEP):
        at = step * JSTEP + j
        inner, queries = inner_of(keys, ia, ib, at)
        weight = jnp.concatenate([wja[pl.ds(at, 1), :], wjb[pl.ds(at, 1), :]], axis=1)
        open_slope = jnp.where(inner > 0, slope, 0.0)
        share = jnp.sum(open_slope * inner, axis=0, keepdims=True)
        rows_a[pl.ds(at, 1), :] = share[:, :128]
        rows_b[pl.ds(at, 1), :] = share[:, 128:]
        coeff = (open_slope * weight).astype(jnp.bfloat16)
        total = total + jnp.dot(coeff, queries, preferred_element_type=jnp.float32)
    acc[...] = total

    @pl.when(step == NI // JSTEP - 1)
    def _():
        quarter = meta[4]
        for b in range(BLOCKS):
            kg[b, 0:UNIT, :] = acc[b * UNIT : (b + 1) * UNIT, :].astype(jnp.bfloat16)
            at = 256 + (b // 4) * UNIT
            extra = jnp.where(quarter == b % 4, acc[at : at + UNIT, :], 0.0)
            kg[b, UNIT:, :] = extra.astype(jnp.bfloat16)


def backward_call(meta, keys, logits, target, ia, ib, wa, wb):
    return pl.pallas_call(
        backward_kernel,
        grid_spec=pltpu.PrefetchScalarGridSpec(
            num_scalar_prefetch=1,
            grid=(NI // JSTEP,),
            in_specs=[HERE] * 10,
            out_specs=[HERE] * 3,
            scratch_shapes=[
                pltpu.VMEM((ROWS, 256), jnp.float32),
                pltpu.VMEM((ROWS, DI), jnp.float32),
            ],
        ),
        out_shape=[
            pltpu.VMEM((NI + 16, 128), jnp.float32),
            pltpu.VMEM((NI + 16, 128), jnp.float32),
            pltpu.VMEM((BLOCKS, 2 * UNIT, DI), jnp.bfloat16),
        ],
        cost_estimate=pl.CostEstimate(
            flops=4 * NI * ROWS * 256 * DI, bytes_accessed=6 << 20, transcendentals=0
        ),
        compiler_params=pltpu.CompilerParams(vmem_limit_bytes=VMEM),
        name="index_backward",
    )(meta, *in_vmem(keys, logits, *target, ia, ib, wa, wb))


PART = 7 * UNIT


def finish_kernel(meta, p0, p1, p2, p3, div, weight, key, held):
    quarter = meta[4]
    for r, pair in enumerate((p0, p1, p2, p3)):
        held[r] = pair[...]
    x, yhi = (quarter & 1) * 2 + meta[3], quarter >> 1
    rows = jnp.zeros((PART - 2 * UNIT, 128), jnp.float32)
    rest = [jnp.zeros((UNIT, DI), jnp.float32)] * 2
    for y in range(2):
        for k in range(4):
            at = pl.ds(pl.multiple_of((yhi ^ y) * PART, UNIT), PART)
            part = held[(x - k) & 3, at, :].astype(jnp.float32)
            rows = rows + part[2 * UNIT :]
            half = k & 1
            first = half * HALF + (y * 2 + (k >> 1)) * UNIT
            key[first : first + UNIT, :] = part[0:UNIT]
            rest[half] = rest[half] + part[UNIT : 2 * UNIT]
    for half in range(2):
        key[half * HALF + 4 * UNIT : (half + 1) * HALF, :] = rest[half]
    weight[...] = rows[0:NI]
    div[...] = rows[NI : NI + 1] + rows[NI + 8 : NI + 9]


def finish_call(meta, *pairs):
    return pl.pallas_call(
        finish_kernel,
        grid_spec=pltpu.PrefetchScalarGridSpec(
            num_scalar_prefetch=1,
            grid=(1,),
            in_specs=[HERE] * 4,
            out_specs=[HERE] * 3,
            scratch_shapes=[pltpu.VMEM((4, 2 * PART, 128), jnp.bfloat16)],
        ),
        out_shape=[jax.ShapeDtypeStruct((rows, 128), jnp.float32) for rows in (1, NI, 2 * HALF)],
        compiler_params=pltpu.CompilerParams(vmem_limit_bytes=2 << 20),
        name="finish",
    )(meta, *in_vmem(*pairs))


def after(value, *others):
    return lax.optimization_barrier((value,) + others)[0]


def body(main_queries, latent_keys, index_queries, index_weights, index_keys, tile_order, offset):
    z, ylo, core = lax.axis_index("z"), lax.axis_index("ylo"), lax.axis_index("core")
    half = lax.axis_index("xp")
    quarter = lax.axis_index("yhi") * 2 + lax.axis_index("xh")

    rows = jnp.arange(TILE, dtype=jnp.int32)
    place = (offset + (tile_order[:, None] * TILE + rows[None, :])).reshape(1, 128)
    pa, wa = place.astype(jnp.float32), index_weights.T
    own = jnp.concatenate([index_keys, latent_keys], axis=1)
    own = lax.dynamic_slice_in_dim(own, half * HALF, HALF, 0)
    meta = jnp.stack([z, ylo, core, half, quarter]).astype(jnp.int32)
    own, meta = lax.optimization_barrier((own, meta))

    queries = main_queries.transpose(0, 2, 1)
    f1, b1 = shift(own, dz=1), shift(own, dz=7)
    queries_far = swap_core(queries)
    f1, b1, left, right = lax.optimization_barrier((f1, b1, queries[:4], queries[4:]))
    left, right = shift(left, dx=1), shift(right, dx=3)
    f2, b2 = shift(f1, dz=1), shift(b1, dz=7)
    y0 = shift(jnp.concatenate([own, f1, b1]), dy=1)
    pb = swap_core(pa)
    f2, b2 = lax.optimization_barrier((f2, b2))
    f3, b3 = shift(f2, dz=1), shift(b2, dz=7)
    f3, b3, left, right, pb, y0 = lax.optimization_barrier((f3, b3, left, right, pb, y0))
    f4 = shift(f3, dz=1)
    left_far, right_far = swap_core(left), swap_core(right)
    f4, ia = lax.optimization_barrier((f4, index_queries.transpose(1, 0, 2)))
    y1, y2 = shift(jnp.concatenate([f2, b2]), dy=1), shift(jnp.concatenate([f3, b3, f4]), dy=3)
    ia, wa = lax.optimization_barrier((ia, wa, f4, left_far, right_far))[:2]
    ib, wb = swap_core(ia), swap_core(wa)

    sides = (queries, queries_far, left, left_far, right, right_far, pa, pb)
    exps, m0, l0, keys = score_call(meta, 0, [own, f1, b1, f2, b2, f3, b3, f4], [], *sides)
    exps, m1, l1, keys = score_call(meta, 1, [y0, y1, y2], in_vmem(exps, keys), *sides)

    logits, ours, sent = forward_call(meta, keys, (m0, l0, m1, l1), ia, ib, pa, pb, wa, wb)
    here, up, down = pair_call(ours, swap_core(sent))
    up, down = shift(up, dx=1), shift(down, dx=3)
    sums = head_sum_call(meta, exps, m0, m1, here, up, down)
    far = shift(sums[3], dx=2, dy=2)
    target = [sums[0], far, shift(sums[1], dx=2), shift(sums[2], dy=2)]

    mine, other, kg = backward_call(meta, keys, logits, target, ia, ib, wa, wb)
    rows_out = mine + swap_core(other)
    rows_high = lax.reduce_precision(rows_out, 8, 7)
    low = jnp.concatenate([jnp.zeros((NI + 8, 128), jnp.float32), (rows_out - rows_high)[NI : NI + 8]])
    tail = rows_high + low
    kg = lax.all_to_all(kg, ("z", "ylo"), 0, 0, tiled=True)
    kg = jnp.sum(kg.astype(jnp.float32), axis=0)
    part = jnp.concatenate([kg, tail]).astype(jnp.bfloat16)
    pair = jnp.concatenate([part, shift(part, dy=2)])
    div, weight, key_grad = finish_call(meta, pair, *(shift(pair, dx=dx) for dx in (1, 2, 3)))
    return div.reshape(128), weight.T, key_grad


def solution(mesh):
    fine = Mesh(np.asarray(mesh.devices).reshape(2, 2, 2, 8, 2, 2), ALL)
    head, ctx = ("yhi", "xh", "xp"), ("z", "ylo", "core")
    in_specs = (
        P(head, ctx, None),
        P(ctx, None),
        P(ctx, None, None),
        P(ctx, None),
        P(ctx, None),
        P(ctx),
        P(),
    )
    out_specs = (P(ctx), P(ctx, None), P(ctx, None))
    return jax.shard_map(body, mesh=fine, in_specs=in_specs, out_specs=out_specs, check_vma=False)
```
